32 devices in a mesh: frames: 4 (over y, x), rows: 8 (over z, core).
Axes of the slice: x: 2, y: 2, z: 4, core: 2. Of those that a mesh axis runs over, the one named last changes fastest.
Arguments:
- kspace: float32 [2, 16, 128, 2, 128], P(None, 'frames', 'rows'), may hold values from -6 to 6
- line_mask: int32 [2, 16, 128], P(None, 'frames', 'rows'), may hold values from 0 to 1
- valid_flags: int32 [2, 16], P(None, 'frames'), may hold values from 0 to 1
- target: float32 [2, 16, 128, 2, 128], P(None, 'frames', 'rows')
- conv_in: float32 [1, 216, 64], P(None, None, 'rows'), may hold values from -0.4375 to 0.4375
- conv_mid: float32 [1, 1, 1728, 64], P(None, None, None, 'rows')
- conv_out: float32 [1, 2, 1728], P(None, None, 'rows')
- conv_bias: float32 [1, 2, 64], P(None, None, 'rows'), may hold values from -1 to 1
- first_in: float32 [1, 216, 64], P(None, None, 'rows'), may hold values from -9.1552734e-05 to 9.1552734e-05
- first_mid: float32 [1, 1, 1728, 64], P(None, None, None, 'rows'), may hold values from -9.1552734e-05 to 9.1552734e-05
- first_out: float32 [1, 2, 1728], P(None, None, 'rows'), may hold values from -9.1552734e-05 to 9.1552734e-05
- first_bias: float32 [1, 2, 64], P(None, None, 'rows'), may hold values from -0.00036621094 to 0.00036621094
- second_in: float32 [1, 216, 64], P(None, None, 'rows'), may hold values from 1.25e-12 to 5e-12
- second_mid: float32 [1, 1, 1728, 64], P(None, None, None, 'rows'), may hold values from 1.953125e-11 to 7.8125e-11
- second_out: float32 [1, 2, 1728], P(None, None, 'rows'), may hold values from 1.953125e-11 to 7.8125e-11
- second_bias: float32 [1, 2, 64], P(None, None, 'rows'), may hold values from 3.125e-10 to 1.25e-09
Outputs:
- loss_sum: float32 [], replicated
- valid_count: float32 [], replicated
- grad_norm: float32 [], replicated
- moment_in: float32 [1, 216, 64], P(None, None, 'rows')
- moment_mid: float32 [1, 1, 1728, 64], P(None, None, None, 'rows')
- moment_out: float32 [1, 2, 1728], P(None, None, 'rows')
- moment_bias: float32 [1, 2, 64], P(None, None, 'rows')
- square_in: float32 [1, 216, 64], P(None, None, 'rows')
- square_mid: float32 [1, 1, 1728, 64], P(None, None, None, 'rows')
- square_out: float32 [1, 2, 1728], P(None, None, 'rows')
- square_bias: float32 [1, 2, 64], P(None, None, 'rows')
- master_in: float32 [1, 216, 64], P(None, None, 'rows')
- master_mid: float32 [1, 1, 1728, 64], P(None, None, None, 'rows')
- master_out: float32 [1, 2, 1728], P(None, None, 'rows')
- master_bias: float32 [1, 2, 64], P(None, None, 'rows')
- copy_in: bfloat16 [1, 216, 64], P(None, None, 'rows')
- copy_mid: bfloat16 [1, 1, 1728, 64], P(None, None, None, 'rows')
- copy_out: bfloat16 [1, 2, 1728], P(None, None, 'rows')
- copy_bias: bfloat16 [1, 2, 64], P(None, None, 'rows')
The draws below stay inside these ranges and needn't reach their ends.
All inputs are finite; a program needn't handle non-finite values.
Results may differ from the reference program's by a relative error of at most 0.0085.
Values may be sent and summed in bfloat16 or wider, within the bound.
No kernel may reach another device: no remote copies, remote signals or barrier semaphores. Data moves between devices by JAX's collectives and lax.ppermute only.
A program may use at most 128 MiB of HBM per device.

```python
import math
import jax
import jax.numpy as jnp
from jax import lax

WIDTH = 64
CIN = 8
NY = 128
NX = 128
FRAMES = 16
CAS = 1
MIDS = 1
MB = 2
STEP = 10


def rising(length, ratio):
    position = jnp.arange(length).astype(jnp.float32) / (length - 1)
    gains = ratio ** position
    return gains / jnp.sqrt(jnp.mean(gains * gains))


def draw_line_mask(key, part):
    key = jax.random.fold_in(key, 5)
    rates = jax.random.randint(jax.random.fold_in(key, 1), (MB, FRAMES, 1), 4, 13)
    counts = jax.random.randint(jax.random.fold_in(key, 2), (MB, FRAMES, NY), 0, 1 << 20)
    return (counts % rates == 0).astype(jnp.int32)


def draw_valid_flags(key, part):
    key = jax.random.fold_in(key, 7)
    frame_index = jnp.arange(FRAMES, dtype=jnp.int32)
    limit = 30 + 60 * frame_index // (FRAMES - 1)
    counts = jax.random.randint(key, (MB, FRAMES), 0, 100)
    return (counts < limit[None, :]).astype(jnp.int32)


def draw_target(key, part):
    key = jax.random.fold_in(key, 9)
    shape = (MB, FRAMES, NY, 2, NX)
    ratio = 3.0
    base = jax.random.normal(key, shape, jnp.float32)
    position = jnp.arange(NY).astype(jnp.float32) / (NY - 1)
    return base * (ratio ** position)[None, None, :, None, None]


def draw_conv_mid(key, part):
    key = jax.random.fold_in(key, 11)
    shape = (CAS, MIDS, 27 * WIDTH, WIDTH)
    ratio = 3.0
    base = jax.random.normal(key, shape, jnp.float32)
    gains = jnp.tile(rising(WIDTH, ratio), 27)
    return base * gains[None, None, :, None] * (27 * WIDTH) ** (-0.5)


def draw_conv_out(key, part):
    key = jax.random.fold_in(key, 13)
    shape = (CAS, 2, 27 * WIDTH)
    ratio = 3.0
    base = jax.random.normal(key, shape, jnp.float32)
    gains = jnp.tile(rising(WIDTH, ratio), 27)
    return base * gains[None, None, :] * (27 * WIDTH) ** (-0.5)


def block_levels(own_key, extent, cuts, smallest, high):
    level, own = 1.0, jax.random.fold_in(own_key, 6)
    for axis_at, parts in cuts:
        heights = jnp.exp(jax.random.uniform(jax.random.fold_in(own, axis_at), (parts,), jnp.float32, smallest / len(cuts), high / len(cuts)))
        level = level * jnp.repeat(heights, extent[axis_at] // parts).reshape([-1 if axis == axis_at else 1 for axis in range(len(extent))])
    return level


def bell_draw(key, shape, deviation, most, cuts=(), held_as=jnp.bfloat16):
    entries = jax.random.normal(key, shape, jnp.float32) * deviation
    if len(cuts) > 0:
        entries = block_levels(key, shape, cuts, -0.22, 0.18) * entries
    return jnp.clip(entries, min=-most, max=most).astype(held_as)


def setup_inputs(seed: int = 0) -> dict:
    key_of = jax.random.split(jax.random.key(seed), 17)
    kspace = bell_draw(key_of[0], (MB, FRAMES, NY, 2, NX), 1.0, 6.0, ((1, 4), (2, 8)), jnp.float32)
    line_mask = draw_line_mask(jax.random.fold_in(key_of[16], 71), 0)
    valid_flags = draw_valid_flags(jax.random.fold_in(key_of[16], 71), 0)
    target = draw_target(jax.random.fold_in(key_of[16], 71), 0)
    conv_in = bell_draw(key_of[4], (CAS, 27 * CIN, WIDTH), (27 * CIN) ** -0.5, 0.4375, ((2, 8),), jnp.float32)
    conv_mid = draw_conv_mid(jax.random.fold_in(key_of[16], 71), 0)
    conv_out = draw_conv_out(jax.random.fold_in(key_of[16], 71), 0)
    conv_bias = bell_draw(key_of[7], (CAS, MIDS + 1, WIDTH), 0.2, 1.0, ((2, 8),), jnp.float32)
    first_in = bell_draw(key_of[8], (CAS, 27 * CIN, WIDTH), (0.0056 * (CAS * (27 * CIN * WIDTH + 27 * WIDTH * WIDTH * MIDS + 54 * WIDTH + (MIDS + 1) * WIDTH)) ** -0.5), 9.1552734375e-05, ((2, 8),), jnp.float32)
    first_mid = bell_draw(key_of[9], (CAS, MIDS, 27 * WIDTH, WIDTH), (0.0056 * (CAS * (27 * CIN * WIDTH + 27 * WIDTH * WIDTH * MIDS + 54 * WIDTH + (MIDS + 1) * WIDTH)) ** -0.5), 9.1552734375e-05, ((3, 8),), jnp.float32)
    first_out = bell_draw(key_of[10], (CAS, 2, 27 * WIDTH), (0.0056 * (CAS * (27 * CIN * WIDTH + 27 * WIDTH * WIDTH * MIDS + 54 * WIDTH + (MIDS + 1) * WIDTH)) ** -0.5), 9.1552734375e-05, ((2, 8),), jnp.float32)
    first_bias = bell_draw(key_of[11], (CAS, MIDS + 1, WIDTH), (0.022 * (CAS * (27 * CIN * WIDTH + 27 * WIDTH * WIDTH * MIDS + 54 * WIDTH + (MIDS + 1) * WIDTH)) ** -0.5), 0.00036621094, ((2, 8),), jnp.float32)
    second_in = jnp.clip(jnp.exp(math.log(4.999999980020986e-12) - 1.3862944 * jax.random.uniform(key_of[12], (CAS, 27 * CIN, WIDTH), jnp.float32) ** block_levels(key_of[12], (CAS, 27 * CIN, WIDTH), ((2, 8),), -0.2, 0.2)), 1.2499999950052465e-12, 4.999999980020986e-12)
    second_mid = jnp.clip(jnp.exp(math.log(7.812499952519758e-11) - 1.3862944 * jax.random.uniform(key_of[13], (CAS, MIDS, 27 * WIDTH, WIDTH), jnp.float32) ** block_levels(key_of[13], (CAS, MIDS, 27 * WIDTH, WIDTH), ((3, 8),), -0.2, 0.2)), 1.9531249881299395e-11, 7.812499952519758e-11)
    second_out = jnp.clip(jnp.exp(math.log(7.812499952519758e-11) - 1.3862944 * jax.random.uniform(key_of[14], (CAS, 2, 27 * WIDTH), jnp.float32) ** block_levels(key_of[14], (CAS, 2, 27 * WIDTH), ((2, 8),), -0.2, 0.2)), 1.9531249881299395e-11, 7.812499952519758e-11)
    second_bias = jnp.clip(jnp.exp(math.log(1.2499999924031613e-09) - 1.3862944 * jax.random.uniform(key_of[15], (CAS, MIDS + 1, WIDTH), jnp.float32) ** block_levels(key_of[15], (CAS, MIDS + 1, WIDTH), ((2, 8),), -0.2, 0.2)), 3.124999981007903e-10, 1.2499999924031613e-09)
    return {"kspace": kspace, "line_mask": line_mask, "valid_flags": valid_flags, "target": target, "conv_in": conv_in, "conv_mid": conv_mid, "conv_out": conv_out, "conv_bias": conv_bias, "first_in": first_in, "first_mid": first_mid, "first_out": first_out, "first_bias": first_bias, "second_in": second_in, "second_mid": second_mid, "second_out": second_out, "second_bias": second_bias}


CLIP = 0.05
RATE = 0.03
BETA_ONE = 0.9
BETA_TWO = 0.999
EPSILON = 1e-08
DECAY = 0.01
HIGHEST = lax.Precision.HIGHEST

@jax.custom_vjp
def low(v):
    return lax.optimization_barrier(v.astype(jnp.bfloat16)).astype(jnp.float32)

@jax.custom_vjp
def low_back(v):
    return v

def low_keep(v):
    return (low(v), None)

def low_pass(kept, grad):
    return (grad,)

def back_keep(v):
    return (v, None)

def back_low(kept, grad):
    return (low(grad),)
low.defvjp(low_keep, low_pass)
low_back.defvjp(back_keep, back_low)

def dft_blocks(length, sign):
    counter = jnp.arange(length, dtype=jnp.int32)
    turns = counter[:, None] * counter[None, :] % length
    angle = turns.astype(jnp.float32) * (2.0 * jnp.pi / length)
    norm_factor = 1.0 / jnp.sqrt(jnp.float32(length))
    cosine = jnp.cos(angle) * norm_factor
    sine = sign * jnp.sin(angle) * norm_factor
    return jnp.stack([jnp.stack([cosine, -sine]), jnp.stack([sine, cosine])])

def transform(image, sign):
    across = jnp.einsum('tyix,oikx->tyok', image, dft_blocks(image.shape[3], sign), precision=HIGHEST)
    return jnp.einsum('tyix,oiky->tkox', across, dft_blocks(image.shape[1], sign), precision=HIGHEST)

def convolve(inputs, kernel):
    width_in = inputs.shape[2]
    shaped = kernel.reshape(3, 3, 3, width_in, kernel.shape[1])
    result = lax.conv_general_dilated(inputs.transpose(0, 1, 3, 2)[None], shaped, (1, 1, 1), 'SAME', dimension_numbers=('NDHWC', 'DHWIO', 'NDHWC'), precision=HIGHEST)
    return result[0].transpose(0, 1, 3, 2)

def share(measured, sampled):
    count_frames = measured.shape[0]
    padded_data = jnp.pad(measured, ((2, 2), (0, 0), (0, 0), (0, 0)))
    padded_mask = jnp.pad(sampled, ((2, 2), (0, 0)))
    windows = []
    for radius in range(3):
        data_sum = padded_data[2 - radius:2 - radius + count_frames]
        mask_sum = padded_mask[2 - radius:2 - radius + count_frames]
        for offset in range(1 - radius, radius + 1):
            data_sum = data_sum + padded_data[2 + offset:2 + offset + count_frames]
            mask_sum = mask_sum + padded_mask[2 + offset:2 + offset + count_frames]
        windows.append(data_sum / jnp.maximum(mask_sum, 1.0)[:, :, None, None])
    return jnp.stack(windows, 1)

def forward_batch(params, measured_full, sampled, wanted, frame_weight):
    conv_in, conv_mid, conv_out, conv_bias = params
    measured = measured_full * sampled[:, :, None, None]
    shared = share(measured, sampled)
    frames, rows_all = (measured.shape[0], measured.shape[1])
    images = transform(shared.reshape(frames * 3, rows_all, 2, NX), 1.0).reshape(frames, 3, rows_all, 2, NX)
    shared_images = images.transpose(0, 2, 1, 3, 4).reshape(frames, rows_all, 6, NX)
    current = images[:, 0]
    unsampled = (1.0 - sampled)[:, :, None, None]
    for cascade in range(CAS):
        feature = low(jnp.concatenate([current, shared_images], axis=2))
        biases = low(conv_bias[cascade])
        hidden = low_back(convolve(feature, low(conv_in[cascade])) + biases[0][None, None, :, None])
        for layer_at in range(MIDS):
            active = low(jax.nn.gelu(hidden))
            hidden = low_back(convolve(active, low(conv_mid[cascade, layer_at])) + biases[layer_at + 1][None, None, :, None])
        active = low(jax.nn.gelu(hidden))
        branch = low_back(convolve(active, low(conv_out[cascade]).T))
        current = transform(unsampled * transform(current + branch, -1.0) + measured, 1.0)
    residual_error = current - wanted
    return jnp.sum(frame_weight[:, None, None, None] * residual_error * residual_error)

def adamw(weight, grad_piece, moment_one, moment_two):
    first_new = BETA_ONE * moment_one + (1.0 - BETA_ONE) * grad_piece
    second_new = BETA_TWO * moment_two + (1.0 - BETA_TWO) * grad_piece * grad_piece
    ascent = first_new / (1.0 - BETA_ONE ** STEP) / (jnp.sqrt(second_new / (1.0 - BETA_TWO ** STEP)) + EPSILON)
    weight_new = weight - RATE * (ascent + DECAY * weight)
    return (first_new, second_new, weight_new, weight_new.astype(jnp.bfloat16))

def reference(kspace, line_mask, valid_flags, target, conv_in, conv_mid, conv_out, conv_bias, first_in, first_mid, first_out, first_bias, second_in, second_mid, second_out, second_bias):
    params = (conv_in, conv_mid, conv_out, conv_bias)

    def one_batch(summed, batch_data):
        measured_full, mask_rows, frame_flags, wanted = batch_data
        sampled = mask_rows.astype(jnp.float32)
        frame_weight = frame_flags.astype(jnp.float32)
        loss_part, pullback = jax.vjp(lambda values: forward_batch(values, measured_full, sampled, wanted, frame_weight), params)
        grads = pullback(jnp.ones_like(loss_part))[0]
        return (jax.tree.map(jnp.add, summed, grads), (loss_part, jnp.sum(frame_weight)))
    initial = jax.tree.map(jnp.zeros_like, params)
    summed, (losses, frame_counts) = lax.scan(one_batch, initial, (kspace, line_mask, valid_flags, target))
    loss_sum = jnp.sum(losses)
    valid_count = 2.0 * NY * NX * jnp.sum(frame_counts)
    divisor = jnp.maximum(valid_count, 1.0)
    grads = [grad_piece / divisor for grad_piece in summed]
    grad_norm = jnp.sqrt(sum((jnp.sum(grad_piece * grad_piece) for grad_piece in grads)))
    factor = jnp.minimum(1.0, CLIP / (grad_norm + 1e-06))
    firsts = (first_in, first_mid, first_out, first_bias)
    seconds = (second_in, second_mid, second_out, second_bias)
    results = [adamw(params[which], grads[which] * factor, firsts[which], seconds[which]) for which in range(4)]
    return (loss_sum, valid_count, grad_norm, results[0][0], results[1][0], results[2][0], results[3][0], results[0][1], results[1][1], results[2][1], results[3][1], results[0][2], results[1][2], results[2][2], results[3][2], results[0][3], results[1][3], results[2][3], results[3][3])
```

```python
import jax
import jax.numpy as jnp
import ml_dtypes
import numpy as np
from jax import lax
from jax.experimental import pallas as pl
from jax.experimental.pallas import tpu as pltpu
from jax.sharding import Mesh
from jax.sharding import PartitionSpec as P

NX = 128
CAS = 1
MIDS = 1
STEP = 10


CLIP = 0.05
RATE = 0.03
BETA_ONE = 0.9
BETA_TWO = 0.999
EPSILON = 1e-08
DECAY = 0.01
HIGHEST = lax.Precision.HIGHEST


def with_halo(shard, sides, width):
    for axis, dim in sides:
        size, length = (lax.axis_size(axis), shard.shape[dim])
        up = [(i, (i + 1) % size) for i in range(size - 1)]
        down = [(j, i) for i, j in up]
        last = lax.slice_in_dim(shard, length - width, length, axis=dim)
        first = lax.slice_in_dim(shard, 0, width, axis=dim)
        before = lax.ppermute(last, axis, up)
        after = lax.ppermute(first, axis, down)
        shard = jnp.concatenate([before, shard, after], axis=dim)
    return shard


def from_behind(block, axis, distance):
    devices = range(lax.axis_size(axis))
    route = [(i - distance, i) for i in devices if i - distance in devices]
    return lax.ppermute(block, axis, route)


def dft_blocks(length, sign):
    counter = jnp.arange(length, dtype=jnp.int32)
    turns = counter[:, None] * counter[None, :] % length
    angle = turns.astype(jnp.float32) * (2.0 * jnp.pi / length)
    norm_factor = 1.0 / jnp.sqrt(jnp.float32(length))
    cosine = jnp.cos(angle) * norm_factor
    sine = sign * jnp.sin(angle) * norm_factor
    return jnp.stack([jnp.stack([cosine, -sine]), jnp.stack([sine, cosine])])


def transform(image, sign):
    rows_here = image.shape[1]
    rows_all = rows_here * lax.axis_size("rows")
    first_row = lax.axis_index("rows") * rows_here
    across = jnp.einsum(
        "byix,oikx->byok", image, dft_blocks(image.shape[3], sign), precision=HIGHEST
    )
    table = dft_blocks(rows_all, sign)
    window = lax.dynamic_slice(
        table, (0, 0, 0, first_row), (2, 2, lax.axis_size("rows") * rows_here, rows_here)
    )
    return lax.psum_scatter(
        jnp.einsum("byix,oiky->kbox", across, window, precision=HIGHEST),
        "rows",
        scatter_dimension=0,
        tiled=True,
    ).transpose(1, 0, 2, 3)


def taps(widened, offset, frames, rows_here, columns):
    time_off = offset // 3
    row_off = offset % 3
    return jnp.concatenate(
        [
            widened[
                time_off : time_off + frames,
                row_off : row_off + rows_here,
                :,
                col_off : col_off + columns,
            ]
            for col_off in range(3)
        ],
        axis=2,
    )


def convolve(padded, kernel):
    frames = padded.shape[0] - 2
    rows_here = padded.shape[1] - 2
    width_in = padded.shape[2]
    columns = padded.shape[3]
    widened = jnp.pad(padded, ((0, 0), (0, 0), (0, 0), (1, 1)))
    blocks = kernel.reshape(9, 3 * width_in, kernel.shape[1])
    summed = jnp.zeros((frames, rows_here, kernel.shape[1], columns), jnp.float32)
    for offset in range(9):
        gathered = taps(widened, offset, frames, rows_here, columns)
        summed = summed + jnp.einsum(
            "tykx,kj->tyjx", gathered, blocks[offset], preferred_element_type=jnp.float32
        )
    return summed


def kernel_grad(padded, grad_out):
    frames, rows_here, columns = (grad_out.shape[0], grad_out.shape[1], grad_out.shape[3])
    widened = jnp.pad(padded, ((0, 0), (0, 0), (0, 0), (1, 1)))
    pieces = [
        jnp.einsum(
            "tykx,tyjx->kj",
            taps(widened, offset, frames, rows_here, columns),
            grad_out,
            preferred_element_type=jnp.float32,
        )
        for offset in range(9)
    ]
    return jnp.concatenate(pieces, axis=0)


def flipped(kernel):
    width_in = kernel.shape[0] // 27
    shaped = kernel.reshape(3, 3, 3, width_in, kernel.shape[1])[::-1, ::-1, ::-1]
    return shaped.transpose(0, 1, 2, 4, 3).reshape(27 * kernel.shape[1], width_in)


def activation_rim(values):
    return with_halo(values, (("frames", 0), ("rows", 1)), 1)


def gradient_rim(values):
    return with_halo(values, (("frames", 0), ("rows", 1)), 1)


def layer_forward(inputs, kernel, bias_row):
    padded = activation_rim(inputs)
    return (padded, convolve(padded, kernel) + bias_row.astype(jnp.float32)[None, None, :, None])


def layer_backward(padded, kernel, grad_hidden, needs_input):
    kernel_delta = kernel_grad(padded, grad_hidden)
    bias_delta = jnp.sum(grad_hidden, axis=(0, 1, 3), dtype=jnp.float32)
    input_delta = None
    if needs_input:
        input_delta = convolve(gradient_rim(grad_hidden), flipped(kernel))
    return (kernel_delta, bias_delta, input_delta)


def share(measured, sampled):
    frames = measured.shape[0]
    reach = (frames + 1) // frames
    before = []
    after = []
    for distance in range(1, reach + 1):
        for direction in (1, -1):
            moved = from_behind((measured, sampled), "frames", direction * distance)
            if direction == 1:
                before.insert(0, moved)
            else:
                after.append(moved)
    data_line = jnp.concatenate(
        [moved_pair[0] for moved_pair in before]
        + [measured]
        + [moved_pair[0] for moved_pair in after],
        axis=0,
    )
    mask_line = jnp.concatenate(
        [moved_pair[1] for moved_pair in before]
        + [sampled]
        + [moved_pair[1] for moved_pair in after],
        axis=0,
    )
    centre = reach * frames
    windows = []
    for radius in range(3):
        data_sum = data_line[centre - radius : centre - radius + frames]
        mask_sum = mask_line[centre - radius : centre - radius + frames]
        for offset in range(1 - radius, radius + 1):
            data_sum = data_sum + data_line[centre + offset : centre + offset + frames]
            mask_sum = mask_sum + mask_line[centre + offset : centre + offset + frames]
        windows.append(data_sum / jnp.maximum(mask_sum, 1.0)[:, :, None, None])
    return jnp.stack(windows, 1)


def adamw(weight, grad_piece, moment_one, moment_two):
    first_new = BETA_ONE * moment_one + (1.0 - BETA_ONE) * grad_piece
    second_new = BETA_TWO * moment_two + (1.0 - BETA_TWO) * grad_piece * grad_piece
    ascent = (
        first_new
        / (1.0 - BETA_ONE**STEP)
        / (jnp.sqrt(second_new / (1.0 - BETA_TWO**STEP)) + EPSILON)
    )
    weight_new = weight - RATE * (ascent + DECAY * weight)
    return (first_new, second_new, weight_new, weight_new.astype(jnp.bfloat16))


def local(
    kspace,
    line_mask,
    valid_flags,
    target,
    conv_in,
    conv_mid,
    conv_out,
    conv_bias,
    first_in,
    first_mid,
    first_out,
    first_bias,
    second_in,
    second_mid,
    second_out,
    second_bias,
):
    masters = (conv_in, conv_mid, conv_out, conv_bias)

    def reduce_grads(grads):
        shards = (
            lax.psum_scatter(
                grads[0].astype(jnp.bfloat16), "rows", scatter_dimension=2, tiled=True
            ).astype(jnp.float32),
            lax.psum_scatter(
                grads[1].astype(jnp.bfloat16), "rows", scatter_dimension=3, tiled=True
            ).astype(jnp.float32),
            lax.psum_scatter(
                grads[2].astype(jnp.bfloat16), "rows", scatter_dimension=2, tiled=True
            ).astype(jnp.float32),
            lax.psum_scatter(
                grads[3].astype(jnp.bfloat16), "rows", scatter_dimension=2, tiled=True
            ).astype(jnp.float32),
        )
        return lax.psum((shards[0], shards[1], shards[2], shards[3]), "frames")

    def micro_batch(carry, batch_data):
        grad_carry, loss_carry, count_carry = carry
        measured_full, mask_rows, frame_flags, wanted = batch_data
        full_in, full_mid, full_out, full_bias = (
            lax.all_gather(conv_in.astype(jnp.bfloat16), "rows", axis=2, tiled=True),
            lax.all_gather(conv_mid.astype(jnp.bfloat16), "rows", axis=3, tiled=True),
            lax.all_gather(conv_out.astype(jnp.bfloat16), "rows", axis=2, tiled=True),
            lax.all_gather(conv_bias.astype(jnp.bfloat16), "rows", axis=2, tiled=True),
        )
        sampled = mask_rows.astype(jnp.float32)
        measured = measured_full * sampled[:, :, None, None]
        shared = share(measured, sampled)
        frames, rows_here = (measured.shape[0], measured.shape[1])
        images = transform(shared.reshape(frames * 3, rows_here, 2, NX), 1.0).reshape(
            frames, 3, rows_here, 2, NX
        )
        shared_images = images.transpose(0, 2, 1, 3, 4).reshape(frames, rows_here, 6, NX)
        current = images[:, 0]
        unsampled = (1.0 - sampled)[:, :, None, None]
        no_bias = jnp.zeros((2,), jnp.bfloat16)

        def kernels_of(cascade):
            return [full_in[cascade]] + [full_mid[cascade, 0]] + [full_out[cascade].T]

        cascade = 0
        kernels = kernels_of(cascade)
        biases = [full_bias[cascade, layer_at] for layer_at in range(MIDS + 1)] + [no_bias]
        inputs = jnp.concatenate([current, shared_images], axis=2).astype(jnp.bfloat16)
        saved = []
        for layer_at in range(MIDS + 2):
            padded, hidden = layer_forward(inputs, kernels[layer_at], biases[layer_at])
            saved.append((padded, hidden))
            if layer_at < MIDS + 1:
                inputs = jax.nn.gelu(hidden).astype(jnp.bfloat16)
        current = transform(unsampled * transform(current + hidden, -1.0) + measured, 1.0)
        kept = [saved]
        frame_weight = frame_flags.astype(jnp.float32)[:, None, None, None]
        residual_error = current - wanted
        loss_part = jnp.sum(frame_weight * residual_error * residual_error)
        count_part = 2.0 * rows_here * NX * jnp.sum(frame_flags.astype(jnp.float32))
        grad_current = 2.0 * frame_weight * residual_error
        delta_in = [None] * CAS
        delta_mid = [None] * CAS
        delta_out = [None] * CAS
        delta_bias = [None] * CAS
        for cascade in reversed(range(CAS)):
            kernels = kernels_of(cascade)
            grad_sum = transform(unsampled * transform(grad_current, -1.0), 1.0)
            grad_hidden = grad_sum.astype(jnp.bfloat16)
            kernel_deltas = [None] * (MIDS + 2)
            bias_deltas = [None] * (MIDS + 2)
            grad_input = None
            for layer_at in reversed(range(MIDS + 2)):
                padded, hidden = kept[cascade][layer_at]
                if layer_at < MIDS + 1:
                    pullback = jax.vjp(jax.nn.gelu, hidden)[1]
                    grad_hidden = pullback(grad_input)[0].astype(jnp.bfloat16)
                needs_input = cascade > 0 or layer_at > 0
                kernel_deltas[layer_at], bias_deltas[layer_at], grad_input = layer_backward(
                    padded, kernels[layer_at], grad_hidden, needs_input
                )
            delta_in[cascade] = kernel_deltas[0]
            delta_mid[cascade] = jnp.stack(kernel_deltas[1 : MIDS + 1])
            delta_out[cascade] = kernel_deltas[MIDS + 1].T
            delta_bias[cascade] = jnp.stack(bias_deltas[0 : MIDS + 1])
        grads = (
            jnp.stack(delta_in),
            jnp.stack(delta_mid),
            jnp.stack(delta_out),
            jnp.stack(delta_bias),
        )
        grads = reduce_grads(grads)
        grad_carry = jax.tree.map(jnp.add, grad_carry, grads)
        return ((grad_carry, loss_carry + loss_part, count_carry + count_part), None)

    start_grads = jax.tree.map(jnp.zeros_like, masters)
    start = (start_grads, jnp.zeros((), jnp.float32), jnp.zeros((), jnp.float32))
    (summed, loss_local, count_local), unused = lax.scan(
        micro_batch, start, (kspace, line_mask, valid_flags, target)
    )
    summed = tuple(summed)
    loss_sum, valid_count = lax.psum((loss_local, count_local), ("frames", "rows"))
    divisor = jnp.maximum(valid_count, 1.0)
    grads = [grad_piece / divisor for grad_piece in summed]
    squares = sum((jnp.sum(grad_piece * grad_piece) for grad_piece in grads))
    grad_norm = jnp.sqrt(lax.psum(squares, "rows"))
    factor = jnp.minimum(1.0, CLIP / (grad_norm + 1e-06))
    firsts = (first_in, first_mid, first_out, first_bias)
    seconds = (second_in, second_mid, second_out, second_bias)
    results = [
        adamw(masters[which], grads[which] * factor, firsts[which], seconds[which])
        for which in range(4)
    ]
    return (
        loss_sum,
        valid_count,
        grad_norm,
        results[0][0],
        results[1][0],
        results[2][0],
        results[3][0],
        results[0][1],
        results[1][1],
        results[2][1],
        results[3][1],
        results[0][2],
        results[1][2],
        results[2][2],
        results[3][2],
        results[0][3],
        results[1][3],
        results[2][3],
        results[3][3],
    )


BF = jnp.bfloat16
F32 = jnp.float32
SQRT_TWO_OVER_PI = 0.7978845608028654
CUBIC = 0.044715 * SQRT_TWO_OVER_PI
UNITS = 16
VMEM = 56 * 2**20


def column_order():
    lanes = np.arange(128)
    return (lanes % 16) * 8 + lanes // 16


def dft_tables(sign):
    counter = np.arange(128)
    angle = (counter[:, None] * counter[None, :] % 128) * (2.0 * np.pi / 128)
    cosine, sine = np.cos(angle) / np.sqrt(128.0), sign * np.sin(angle) / np.sqrt(128.0)
    return np.stack([np.stack([cosine, -sine]), np.stack([sine, cosine])])


def make_tables():
    inverse, forward = dft_tables(1.0), dft_tables(-1.0)
    order = column_order()
    columns = inverse[:, :, :, order].transpose(1, 2, 0, 3).reshape(256, 256)
    blocks = np.arange(UNITS)[:, None] * 8

    def rows_of(first, kept):
        rows = blocks + first + np.arange(16)[None, :]
        inside = (rows >= 0) & (rows < 128) & (np.arange(16)[None, :] < kept)
        return np.clip(rows, 0, 127), inside

    rows, inside = rows_of(-3, 14)
    feature = inverse[:, :, rows, :] * inside[None, None, :, :, None]
    feature = feature.transpose(2, 3, 0, 1, 4).reshape(UNITS, 16, 2, 256)
    feature = np.tile(feature, (1, 1, 4, 1)).reshape(UNITS, 128, 256)
    to_lines = forward.reshape(2, 2, 128, UNITS, 8).transpose(0, 2, 3, 1, 4).reshape(256, 256)
    to_rows = inverse.transpose(0, 2, 1, 3).reshape(256, 256)
    lines_again = forward.transpose(0, 2, 1, 3).reshape(256, 256)
    rows, inside = rows_of(-2, 12)
    spread = inverse[:, :, rows, :] * inside[None, None, :, :, None]
    spread = spread.transpose(2, 0, 3, 1, 4).reshape(UNITS * 32, 256)
    permute = np.zeros((128, 128))
    permute[order, np.arange(128)] = 1.0
    pick_out = np.zeros((64, 10, 256))
    pick_back = np.zeros((10, 288, 64))
    for time_off in range(3):
        for row_off in range(3):
            for col_off in range(3):
                tap = (time_off * 3 + row_off) * 3 + col_off
                for part in range(2):
                    for row in range(8):
                        lane = (time_off * 3 + col_off) * 16 + part * 8 + row
                        pick_out[tap * 2 + part, row + row_off, lane] = 1.0
                    for row in range(12):
                        into = row + row_off - 2
                        if 0 <= into < 10:
                            at = (time_off * 3 + col_off) * 32 + part * 16 + row
                            pick_back[into, at, tap * 2 + part] = 1.0
    made = dict(
        columns=columns,
        feature=feature,
        to_lines=to_lines,
        to_rows=to_rows,
        lines_again=lines_again,
        spread=spread,
        permute=permute,
        pick_out=pick_out.reshape(64, 2560),
        pick_back=pick_back.reshape(2880, 64),
    )
    return {name: jnp.asarray(table.astype(ml_dtypes.bfloat16)) for name, table in made.items()}


def dot(left, right):
    return jnp.dot(left, right, preferred_element_type=F32)


def dot_first(left, right):
    return lax.dot_general(left, right, (((0,), (0,)), ((), ())), preferred_element_type=F32)


def next_column(values):
    lane = lax.broadcasted_iota(jnp.int32, values.shape, 1)
    inner = pltpu.roll(values, 112, 1)
    wrapped = jnp.where(lane == 127, 0.0, pltpu.roll(values, 111, 1))
    return jnp.where(lane < 112, inner, wrapped)


def previous_column(values):
    lane = lax.broadcasted_iota(jnp.int32, values.shape, 1)
    inner = pltpu.roll(values, 16, 1)
    wrapped = jnp.where(lane == 0, 0.0, pltpu.roll(values, 17, 1))
    return jnp.where(lane >= 16, inner, wrapped)


def put_slabs(store, values):
    store(slice(1, 9), values.astype(BF).reshape(8, 16, 128))
    first, last = values[0:16], values[112:128]
    at = lax.broadcasted_iota(jnp.int32, (16, 128), 0)
    before = jnp.where(at == 0, 0.0, pltpu.roll(last, 1, 0))
    after = jnp.where(at == 15, 0.0, pltpu.roll(first, 15, 0))
    store(slice(0, 1), before.astype(BF).reshape(1, 16, 128))
    store(slice(9, 10), after.astype(BF).reshape(1, 16, 128))


def two_rows(ref, frame, pair, count, first_slab):
    upper = ref[frame, pair : pair + count, first_slab : first_slab + 8]
    lower = ref[frame, pair + 1 : pair + 1 + count, first_slab : first_slab + 8]
    rows = count * 128
    return jnp.concatenate([upper.reshape(rows, 128), lower.reshape(rows, 128)], axis=1)


def gelu_and_slope(hidden):
    square = hidden * hidden
    half = 0.5 * jnp.tanh(hidden * (CUBIC * square + SQRT_TWO_OVER_PI)) + 0.5
    active = hidden * half
    slope = half + active * (1.0 - half) * (6.0 * CUBIC * square + 2.0 * SQRT_TWO_OVER_PI)
    return active, slope


def pack_kernel(mid, first, last, bias, packed, tiles):
    tiles[...] = jnp.zeros_like(tiles)
    for tile in range(13):
        tiles[tile] = mid[:, tile * 128 : tile * 128 + 128]
    tiles[13, :, 0:64] = mid[:, 1664:1728]
    for part in range(2):
        for piece in range(4):
            tiles[13, part * 4 + piece : part * 4 + piece + 1, 64:118] = last[
                part : part + 1, piece * 54 : piece * 54 + 54
            ]
    tiles[14] = first[:, 0:128]
    tiles[15, :, 0:88] = first[:, 128:216]
    tiles[15, :, 88:90] = bias[...]
    packed[...] = tiles[...].reshape(128, 128).astype(BF)


def weight_kernel(info, own, other, pick_out, pick_back, fwd_in, fwd_mid, fwd_out, bwd_mid, bwd_out, bias, whole, line, taps):
    z, core = info[1], info[2]
    for source, side in ((own, 0), (other, 1)):
        for slot in range(4):
            chip = lax.rem(z + 4 - slot, 4)
            row = pl.multiple_of((chip * 2 + (core if side == 0 else 1 - core)) * 8, 8)
            values = source[slot * 128 : slot * 128 + 128].astype(F32).reshape(16, 8, 128)
            whole[:, pl.ds(row, 8), :] = values
    zero = jnp.zeros((64, 64), F32)
    turned = [jnp.transpose(whole[tile]) for tile in range(16)]
    plain = [whole[tile] for tile in range(14)]

    def forward_tap(time_off, row_off, col_off):
        tap = (time_off * 3 + row_off) * 3 + col_off
        return turned[tap // 2][(tap % 2) * 64 : (tap % 2) * 64 + 64]

    def backward_tap(time_off, row_off, col_off):
        tap = (time_off * 3 + row_off) * 3 + col_off
        return plain[tap // 2][:, (tap % 2) * 64 : (tap % 2) * 64 + 64]

    fwd_mid[...] = jnp.zeros_like(fwd_mid)
    bwd_mid[...] = jnp.zeros_like(bwd_mid)
    for time_off in range(3):
        for col_off in range(3):
            for level in range(4):
                left = forward_tap(time_off, level, col_off) if level < 3 else zero
                right = forward_tap(time_off, level - 1, col_off) if level > 0 else zero
                strip = jnp.concatenate([left, right], axis=1).astype(BF)
                for pair in range(2):
                    at = ((time_off + pair) * 3 + col_off) * 256 + level * 64
                    fwd_mid[at : at + 64, pair * 128 : pair * 128 + 128] = strip
                left = backward_tap(time_off, 2 - level, col_off) if level < 3 else zero
                right = backward_tap(time_off, 3 - level, col_off) if level > 0 else zero
                strip = jnp.concatenate([left, right], axis=1).astype(BF)
                for pair in range(2):
                    at = ((2 + pair - time_off) * 3 + 2 - col_off) * 256 + level * 64
                    bwd_mid[at : at + 64, pair * 128 : pair * 128 + 128] = strip
    first = jnp.concatenate([turned[14], turned[15]], axis=0)
    fwd_in[...] = jnp.zeros_like(fwd_in)
    pad = jnp.zeros((8, 64), F32)
    for time_off in range(3):
        for col_off in range(3):
            three = []
            for row_off in range(3):
                tap = (time_off * 3 + row_off) * 3 + col_off
                three.append(first[tap * 8 : tap * 8 + 8, 0:64])
            left = jnp.concatenate(three + [pad], axis=0)
            right = jnp.concatenate([pad] + three, axis=0)
            strip = jnp.concatenate([left, right], axis=1).astype(BF)
            at = (time_off * 3 + col_off) * 128
            for pair in range(6):
                fwd_in[at + pair * 16 : at + pair * 16 + 32, pair * 128 : pair * 128 + 128] = strip
    bias[...] = jnp.zeros_like(bias)
    for layer in range(2):
        row = turned[15][88 + layer : 89 + layer, 0:64]
        row = jnp.concatenate([row, row], axis=1)
        for pair in range(6):
            bias[layer : layer + 1, pair * 128 : pair * 128 + 128] = row
    for owner in range(8):
        for part in range(2):
            for piece in range(4):
                at = owner * 216 + piece * 54
                row = owner * 8 + part * 4 + piece
                line[part : part + 1, at : at + 54] = whole[13, row : row + 1, 64:118]
    taps[...] = jnp.zeros_like(taps)
    for tap in range(27):
        for part in range(2):
            row = tap * 2 + part
            taps[row : row + 1, 0:64] = line[part : part + 1, tap * 64 : tap * 64 + 64]
    last = taps[...].astype(BF)
    spread = dot_first(last[:, 0:64], pick_out[...]).astype(BF)
    for row in range(10):
        fwd_out[row * 64 : row * 64 + 64, :] = spread[:, row * 256 : row * 256 + 256]
    back = dot(pick_back[...], last[:, 0:64]).astype(BF)
    for pair in range(5):
        at = pair * 2 * 288
        bwd_out[:, pair * 128 : pair * 128 + 128] = jnp.concatenate(
            [back[at : at + 288], back[at + 288 : at + 576]], axis=1
        )


def forward_kernel(
    info, own, near_a, near_b, far_a, far_b, rows_table, columns_table, fwd_in, fwd_mid, fwd_out, bias,
    branch, lines, stats, natural, turned, active_out, slope_in, slope_out,
    spectrum, masks, seen, feature, active, hidden, taps,
):
    f, z, core, block = info[0], info[1], info[2], info[3]
    spectrum[0:2] = jnp.zeros((2, 128, 256), BF)
    spectrum[18:20] = jnp.zeros((2, 128, 256), BF)
    total = jnp.zeros((1, 128), F32)
    for turn in range(4):
        group = jnp.bitwise_xor(f, turn)
        seen_here = jnp.zeros((16, 128), F32)
        for slot in range(4):
            if turn == 0:
                source, at = own, slot
            elif slot < 2:
                source, at = ((near_a, slot), (far_a, slot), (far_a, slot + 2))[turn - 1]
            else:
                source, at = ((far_b, slot - 2), (near_b, slot - 2), (far_b, slot))[turn - 1]
            at = at * 144
            chip = lax.rem(z + 4 - slot, 4)
            made = dot(source[at : at + 128], columns_table[...]).astype(BF)
            for side in range(2):
                row = pl.multiple_of(chip * 32 + 16 * (core if side == 0 else 1 - core), 16)
                for frame in range(4):
                    piece = made[side * 64 + frame * 16 : side * 64 + frame * 16 + 16]
                    spectrum[2 + group * 4 + frame, pl.ds(row, 16), :] = piece
            seen_here = seen_here + source[at + 128 : at + 144, 0:128].astype(F32)
            if slot == 0:
                total = total + 0.5 * seen_here[8:9]
        masks[group] = seen_here[0:8]
    seen[...] = jnp.zeros_like(seen)
    for group in range(4):
        seen[2 + group * 4 : 6 + group * 4] = masks[group][0:4]
    sampled = seen[0:20]
    reach = [sampled[2:18]]
    reach.append(sampled[1:17] + sampled[2:18] + sampled[3:19])
    reach.append(reach[1] + sampled[0:16] + sampled[4:20])
    scales = [1.0 / jnp.maximum(count, 1.0) for count in reach]
    scales = [jnp.concatenate([scale, scale], axis=1) for scale in scales]
    unsampled = 1.0 - seen[pl.ds(2 + block, 1), :]
    stats[...] = jnp.zeros_like(stats)
    stats[0:1, 0:128] = unsampled
    stats[0:1, 128:256] = unsampled
    stats[1:2, 0:128] = total
    mine = spectrum[2 + block]
    lines[0:128] = mine[:, 0:128]
    lines[128:256] = mine[:, 128:256]

    feature[0] = jnp.zeros((10, 16, 128), BF)
    feature[17] = jnp.zeros((10, 16, 128), BF)
    channel = lax.rem(lax.broadcasted_iota(jnp.int32, (128, 256), 0), 8)
    table = rows_table[...].astype(F32)
    tables = [
        jnp.where(channel < 4, table, 0.0),
        jnp.where((channel == 4) | (channel == 5), table, 0.0),
        jnp.where(channel > 5, table, 0.0),
    ]
    for frame in range(16):
        near = [spectrum[frame + step].astype(F32) for step in range(5)]
        sums = [near[2]]
        sums.append(near[1] + near[2] + near[3])
        sums.append(sums[1] + near[0] + near[4])
        left = [(tables[radius] * scales[radius][frame : frame + 1]).astype(BF) for radius in range(3)]
        right = []
        for radius in range(3):
            value = sums[radius].astype(BF)
            right += [value[:, 0:128], value[:, 128:256]]
        image = dot(jnp.concatenate(left, axis=1), jnp.concatenate(right, axis=0))
        natural[frame, 0] = previous_column(image).astype(BF)
        natural[frame, 1] = image.astype(BF)
        natural[frame, 2] = next_column(image).astype(BF)

        def store(slabs, values, frame=frame):
            feature[frame + 1, slabs] = values

        put_slabs(store, jnp.transpose(image))

    active[0] = jnp.zeros((6, 10, 16, 128), BF)
    active[17] = jnp.zeros((6, 10, 16, 128), BF)
    turned[0] = jnp.zeros((128, 512), BF)
    turned[17] = jnp.zeros((128, 512), BF)
    half_lane = lax.broadcasted_iota(jnp.int32, (1, 128), 1) // 64

    def first_layer(group, carry):
        pieces = []
        for time_off in range(3):
            for col_off in range(3):
                piece = feature[pl.ds(group * 4 + time_off, 4), col_off : col_off + 8]
                pieces.append(piece.reshape(512, 128))
        hidden[...] = dot(jnp.concatenate(pieces, axis=1), fwd_in[...])

        def finish(step, carry):
            frame = group * 4 + step
            for pair in range(6):
                chunk = hidden[pl.ds(step * 128, 128), pair * 128 : pair * 128 + 128]
                value, slope = gelu_and_slope(chunk + bias[0:1, pair * 128 : pair * 128 + 128])
                if pair in (0, 5):
                    row = block * 8 - 2 + 2 * pair + half_lane
                    value = jnp.where((row >= 0) & (row < 128), value, 0.0)
                else:
                    at = (pair - 1) * 128
                    slope_in[pl.ds(frame * 128, 128), at : at + 128] = slope.astype(BF)
                    turned[frame + 1, :, at : at + 128] = jnp.transpose(value.astype(BF))

                def store(slabs, values):
                    active[frame + 1, pair, slabs] = values

                put_slabs(store, value)
            return carry

        return lax.fori_loop(0, 4, finish, carry)

    lax.fori_loop(0, 4, first_layer, 0)

    def second_layer(pair_of, carry):
        pieces = []
        for step in range(4):
            for col_off in range(3):
                pieces.append(two_rows(active, pair_of * 2 + step, 0, 5, col_off))
        result = dot(jnp.concatenate(pieces, axis=1), fwd_mid[...])
        for pair in range(5):
            for side in range(2):
                chunk = result[pair * 128 : pair * 128 + 128, side * 128 : side * 128 + 128]
                value, slope = gelu_and_slope(chunk + bias[1:2, 0:128])
                if pair in (0, 4):
                    row = block * 8 - 1 + 2 * pair + half_lane
                    inside = (row >= 0) & (row < 128)
                    value = jnp.where(inside, value, 0.0)
                    slope = jnp.where(inside, slope, 0.0)
                at = pl.multiple_of((pair_of * 2 + side) * 128, 128)
                active_out[pl.ds(at, 128), pair * 128 : pair * 128 + 128] = value.astype(BF)
                slope_out[pl.ds(at, 128), pair * 128 : pair * 128 + 128] = slope.astype(BF)
        return carry

    lax.fori_loop(0, 8, second_layer, 0)

    taps[0] = jnp.zeros((144, 128), F32)
    taps[17] = jnp.zeros((144, 128), F32)
    for frame in range(16):
        made = dot(active_out[frame * 128 : frame * 128 + 128], fwd_out[...])
        made = jnp.transpose(made)
        taps[frame + 1] = made[0:144]
    for frame in range(16):
        columns = []
        for col_off in range(3):
            value = None
            for time_off in range(3):
                at = (time_off * 3 + col_off) * 16
                piece = taps[frame + time_off, at : at + 16]
                value = piece if value is None else value + piece
            columns.append(value)
        result = previous_column(columns[0]) + columns[1] + next_column(columns[2])
        branch[frame * 16 : frame * 16 + 16] = result.astype(BF)


def consistency_kernel(info, gathered, lines, stats, wanted, to_lines, to_rows, lines_again, spread, permute, out, loss, target):
    z, core = info[1], info[2]
    for slot in range(4):
        chip = lax.rem(z + 4 - slot, 4)
        for side in range(2):
            row = pl.multiple_of(chip * 32 + 16 * (core if side == 0 else 1 - core), 16)
            at = slot * 32 + side * 16
            for part in range(2):
                piece = dot(wanted[at : at + 16, part * 128 : part * 128 + 128], permute[...])
                target[pl.ds(part * 128 + row, 16), :] = piece
    unsampled = stats[0:1]
    held = lines[...]
    mixed = (dot(to_lines[...], gathered[...]) + held.astype(F32)).astype(BF)
    table = to_rows[...]
    current = dot((table.astype(F32) * unsampled).astype(BF), mixed) + dot(table, held)
    weight = info[4].astype(F32)
    residual = current - target[...]
    loss[...] = jnp.zeros((8, 128), F32) + jnp.sum(residual * residual) * weight
    grad = (2.0 * weight * residual).astype(BF)
    spectrum = dot(lines_again[...], grad).astype(BF)
    out[...] = dot((spread[...].astype(F32) * unsampled).astype(BF), spectrum).astype(BF)


def backward_kernel(
    grads, natural, turned, active, slope_in, slope_out, bwd_mid, bwd_out,
    out,
    stack, product, grad_mid, grad_in, sum_mid, sum_out, sum_in, patches, tall, tiles, line,
):
    zero32 = jnp.zeros((96, 128), BF)
    stack[0:96, 1920:2048] = zero32
    stack[192:288, 0:128] = zero32
    for frame in range(16):
        value = grads[frame * 32 : frame * 32 + 32].astype(F32)
        shifted = [next_column(value).astype(BF), value.astype(BF), previous_column(value).astype(BF)]
        for time_off in range(3):
            to = frame + time_off - 1
            if 0 <= to < 16:
                for col_off in range(3):
                    at = (time_off * 3 + col_off) * 32
                    stack[at : at + 32, to * 128 : to * 128 + 128] = shifted[col_off]
    result = dot(stack[...], active[...])
    for pair in range(5):
        sum_out[pair] = result[:, pair * 128 : pair * 128 + 128]
    grad_mid[0] = jnp.zeros((5, 10, 16, 128), BF)
    grad_mid[17] = jnp.zeros((5, 10, 16, 128), BF)
    for group in range(4):
        product[...] = dot_first(stack[:, group * 512 : group * 512 + 512], bwd_out[...])

        def finish_mid(step, carry):
            frame = group * 4 + step
            added = []
            for pair in range(5):
                chunk = product[pl.ds(step * 128, 128), pair * 128 : pair * 128 + 128]
                slope = slope_out[pl.ds(frame * 128, 128), pair * 128 : pair * 128 + 128]
                value = (chunk * slope.astype(F32)).astype(BF).astype(F32)
                added.append(jnp.sum(value, axis=0, keepdims=True))

                def store(slabs, values):
                    grad_mid[frame + 1, pair, slabs] = values

                put_slabs(store, value)
            lane = lax.broadcasted_iota(jnp.int32, (1, 128), 1)
            own = added[1] + added[2] + added[3]
            own = own + jnp.where(lane >= 64, added[0], 0.0) + jnp.where(lane < 64, added[4], 0.0)
            return carry + own

        if group == 0:
            bias_mid = jnp.zeros((1, 128), F32)
        bias_mid = lax.fori_loop(0, 4, finish_mid, bias_mid)

    def input_side(pair_of, carry):
        pieces = []
        for step in range(4):
            for col_off in range(3):
                pieces.append(two_rows(grad_mid, pair_of * 2 + step, 0, 4, col_off))
        result = dot(jnp.concatenate(pieces, axis=1), bwd_mid[...])
        for pair in range(4):
            for side in range(2):
                frame = pair_of * 2 + side
                chunk = result[pair * 128 : pair * 128 + 128, side * 128 : side * 128 + 128]
                slope = slope_in[pl.ds(pl.multiple_of(frame * 128, 128), 128), pair * 128 : pair * 128 + 128]
                value = (chunk * slope.astype(F32)).astype(BF)
                at = pl.multiple_of(frame * 512 + pair * 128, 128)
                grad_in[pl.ds(at, 128), :] = value
                carry = carry + jnp.sum(value.astype(F32), axis=0, keepdims=True)
        return carry

    bias_in = lax.fori_loop(0, 8, input_side, jnp.zeros((1, 128), F32))

    sum_mid[...] = jnp.zeros_like(sum_mid)

    def mid_weights(frame, carry):
        left = turned[pl.ds(frame, 3)].reshape(384, 512)
        for col_off in range(3):
            right = two_rows(grad_mid, frame + 1, 0, 4, 2 - col_off)
            sum_mid[col_off] = sum_mid[col_off] + dot(left, right)
        return carry

    lax.fori_loop(0, 16, mid_weights, 0)

    patches[0:96, 0:512] = jnp.zeros((96, 512), BF)
    patches[192:288, 7680:8192] = jnp.zeros((96, 512), BF)
    for frame in range(16):
        for col_off in range(3):
            for pair in range(4):
                value = natural[frame, col_off, pair * 16 + 16 : pair * 16 + 48]
                for time_off in range(3):
                    to = frame - time_off + 1
                    if 0 <= to < 16:
                        at = (time_off * 3 + col_off) * 32
                        lane = (to * 4 + pair) * 128
                        patches[at : at + 32, lane : lane + 128] = value
    sum_in[...] = dot(patches[...], grad_in[...])

    tall[...] = jnp.zeros_like(tall)
    for time_off in range(3):
        for row_off in range(3):
            for col_off in range(3):
                tap = (time_off * 3 + row_off) * 3 + col_off
                at = time_off * 128
                upper = sum_mid[col_off, at : at + 64, (2 - row_off) * 64 : (2 - row_off) * 64 + 64]
                lower = sum_mid[col_off, at + 64 : at + 128, (3 - row_off) * 64 : (3 - row_off) * 64 + 64]
                tall[tap * 64 : tap * 64 + 64, 0:64] = upper + lower
                at = (time_off * 3 + col_off) * 32 + row_off * 8
                upper = sum_in[at : at + 8, 0:64]
                lower = sum_in[at + 8 : at + 16, 64:128]
                tall[1792 + tap * 8 : 1792 + tap * 8 + 8, 0:64] = upper + lower
    tall[2008:2009, 0:64] = bias_in[:, 0:64] + bias_in[:, 64:128]
    tall[2009:2010, 0:64] = bias_mid[:, 0:64] + bias_mid[:, 64:128]
    for tile in range(16):
        tiles[tile] = jnp.transpose(tall[tile * 128 : tile * 128 + 128])[0:64]
    for row_off in range(3):
        value = None
        for row in range(2, 10):
            lane = (row - 2 + row_off) * 64
            piece = sum_out[lane // 128, pl.ds(row, 18, stride=16), :][:, lane % 128 : lane % 128 + 64]
            value = piece if value is None else value + piece
        for time_off in range(3):
            for col_off in range(3):
                tap = (time_off * 3 + row_off) * 3 + col_off
                for part in range(2):
                    row = (time_off * 3 + col_off) * 2 + part
                    line[part : part + 1, tap * 64 : tap * 64 + 64] = value[row : row + 1]
    for owner in range(8):
        for part in range(2):
            for piece in range(4):
                at = owner * 216 + piece * 54
                row = owner * 8 + part * 4 + piece
                tiles[13, row : row + 1, 64:118] = line[part : part + 1, at : at + 54]
    for quarter in range(4):
        for owner in range(8):
            value = tiles[quarter * 4 : quarter * 4 + 4, owner * 8 : owner * 8 + 8]
            out[quarter * 8 + owner] = value.reshape(32, 128).astype(BF)


def sum_kernel(parts, stats, loss, shard, shared):
    total = parts[0].astype(F32)
    for source in range(1, 32):
        total = total + parts[source].astype(F32)
    divisor = jnp.maximum(stats[1:2, 0:1] * (2.0 * 128 * 128), 1.0)
    total = total / divisor
    shard[...] = total
    row = lax.broadcasted_iota(jnp.int32, (8, 128), 0)
    message = jnp.where(row == 0, jnp.sum(total * total), loss[...])
    for dest in range(32):
        shared[dest] = message


def update_kernel(
    info, own, near, mid, far, messages, stats,
    w_in, w_mid, w_out, w_bias, f_in, f_mid, f_out, f_bias, s_in, s_mid, s_out, s_bias,
    scalars, mf_in, mf_mid, mf_out, mf_bias, ms_in, ms_mid, ms_out, ms_bias,
    mw_in, mw_mid, mw_out, mw_bias, mc_in, mc_mid, mc_out, mc_bias,
    shards, g_mid, g_in, g_out, g_bias,
):
    f = info[0]
    for slot, source in enumerate((own, near, mid, far)):
        shards[lax.rem(f + 4 - slot, 4)] = source[...]
    message = messages[0]
    for source in range(1, 32):
        message = message + messages[source]
    norm = jnp.sqrt(message[0:1])
    scalars[...] = jnp.zeros_like(scalars)
    scalars[0:1] = message[1:2]
    scalars[1:2] = stats[1:2, 0:1] * (2.0 * 128 * 128) + jnp.zeros((1, 128), F32)
    scalars[2:3] = norm
    factor = jnp.minimum(1.0, CLIP / (norm[:, 0:1] + 1e-06))

    def tile_of(tile):
        at = (tile % 4) * 8
        return shards[tile // 4, at : at + 8]

    for tile in range(13):
        g_mid[:, tile * 128 : tile * 128 + 128] = tile_of(tile)
    mixed = tile_of(13)
    g_mid[:, 1664:1728] = mixed[:, 0:64]
    for part in range(2):
        for piece in range(4):
            row = part * 4 + piece
            g_out[part : part + 1, piece * 54 : piece * 54 + 54] = mixed[row : row + 1, 64:118]
    g_in[:, 0:128] = tile_of(14)
    mixed = tile_of(15)
    g_in[:, 128:216] = mixed[:, 0:88]
    square = jnp.concatenate([mixed, jnp.zeros((120, 128), F32)], axis=0)
    g_bias[...] = jnp.transpose(square)[88:90, 0:8]
    for grad, weight, one, two, new_one, new_two, new_weight, new_copy in (
        (g_in, w_in, f_in, s_in, mf_in, ms_in, mw_in, mc_in),
        (g_mid, w_mid, f_mid, s_mid, mf_mid, ms_mid, mw_mid, mc_mid),
        (g_out, w_out, f_out, s_out, mf_out, ms_out, mw_out, mc_out),
        (g_bias, w_bias, f_bias, s_bias, mf_bias, ms_bias, mw_bias, mc_bias),
    ):
        results = adamw(weight[...], grad[...] * factor, one[...], two[...])
        for ref, value in zip((new_one, new_two, new_weight, new_copy), results):
            ref[...] = value


def kernel_call(kernel, name, out_shape, scratch, with_info, *operands):
    specs = [pl.BlockSpec(memory_space=pltpu.VMEM) for _ in operands]
    if with_info:
        specs[0] = pl.BlockSpec(memory_space=pltpu.SMEM)
    return pl.pallas_call(
        kernel,
        name=name,
        out_shape=out_shape,
        in_specs=specs,
        scratch_shapes=scratch,
        compiler_params=pltpu.CompilerParams(vmem_limit_bytes=VMEM),
    )(*operands)


def shape(*dims, dtype=BF):
    return jax.ShapeDtypeStruct(dims, dtype)


def by_rows(
    kspace, line_mask, valid_flags, target, conv_in, conv_mid, conv_out, conv_bias,
    first_in, first_mid, first_out, first_bias, second_in, second_mid, second_out, second_bias,
):
    tables = make_tables()
    f, z, core = (lax.axis_index(name) for name in ("frames", "z", "core"))
    block = f * 4 + z
    mine_valid = lax.dynamic_slice(valid_flags, (core, z), (1, 1))[0, 0]
    info = jnp.stack([f, z, core, block, mine_valid]).astype(jnp.int32)

    def exchange(value):
        return lax.ppermute(value, "core", [(0, 1), (1, 0)])

    def turn(value, axis, step):
        return lax.ppermute(value, axis, [(i, (i + step) % 4) for i in range(4)])

    def swap(value, bit):
        return lax.ppermute(value, "frames", [(i, i ^ bit) for i in range(4)])

    sampled = line_mask.astype(F32)
    measured = (kspace * sampled[:, :, :, None, None]).astype(BF).reshape(2, 64, 256)
    wanted = target.astype(BF).reshape(2, 64, 256)
    flags = jnp.zeros((2, 16, 256), BF)
    flags = lax.dynamic_update_slice(flags, sampled.astype(BF), (0, 0, (z * 2 + core) * 16))
    flags = flags.at[:, 8, :].set(jnp.sum(valid_flags).astype(BF))
    batches = jnp.concatenate([measured, wanted, flags], axis=1)
    mine = lax.dynamic_index_in_dim(batches, core, 0, keepdims=False)
    theirs = exchange(lax.dynamic_index_in_dim(batches, 1 - core, 0, keepdims=False))
    held = jnp.concatenate([mine[0:64], theirs[0:64], mine[128:144] + theirs[128:144]], axis=0)

    packed = kernel_call(
        pack_kernel,
        "pack_weights",
        shape(128, 128),
        [pltpu.VMEM((16, 8, 128), F32)],
        False,
        conv_mid[0, 0].T,
        conv_in[0].T,
        conv_out[0],
        conv_bias[0].T,
    )
    chips = jnp.concatenate([packed] + [turn(packed, "z", step) for step in (1, 2, 3)], axis=0)
    others = exchange(chips)

    column = jnp.concatenate([held] + [turn(held, "z", step) for step in (1, 2, 3)], axis=0)
    half_a, half_b = column[0:288], column[288:576]
    near_a, near_b = swap(half_a, 1), swap(half_b, 2)
    far_a = swap(jnp.concatenate([half_a, near_a], axis=0), 2)
    far_b = swap(jnp.concatenate([half_b, near_b], axis=0), 1)

    images = jnp.stack([mine[64:128], theirs[64:128]]).reshape(2, 4, 16, 256)

    def frame_of(step):
        return lax.dynamic_index_in_dim(images, lax.rem(z + step, 4), 1, keepdims=False).reshape(32, 256)

    wanted = jnp.concatenate([frame_of(0)] + [turn(frame_of(step), "z", step) for step in (1, 2, 3)], axis=0)

    fwd_in, fwd_mid, fwd_out, bwd_mid, bwd_out, bias = kernel_call(
        weight_kernel,
        "lay_out_weights",
        (shape(1152, 768), shape(3072, 256), shape(640, 256), shape(3072, 256), shape(288, 640), shape(8, 768, dtype=F32)),
        [pltpu.VMEM((16, 64, 128), F32), pltpu.VMEM((2, 1792), F32), pltpu.VMEM((64, 128), F32)],
        True,
        info,
        chips,
        others,
        tables["pick_out"],
        tables["pick_back"],
    )
    rows_table = lax.dynamic_index_in_dim(tables["feature"], block, 0, keepdims=False)
    branch, lines, stats, natural, turned, active, slope_in, slope_out = kernel_call(
        forward_kernel,
        "features_and_branch",
        (
            shape(256, 128), shape(256, 128), shape(8, 256, dtype=F32), shape(16, 3, 128, 128), shape(18, 128, 512),
            shape(2048, 640), shape(2048, 512), shape(2048, 640),
        ),
        [
            pltpu.VMEM((20, 128, 256), BF),
            pltpu.VMEM((4, 8, 128), F32),
            pltpu.VMEM((24, 128), F32),
            pltpu.VMEM((18, 10, 16, 128), BF),
            pltpu.VMEM((18, 6, 10, 16, 128), BF),
            pltpu.VMEM((512, 768), F32),
            pltpu.VMEM((18, 144, 128), F32),
        ],
        True,
        info, column, near_a, near_b, far_a, far_b, rows_table, tables["columns"], fwd_in, fwd_mid, fwd_out, bias,
    )
    by_frame = lax.all_to_all(branch.reshape(16, 16, 128), ("frames", "z"), 0, 0, tiled=True)
    grads, loss = kernel_call(
        consistency_kernel,
        "data_consistency",
        (shape(512, 128), shape(8, 128, dtype=F32)),
        [pltpu.VMEM((256, 128), F32)],
        True,
        info, by_frame.reshape(256, 128), lines, stats, wanted,
        tables["to_lines"], tables["to_rows"], tables["lines_again"], tables["spread"], tables["permute"],
    )
    by_block = lax.all_to_all(grads.reshape(16, 32, 128), ("frames", "z"), 0, 0, tiled=True)
    parts = kernel_call(
        backward_kernel,
        "weight_gradients",
        shape(32, 32, 128),
        [
            pltpu.VMEM((288, 2048), BF),
            pltpu.VMEM((512, 640), F32),
            pltpu.VMEM((18, 5, 10, 16, 128), BF),
            pltpu.VMEM((8192, 128), BF),
            pltpu.VMEM((3, 384, 256), F32),
            pltpu.VMEM((5, 288, 128), F32),
            pltpu.VMEM((288, 128), F32),
            pltpu.VMEM((288, 8192), BF),
            pltpu.VMEM((2048, 128), F32),
            pltpu.VMEM((16, 64, 128), F32),
            pltpu.VMEM((2, 1792), F32),
        ],
        False,
        by_block.reshape(512, 128), natural, turned, active, slope_in, slope_out, bwd_mid, bwd_out,
    )
    parts = lax.all_to_all(parts, ("frames", "z", "core"), 0, 0, tiled=True)
    shard, messages = kernel_call(
        sum_kernel,
        "sum_gradients",
        (shape(32, 128, dtype=F32), shape(32, 8, 128, dtype=F32)),
        [],
        False,
        parts, stats, loss,
    )
    shards = [shard] + [turn(shard, "frames", step) for step in (1, 2, 3)]
    messages = lax.all_to_all(messages, ("frames", "z", "core"), 0, 0, tiled=True)
    groups = ((conv_in, conv_mid, conv_out, conv_bias), (first_in, first_mid, first_out, first_bias), (second_in, second_mid, second_out, second_bias))
    state = []
    for of_in, of_mid, of_out, of_bias in groups:
        state += [of_in[0].T, of_mid[0, 0].T, of_out[0], of_bias[0]]
    shapes = [(8, 216), (8, 1728), (2, 216), (2, 8)]
    results = kernel_call(
        update_kernel,
        "adamw",
        [shape(8, 128, dtype=F32)]
        + [shape(*dims, dtype=F32) for dims in shapes * 3]
        + [shape(*dims, dtype=BF) for dims in shapes],
        [
            pltpu.VMEM((4, 32, 128), F32),
            pltpu.VMEM((8, 1728), F32),
            pltpu.VMEM((8, 216), F32),
            pltpu.VMEM((2, 216), F32),
            pltpu.VMEM((2, 8), F32),
        ],
        True,
        info, *shards, messages, stats, *state,
    )
    scalars = results[0]
    outputs = [scalars[0, 0], scalars[1, 0], scalars[2, 0]]
    for at in range(1, 17, 4):
        of_in, of_mid, of_out, of_bias = results[at : at + 4]
        outputs += [of_in.T[None], of_mid.T[None, None], of_out[None], of_bias[None]]
    return tuple(outputs)


def specs_for(rows):
    lines = P(None, "frames", rows)
    images = P(None, "frames", rows, None, None)
    weights = [P(None, None, rows), P(None, None, None, rows), P(None, None, rows), P(None, None, rows)]
    in_specs = (images, lines, P(None, "frames"), images, *(weights * 3))
    out_specs = (P(), P(), P(), *(weights * 4))
    return in_specs, out_specs


def solution(mesh):
    frames, rows = (mesh.shape[axis] for axis in ("frames", "rows"))
    if (frames, rows) != (4, 8):
        in_specs, out_specs = specs_for("rows")
        return jax.shard_map(local, mesh=mesh, in_specs=in_specs, out_specs=out_specs, check_vma=False)
    chips = Mesh(mesh.devices.reshape(frames, rows // 2, 2), ("frames", "z", "core"))
    in_specs, out_specs = specs_for(("z", "core"))
    return jax.shard_map(by_rows, mesh=chips, in_specs=in_specs, out_specs=out_specs, check_vma=False)
```

```python
import jax
import jax.numpy as jnp
import ml_dtypes
import numpy as np
from jax import lax
from jax.experimental import pallas as pl
from jax.experimental.pallas import tpu as pltpu
from jax.sharding import Mesh
from jax.sharding import PartitionSpec as P

NX = 128
CAS = 1
MIDS = 1
STEP = 10


CLIP = 0.05
RATE = 0.03
BETA_ONE = 0.9
BETA_TWO = 0.999
EPSILON = 1e-08
DECAY = 0.01
HIGHEST = lax.Precision.HIGHEST


def with_halo(shard, sides, width):
    for axis, dim in sides:
        size, length = (lax.axis_size(axis), shard.shape[dim])
        up = [(i, (i + 1) % size) for i in range(size - 1)]
        down = [(j, i) for i, j in up]
        last = lax.slice_in_dim(shard, length - width, length, axis=dim)
        first = lax.slice_in_dim(shard, 0, width, axis=dim)
        before = lax.ppermute(last, axis, up)
        after = lax.ppermute(first, axis, down)
        shard = jnp.concatenate([before, shard, after], axis=dim)
    return shard


def from_behind(block, axis, distance):
    devices = range(lax.axis_size(axis))
    route = [(i - distance, i) for i in devices if i - distance in devices]
    return lax.ppermute(block, axis, route)


def dft_blocks(length, sign):
    counter = jnp.arange(length, dtype=jnp.int32)
    turns = counter[:, None] * counter[None, :] % length
    angle = turns.astype(jnp.float32) * (2.0 * jnp.pi / length)
    norm_factor = 1.0 / jnp.sqrt(jnp.float32(length))
    cosine = jnp.cos(angle) * norm_factor
    sine = sign * jnp.sin(angle) * norm_factor
    return jnp.stack([jnp.stack([cosine, -sine]), jnp.stack([sine, cosine])])


def transform(image, sign):
    rows_here = image.shape[1]
    rows_all = rows_here * lax.axis_size("rows")
    first_row = lax.axis_index("rows") * rows_here
    across = jnp.einsum(
        "byix,oikx->byok", image, dft_blocks(image.shape[3], sign), precision=HIGHEST
    )
    table = dft_blocks(rows_all, sign)
    window = lax.dynamic_slice(
        table, (0, 0, 0, first_row), (2, 2, lax.axis_size("rows") * rows_here, rows_here)
    )
    return lax.psum_scatter(
        jnp.einsum("byix,oiky->kbox", across, window, precision=HIGHEST),
        "rows",
        scatter_dimension=0,
        tiled=True,
    ).transpose(1, 0, 2, 3)


def taps(widened, offset, frames, rows_here, columns):
    time_off = offset // 3
    row_off = offset % 3
    return jnp.concatenate(
        [
            widened[
                time_off : time_off + frames,
                row_off : row_off + rows_here,
                :,
                col_off : col_off + columns,
            ]
            for col_off in range(3)
        ],
        axis=2,
    )


def convolve(padded, kernel):
    frames = padded.shape[0] - 2
    rows_here = padded.shape[1] - 2
    width_in = padded.shape[2]
    columns = padded.shape[3]
    widened = jnp.pad(padded, ((0, 0), (0, 0), (0, 0), (1, 1)))
    blocks = kernel.reshape(9, 3 * width_in, kernel.shape[1])
    summed = jnp.zeros((frames, rows_here, kernel.shape[1], columns), jnp.float32)
    for offset in range(9):
        gathered = taps(widened, offset, frames, rows_here, columns)
        summed = summed + jnp.einsum(
            "tykx,kj->tyjx", gathered, blocks[offset], preferred_element_type=jnp.float32
        )
    return summed


def kernel_grad(padded, grad_out):
    frames, rows_here, columns = (grad_out.shape[0], grad_out.shape[1], grad_out.shape[3])
    widened = jnp.pad(padded, ((0, 0), (0, 0), (0, 0), (1, 1)))
    pieces = [
        jnp.einsum(
            "tykx,tyjx->kj",
            taps(widened, offset, frames, rows_here, columns),
            grad_out,
            preferred_element_type=jnp.float32,
        )
        for offset in range(9)
    ]
    return jnp.concatenate(pieces, axis=0)


def flipped(kernel):
    width_in = kernel.shape[0] // 27
    shaped = kernel.reshape(3, 3, 3, width_in, kernel.shape[1])[::-1, ::-1, ::-1]
    return shaped.transpose(0, 1, 2, 4, 3).reshape(27 * kernel.shape[1], width_in)


def activation_rim(values):
    return with_halo(values, (("frames", 0), ("rows", 1)), 1)


def gradient_rim(values):
    return with_halo(values, (("frames", 0), ("rows", 1)), 1)


def layer_forward(inputs, kernel, bias_row):
    padded = activation_rim(inputs)
    return (padded, convolve(padded, kernel) + bias_row.astype(jnp.float32)[None, None, :, None])


def layer_backward(padded, kernel, grad_hidden, needs_input):
    kernel_delta = kernel_grad(padded, grad_hidden)
    bias_delta = jnp.sum(grad_hidden, axis=(0, 1, 3), dtype=jnp.float32)
    input_delta = None
    if needs_input:
        input_delta = convolve(gradient_rim(grad_hidden), flipped(kernel))
    return (kernel_delta, bias_delta, input_delta)


def share(measured, sampled):
    frames = measured.shape[0]
    reach = (frames + 1) // frames
    before = []
    after = []
    for distance in range(1, reach + 1):
        for direction in (1, -1):
            moved = from_behind((measured, sampled), "frames", direction * distance)
            if direction == 1:
                before.insert(0, moved)
            else:
                after.append(moved)
    data_line = jnp.concatenate(
        [moved_pair[0] for moved_pair in before]
        + [measured]
        + [moved_pair[0] for moved_pair in after],
        axis=0,
    )
    mask_line = jnp.concatenate(
        [moved_pair[1] for moved_pair in before]
        + [sampled]
        + [moved_pair[1] for moved_pair in after],
        axis=0,
    )
    centre = reach * frames
    windows = []
    for radius in range(3):
        data_sum = data_line[centre - radius : centre - radius + frames]
        mask_sum = mask_line[centre - radius : centre - radius + frames]
        for offset in range(1 - radius, radius + 1):
            data_sum = data_sum + data_line[centre + offset : centre + offset + frames]
            mask_sum = mask_sum + mask_line[centre + offset : centre + offset + frames]
        windows.append(data_sum / jnp.maximum(mask_sum, 1.0)[:, :, None, None])
    return jnp.stack(windows, 1)


def adamw(weight, grad_piece, moment_one, moment_two):
    first_new = BETA_ONE * moment_one + (1.0 - BETA_ONE) * grad_piece
    second_new = BETA_TWO * moment_two + (1.0 - BETA_TWO) * grad_piece * grad_piece
    ascent = (
        first_new
        / (1.0 - BETA_ONE**STEP)
        / (jnp.sqrt(second_new / (1.0 - BETA_TWO**STEP)) + EPSILON)
    )
    weight_new = weight - RATE * (ascent + DECAY * weight)
    return (first_new, second_new, weight_new, weight_new.astype(jnp.bfloat16))


def local(
    kspace,
    line_mask,
    valid_flags,
    target,
    conv_in,
    conv_mid,
    conv_out,
    conv_bias,
    first_in,
    first_mid,
    first_out,
    first_bias,
    second_in,
    second_mid,
    second_out,
    second_bias,
):
    masters = (conv_in, conv_mid, conv_out, conv_bias)

    def reduce_grads(grads):
        shards = (
            lax.psum_scatter(
                grads[0].astype(jnp.bfloat16), "rows", scatter_dimension=2, tiled=True
            ).astype(jnp.float32),
            lax.psum_scatter(
                grads[1].astype(jnp.bfloat16), "rows", scatter_dimension=3, tiled=True
            ).astype(jnp.float32),
            lax.psum_scatter(
                grads[2].astype(jnp.bfloat16), "rows", scatter_dimension=2, tiled=True
            ).astype(jnp.float32),
            lax.psum_scatter(
                grads[3].astype(jnp.bfloat16), "rows", scatter_dimension=2, tiled=True
            ).astype(jnp.float32),
        )
        return lax.psum((shards[0], shards[1], shards[2], shards[3]), "frames")

    def micro_batch(carry, batch_data):
        grad_carry, loss_carry, count_carry = carry
        measured_full, mask_rows, frame_flags, wanted = batch_data
        full_in, full_mid, full_out, full_bias = (
            lax.all_gather(conv_in.astype(jnp.bfloat16), "rows", axis=2, tiled=True),
            lax.all_gather(conv_mid.astype(jnp.bfloat16), "rows", axis=3, tiled=True),
            lax.all_gather(conv_out.astype(jnp.bfloat16), "rows", axis=2, tiled=True),
            lax.all_gather(conv_bias.astype(jnp.bfloat16), "rows", axis=2, tiled=True),
        )
        sampled = mask_rows.astype(jnp.float32)
        measured = measured_full * sampled[:, :, None, None]
        shared = share(measured, sampled)
        frames, rows_here = (measured.shape[0], measured.shape[1])
        images = transform(shared.reshape(frames * 3, rows_here, 2, NX), 1.0).reshape(
            frames, 3, rows_here, 2, NX
        )
        shared_images = images.transpose(0, 2, 1, 3, 4).reshape(frames, rows_here, 6, NX)
        current = images[:, 0]
        unsampled = (1.0 - sampled)[:, :, None, None]
        no_bias = jnp.zeros((2,), jnp.bfloat16)

        def kernels_of(cascade):
            return [full_in[cascade]] + [full_mid[cascade, 0]] + [full_out[cascade].T]

        cascade = 0
        kernels = kernels_of(cascade)
        biases = [full_bias[cascade, layer_at] for layer_at in range(MIDS + 1)] + [no_bias]
        inputs = jnp.concatenate([current, shared_images], axis=2).astype(jnp.bfloat16)
        saved = []
        for layer_at in range(MIDS + 2):
            padded, hidden = layer_forward(inputs, kernels[layer_at], biases[layer_at])
            saved.append((padded, hidden))
            if layer_at < MIDS + 1:
                inputs = jax.nn.gelu(hidden).astype(jnp.bfloat16)
        current = transform(unsampled * transform(current + hidden, -1.0) + measured, 1.0)
        kept = [saved]
        frame_weight = frame_flags.astype(jnp.float32)[:, None, None, None]
        residual_error = current - wanted
        loss_part = jnp.sum(frame_weight * residual_error * residual_error)
        count_part = 2.0 * rows_here * NX * jnp.sum(frame_flags.astype(jnp.float32))
        grad_current = 2.0 * frame_weight * residual_error
        delta_in = [None] * CAS
        delta_mid = [None] * CAS
        delta_out = [None] * CAS
        delta_bias = [None] * CAS
        for cascade in reversed(range(CAS)):
            kernels = kernels_of(cascade)
            grad_sum = transform(unsampled * transform(grad_current, -1.0), 1.0)
            grad_hidden = grad_sum.astype(jnp.bfloat16)
            kernel_deltas = [None] * (MIDS + 2)
            bias_deltas = [None] * (MIDS + 2)
            grad_input = None
            for layer_at in reversed(range(MIDS + 2)):
                padded, hidden = kept[cascade][layer_at]
                if layer_at < MIDS + 1:
                    pullback = jax.vjp(jax.nn.gelu, hidden)[1]
                    grad_hidden = pullback(grad_input)[0].astype(jnp.bfloat16)
                needs_input = cascade > 0 or layer_at > 0
                kernel_deltas[layer_at], bias_deltas[layer_at], grad_input = layer_backward(
                    padded, kernels[layer_at], grad_hidden, needs_input
                )
            delta_in[cascade] = kernel_deltas[0]
            delta_mid[cascade] = jnp.stack(kernel_deltas[1 : MIDS + 1])
            delta_out[cascade] = kernel_deltas[MIDS + 1].T
            delta_bias[cascade] = jnp.stack(bias_deltas[0 : MIDS + 1])
        grads = (
            jnp.stack(delta_in),
            jnp.stack(delta_mid),
            jnp.stack(delta_out),
            jnp.stack(delta_bias),
        )
        grads = reduce_grads(grads)
        grad_carry = jax.tree.map(jnp.add, grad_carry, grads)
        return ((grad_carry, loss_carry + loss_part, count_carry + count_part), None)

    start_grads = jax.tree.map(jnp.zeros_like, masters)
    start = (start_grads, jnp.zeros((), jnp.float32), jnp.zeros((), jnp.float32))
    (summed, loss_local, count_local), unused = lax.scan(
        micro_batch, start, (kspace, line_mask, valid_flags, target)
    )
    summed = tuple(summed)
    loss_sum, valid_count = lax.psum((loss_local, count_local), ("frames", "rows"))
    divisor = jnp.maximum(valid_count, 1.0)
    grads = [grad_piece / divisor for grad_piece in summed]
    squares = sum((jnp.sum(grad_piece * grad_piece) for grad_piece in grads))
    grad_norm = jnp.sqrt(lax.psum(squares, "rows"))
    factor = jnp.minimum(1.0, CLIP / (grad_norm + 1e-06))
    firsts = (first_in, first_mid, first_out, first_bias)
    seconds = (second_in, second_mid, second_out, second_bias)
    results = [
        adamw(masters[which], grads[which] * factor, firsts[which], seconds[which])
        for which in range(4)
    ]
    return (
        loss_sum,
        valid_count,
        grad_norm,
        results[0][0],
        results[1][0],
        results[2][0],
        results[3][0],
        results[0][1],
        results[1][1],
        results[2][1],
        results[3][1],
        results[0][2],
        results[1][2],
        results[2][2],
        results[3][2],
        results[0][3],
        results[1][3],
        results[2][3],
        results[3][3],
    )


BF = jnp.bfloat16
F32 = jnp.float32
SQRT_TWO_OVER_PI = 0.7978845608028654
CUBIC = 0.044715 * SQRT_TWO_OVER_PI
UNITS = 16
VMEM = 56 * 2**20


def column_order():
    lanes = np.arange(128)
    return (lanes % 16) * 8 + lanes // 16


def dft_tables(sign):
    counter = np.arange(128)
    angle = (counter[:, None] * counter[None, :] % 128) * (2.0 * np.pi / 128)
    cosine, sine = np.cos(angle) / np.sqrt(128.0), sign * np.sin(angle) / np.sqrt(128.0)
    return np.stack([np.stack([cosine, -sine]), np.stack([sine, cosine])])


def make_tables():
    inverse, forward = dft_tables(1.0), dft_tables(-1.0)
    order = column_order()
    columns = inverse[:, :, :, order].transpose(1, 2, 0, 3).reshape(256, 256)
    blocks = np.arange(UNITS)[:, None] * 8

    def rows_of(first, kept):
        rows = blocks + first + np.arange(16)[None, :]
        inside = (rows >= 0) & (rows < 128) & (np.arange(16)[None, :] < kept)
        return np.clip(rows, 0, 127), inside

    rows, inside = rows_of(-3, 14)
    feature = inverse[:, :, rows, :] * inside[None, None, :, :, None]
    feature = feature.transpose(2, 3, 0, 1, 4).reshape(UNITS, 16, 2, 256)
    feature = np.tile(feature, (1, 1, 4, 1)).reshape(UNITS, 128, 256)
    to_lines = forward.reshape(2, 2, 128, UNITS, 8).transpose(0, 2, 3, 1, 4).reshape(256, 256)
    to_rows = inverse.transpose(0, 2, 1, 3).reshape(256, 256)
    lines_again = forward.transpose(0, 2, 1, 3).reshape(256, 256)
    rows, inside = rows_of(-2, 12)
    spread = inverse[:, :, rows, :] * inside[None, None, :, :, None]
    spread = spread.transpose(2, 0, 3, 1, 4).reshape(UNITS * 32, 256)
    permute = np.zeros((128, 128))
    permute[order, np.arange(128)] = 1.0
    pick_out = np.zeros((64, 10, 256))
    pick_back = np.zeros((10, 288, 64))
    for time_off in range(3):
        for row_off in range(3):
            for col_off in range(3):
                tap = (time_off * 3 + row_off) * 3 + col_off
                for part in range(2):
                    for row in range(8):
                        lane = (time_off * 3 + col_off) * 16 + part * 8 + row
                        pick_out[tap * 2 + part, row + row_off, lane] = 1.0
                    for row in range(12):
                        into = row + row_off - 2
                        if 0 <= into < 10:
                            at = (time_off * 3 + col_off) * 32 + part * 16 + row
                            pick_back[into, at, tap * 2 + part] = 1.0
    made = dict(
        columns=columns,
        feature=feature,
        to_lines=to_lines,
        lines_again=lines_again,
        to_rows=to_rows,
        spread=spread,
        permute=permute,
        pick_out=pick_out.reshape(64, 2560),
        pick_back=pick_back.reshape(2880, 64),
    )
    return {name: jnp.asarray(table.astype(ml_dtypes.bfloat16)) for name, table in made.items()}


def dot(left, right):
    return jnp.dot(left, right, preferred_element_type=F32)


def dot_first(left, right):
    return lax.dot_general(left, right, (((0,), (0,)), ((), ())), preferred_element_type=F32)


def next_column(values):
    lane = lax.broadcasted_iota(jnp.int32, values.shape, 1)
    inner = pltpu.roll(values, 112, 1)
    wrapped = jnp.where(lane == 127, 0.0, pltpu.roll(values, 111, 1))
    return jnp.where(lane < 112, inner, wrapped)


def previous_column(values):
    lane = lax.broadcasted_iota(jnp.int32, values.shape, 1)
    inner = pltpu.roll(values, 16, 1)
    wrapped = jnp.where(lane == 0, 0.0, pltpu.roll(values, 17, 1))
    return jnp.where(lane >= 16, inner, wrapped)


def put_slabs(store, values):
    store(slice(1, 9), values.astype(BF).reshape(8, 16, 128))
    first, last = values[0:16], values[112:128]
    at = lax.broadcasted_iota(jnp.int32, (16, 128), 0)
    before = jnp.where(at == 0, 0.0, pltpu.roll(last, 1, 0))
    after = jnp.where(at == 15, 0.0, pltpu.roll(first, 15, 0))
    store(slice(0, 1), before.astype(BF).reshape(1, 16, 128))
    store(slice(9, 10), after.astype(BF).reshape(1, 16, 128))


def two_rows(ref, frame, pair, count, first_slab):
    upper = ref[frame, pair : pair + count, first_slab : first_slab + 8]
    lower = ref[frame, pair + 1 : pair + 1 + count, first_slab : first_slab + 8]
    rows = count * 128
    return jnp.concatenate([upper.reshape(rows, 128), lower.reshape(rows, 128)], axis=1)


def gelu_and_slope(hidden):
    square = hidden * hidden
    half = 0.5 * jnp.tanh(hidden * (CUBIC * square + SQRT_TWO_OVER_PI)) + 0.5
    active = hidden * half
    slope = half + active * (1.0 - half) * (6.0 * CUBIC * square + 2.0 * SQRT_TWO_OVER_PI)
    return active, slope


def place():
    return tuple(lax.axis_index(name) for name in ("frames", "half", "chip", "core"))


def lines_kernel(
    valid, kspace, line_mask, target, permute, conv_mid, conv_in, conv_out, conv_bias,
    mine, theirs, mine_target, theirs_target, both, images, tiles,
):
    f, half, chip, core = place()
    quarter = chip * 2 + core
    sampled = line_mask[...].astype(F32)
    wide = jnp.concatenate([sampled, jnp.zeros((8, 112), F32)], axis=1)
    column = jnp.transpose(jnp.concatenate([wide, jnp.zeros((120, 128), F32)], axis=0))
    placed = pltpu.roll(wide, (half * 4 + quarter) * 16, 1)
    total = jnp.zeros((1, 128), F32)
    flags = []
    for batch in range(2):
        for frame in range(4):
            flag = jnp.zeros((1, 128), F32) + valid[batch, frame].astype(F32)
            flags.append(flag)
            total = total + flag
    for batch in range(2):
        shown = [[], []]
        for frame in range(4):
            at = batch * 4 + frame
            own = column[0:16, at : at + 1]
            lines = [kspace[batch, frame, pl.ds(part, 16, stride=2), :] * own for part in range(2)]
            both[batch, frame * 16 : frame * 16 + 16] = jnp.concatenate(lines, axis=1).astype(BF)
            for part in range(2):
                shown[part].append(target[batch, frame, pl.ds(part, 16, stride=2), :])
        rows = [placed[batch * 4 : batch * 4 + 4]] + flags[batch * 4 : batch * 4 + 4] + [total, jnp.zeros((7, 128), F32)]
        both[batch, 64:80, 0:128] = jnp.concatenate(rows, axis=0).astype(BF)
        both[batch, 64:80, 128:256] = jnp.zeros((16, 128), BF)
        for part in range(2):
            image = jnp.concatenate(shown[part], axis=0).astype(BF)
            image = dot(image, permute[...]).astype(BF)
            for frame in range(4):
                row = pl.multiple_of(16 * jnp.bitwise_xor(quarter, frame), 16)
                images[batch, pl.ds(row, 16), part * 128 : part * 128 + 128] = image[frame * 16 : frame * 16 + 16]
    mine[0:80] = both[half]
    theirs[0:80] = both[1 - half]
    mine_target[...] = images[half]
    theirs_target[...] = images[1 - half]
    tiles[...] = jnp.zeros_like(tiles)
    for tile in range(13):
        tiles[tile] = conv_mid[:, tile * 128 : tile * 128 + 128]
    tiles[13, :, 0:64] = conv_mid[:, 1664:1728]
    for part in range(2):
        for piece in range(4):
            row = part * 4 + piece
            tiles[13, row : row + 1, 64:118] = conv_out[part : part + 1, piece * 54 : piece * 54 + 54]
    tiles[14] = conv_in[:, 0:128]
    tiles[15, :, 0:88] = conv_in[:, 128:216]
    wide = jnp.concatenate([conv_bias[...], jnp.zeros((2, 120), F32)], axis=1)
    wide = jnp.transpose(jnp.concatenate([wide, jnp.zeros((126, 128), F32)], axis=0))
    tiles[15, :, 88:90] = wide[0:8, 0:2]
    packed = tiles[...].reshape(128, 128).astype(BF)
    packed = jnp.concatenate([packed[0:64], packed[64:128]], axis=1)
    mine[80:144] = packed
    theirs[80:144] = packed


def unpack_weights(own, other, whole):
    f, half, chip, core = place()
    for side, source in enumerate((own, other)):
        for slot in range(4):
            row = jnp.bitwise_xor(half * 4 + chip * 2 + core, slot * 2 + side)
            row = pl.multiple_of(row * 8, 8)
            values = source[slot * 64 : slot * 64 + 64].astype(F32)
            for part in range(2):
                half_of = values[:, part * 128 : part * 128 + 128].reshape(8, 8, 128)
                whole[part * 8 : part * 8 + 8, pl.ds(row, 8), :] = half_of


def unpack_last(whole, line, taps):
    for owner in range(8):
        for part in range(2):
            for piece in range(4):
                at = owner * 216 + piece * 54
                row = owner * 8 + part * 4 + piece
                line[part : part + 1, at : at + 54] = whole[13, row : row + 1, 64:118]
    taps[...] = jnp.zeros_like(taps)
    for tap in range(27):
        for part in range(2):
            row = tap * 2 + part
            taps[row : row + 1, 0:64] = line[part : part + 1, tap * 64 : tap * 64 + 64]
    return taps[...].astype(BF)[:, 0:64]


def forward_weight_kernel(own, other, pick_out, fwd_in, fwd_mid, fwd_out, bias, whole, line, taps):
    unpack_weights(own, other, whole)
    zero = jnp.zeros((64, 64), F32)
    turned = [jnp.transpose(whole[tile]) for tile in range(16)]

    def of_tap(time_off, row_off, col_off):
        tap = (time_off * 3 + row_off) * 3 + col_off
        return turned[tap // 2][(tap % 2) * 64 : (tap % 2) * 64 + 64]

    for time_off in range(4):
        for col_off in range(3):
            at = (time_off * 3 + col_off) * 256
            if time_off == 0:
                fwd_mid[at : at + 256, 128:256] = jnp.zeros((256, 128), BF)
            if time_off == 3:
                fwd_mid[at : at + 256, 0:128] = jnp.zeros((256, 128), BF)
    for time_off in range(3):
        for col_off in range(3):
            for level in range(4):
                left = of_tap(time_off, level, col_off) if level < 3 else zero
                right = of_tap(time_off, level - 1, col_off) if level > 0 else zero
                strip = jnp.concatenate([left, right], axis=1).astype(BF)
                for pair in range(2):
                    at = ((time_off + pair) * 3 + col_off) * 256 + level * 64
                    fwd_mid[at : at + 64, pair * 128 : pair * 128 + 128] = strip
    first = jnp.concatenate([turned[14], turned[15]], axis=0)
    fwd_in[...] = jnp.zeros_like(fwd_in)
    pad = jnp.zeros((8, 64), F32)
    for time_off in range(3):
        for col_off in range(3):
            three = []
            for row_off in range(3):
                tap = (time_off * 3 + row_off) * 3 + col_off
                three.append(first[tap * 8 : tap * 8 + 8, 0:64])
            left = jnp.concatenate(three + [pad], axis=0)
            right = jnp.concatenate([pad] + three, axis=0)
            strip = jnp.concatenate([left, right], axis=1).astype(BF)
            at = (time_off * 3 + col_off) * 128
            for pair in range(6):
                fwd_in[at + pair * 16 : at + pair * 16 + 32, pair * 128 : pair * 128 + 128] = strip
    bias[...] = jnp.zeros_like(bias)
    for layer in range(2):
        row = turned[15][88 + layer : 89 + layer, 0:64]
        row = jnp.concatenate([row, row], axis=1)
        for pair in range(6):
            bias[layer : layer + 1, pair * 128 : pair * 128 + 128] = row
    spread = dot_first(unpack_last(whole, line, taps), pick_out[...]).astype(BF)
    for row in range(10):
        fwd_out[row * 64 : row * 64 + 64, :] = spread[:, row * 256 : row * 256 + 256]


def backward_weight_kernel(own, other, pick_back, bwd_mid, bwd_out, whole, line, taps):
    unpack_weights(own, other, whole)
    zero = jnp.zeros((64, 64), F32)
    plain = [whole[tile] for tile in range(14)]

    def of_tap(time_off, row_off, col_off):
        tap = (time_off * 3 + row_off) * 3 + col_off
        return plain[tap // 2][:, (tap % 2) * 64 : (tap % 2) * 64 + 64]

    for time_off in range(4):
        for col_off in range(3):
            at = (time_off * 3 + col_off) * 256
            if time_off == 0:
                bwd_mid[at : at + 256, 128:256] = jnp.zeros((256, 128), BF)
            if time_off == 3:
                bwd_mid[at : at + 256, 0:128] = jnp.zeros((256, 128), BF)
    for time_off in range(3):
        for col_off in range(3):
            for level in range(4):
                left = of_tap(time_off, 2 - level, col_off) if level < 3 else zero
                right = of_tap(time_off, 3 - level, col_off) if level > 0 else zero
                strip = jnp.concatenate([left, right], axis=1).astype(BF)
                for pair in range(2):
                    at = ((2 + pair - time_off) * 3 + 2 - col_off) * 256 + level * 64
                    bwd_mid[at : at + 64, pair * 128 : pair * 128 + 128] = strip
    back = dot(pick_back[...], unpack_last(whole, line, taps)).astype(BF)
    for pair in range(5):
        at = pair * 2 * 288
        bwd_out[:, pair * 128 : pair * 128 + 128] = jnp.concatenate(
            [back[at : at + 288], back[at + 288 : at + 576]], axis=1
        )


def move(source, target, semaphores, at):
    copy = pltpu.make_async_copy(source, target, semaphores.at[at])
    copy.start()
    return copy


def forward_kernel(*refs):
    gathered_hbm, refs = refs[0:12], refs[12:]
    row_tables, columns_table, fwd_in_hbm, fwd_mid_hbm, fwd_out, bias = refs[0:6]
    branch, stats, lines, natural_hbm, turned_hbm, active_hbm, slope_in_hbm, slope_out_hbm = refs[6:14]
    gathered, refs = refs[14:26], refs[26:]
    rows_table, fwd_in, fwd_mid, came = refs[0:4]
    spectrum, masks, seen, feature, active, hidden, taps, natural, turned, active_out, slope_in, slope_out, done = refs[4:]
    f, half, chip, core = place()
    quarter = chip * 2 + core
    block = f * 4 + quarter
    sources = (*gathered_hbm, row_tables.at[block], fwd_in_hbm, fwd_mid_hbm)
    targets = (*gathered, rows_table, fwd_in, fwd_mid)
    loads = [move(source, to, came, at) for at, (source, to) in enumerate(zip(sources, targets))]
    spectrum[0:2] = jnp.zeros((2, 128, 256), BF)
    spectrum[18:20] = jnp.zeros((2, 128, 256), BF)
    feature[0] = jnp.zeros((10, 16, 128), BF)
    feature[17] = jnp.zeros((10, 16, 128), BF)
    active[0] = jnp.zeros((6, 10, 16, 128), BF)
    active[17] = jnp.zeros((6, 10, 16, 128), BF)
    turned[0] = jnp.zeros((128, 512), BF)
    turned[17] = jnp.zeros((128, 512), BF)
    taps[0] = jnp.zeros((144, 128), F32)
    taps[17] = jnp.zeros((144, 128), F32)
    total = jnp.zeros((1, 128), F32)
    masks[...] = jnp.zeros_like(masks)
    for at in range(12):
        loads[at].wait()
        side, which = at // 6, at % 6
        held = ((0,), (0,), (1,), (2,), (2, 3), (1, 3))[which]
        for piece, turn in enumerate(held):
            group = jnp.bitwise_xor(f, turn)
            rows = gathered[at][piece * 144 : piece * 144 + 144]
            made = dot(rows[0:128], columns_table[...]).astype(BF)
            for other in range(2):
                chips_away = which % 2 * 2 + other
                row = jnp.bitwise_xor(half * 4 + quarter, chips_away * 2 + side) * 16
                row = pl.multiple_of(row, 16)
                for frame in range(4):
                    line = made[other * 64 + frame * 16 : other * 64 + frame * 16 + 16]
                    spectrum[2 + group * 4 + frame, pl.ds(row, 16), :] = line
            flags = rows[128:144, 0:128].astype(F32)
            if side == 0 and which % 2 == 0:
                total = total + 0.5 * flags[8:9]
                masks[group] = masks[group] + flags[0:8]
            else:
                masks[group, 0:4] = masks[group, 0:4] + flags[0:4]
    seen[...] = jnp.zeros_like(seen)
    for group in range(4):
        seen[2 + group * 4 : 6 + group * 4] = masks[group, 0:4]
    stats[...] = jnp.zeros_like(stats)
    for part in range(2):
        stats[0:1, part * 128 : part * 128 + 128] = 1.0 - masks[f, pl.ds(quarter, 1), :]
    stats[1:2, 0:128] = total
    stats[2:3, 0:128] = 0.5 * masks[f, pl.ds(4 + quarter, 1), :]
    mine = spectrum[2 + block]
    lines[0:128] = mine[:, 0:128]
    lines[128:256] = mine[:, 128:256]
    sampled = seen[0:20]
    reach = [sampled[2:18]]
    reach.append(sampled[1:17] + sampled[2:18] + sampled[3:19])
    reach.append(reach[1] + sampled[0:16] + sampled[4:20])
    scales = [1.0 / jnp.maximum(count, 1.0) for count in reach]
    scales = [jnp.concatenate([scale, scale], axis=1) for scale in scales]

    loads[12].wait()
    channel = lax.rem(lax.broadcasted_iota(jnp.int32, (128, 256), 0), 8)
    table = rows_table[...].astype(F32)
    tables = [
        jnp.where(channel < 4, table, 0.0),
        jnp.where((channel == 4) | (channel == 5), table, 0.0),
        jnp.where(channel > 5, table, 0.0),
    ]
    for frame in range(16):
        near = [spectrum[frame + step].astype(F32) for step in range(5)]
        sums = [near[2]]
        sums.append(near[1] + near[2] + near[3])
        sums.append(sums[1] + near[0] + near[4])
        left = [(tables[radius] * scales[radius][frame : frame + 1]).astype(BF) for radius in range(3)]
        right = []
        for radius in range(3):
            value = sums[radius].astype(BF)
            right += [value[:, 0:128], value[:, 128:256]]
        image = dot(jnp.concatenate(left, axis=1), jnp.concatenate(right, axis=0))
        natural[frame] = image.astype(BF)

        def store(slabs, values, frame=frame):
            feature[frame + 1, slabs] = values

        put_slabs(store, jnp.transpose(image))
    copies = [move(natural, natural_hbm, done, 0)]
    loads[13].wait()
    half_lane = lax.broadcasted_iota(jnp.int32, (1, 128), 1) // 64

    def first_layer(group, carry):
        pieces = []
        for time_off in range(3):
            for col_off in range(3):
                piece = feature[pl.ds(group * 4 + time_off, 4), col_off : col_off + 8]
                pieces.append(piece.reshape(512, 128))
        hidden[...] = dot(jnp.concatenate(pieces, axis=1), fwd_in[...])

        def finish(step, carry):
            frame = group * 4 + step
            for pair in range(6):
                chunk = hidden[pl.ds(step * 128, 128), pair * 128 : pair * 128 + 128]
                value, slope = gelu_and_slope(chunk + bias[0:1, pair * 128 : pair * 128 + 128])
                if pair in (0, 5):
                    row = block * 8 - 2 + 2 * pair + half_lane
                    value = jnp.where((row >= 0) & (row < 128), value, 0.0)
                else:
                    at = (pair - 1) * 128
                    slope_in[pl.ds(frame * 128, 128), at : at + 128] = slope.astype(BF)
                    turned[frame + 1, :, at : at + 128] = jnp.transpose(value.astype(BF))

                def store(slabs, values):
                    active[frame + 1, pair, slabs] = values

                put_slabs(store, value)
            return carry

        return lax.fori_loop(0, 4, finish, carry)

    lax.fori_loop(0, 4, first_layer, 0)
    copies.append(move(turned, turned_hbm, done, 1))
    copies.append(move(slope_in, slope_in_hbm, done, 2))
    loads[14].wait()

    def second_layer(pair_of, carry):
        pieces = []
        for step in range(4):
            for col_off in range(3):
                pieces.append(two_rows(active, pair_of * 2 + step, 0, 5, col_off))
        result = dot(jnp.concatenate(pieces, axis=1), fwd_mid[...])
        for pair in range(5):
            for side in range(2):
                chunk = result[pair * 128 : pair * 128 + 128, side * 128 : side * 128 + 128]
                value, slope = gelu_and_slope(chunk + bias[1:2, 0:128])
                if pair in (0, 4):
                    row = block * 8 - 1 + 2 * pair + half_lane
                    inside = (row >= 0) & (row < 128)
                    value = jnp.where(inside, value, 0.0)
                    slope = jnp.where(inside, slope, 0.0)
                at = pl.multiple_of((pair_of * 2 + side) * 128, 128)
                active_out[pl.ds(at, 128), pair * 128 : pair * 128 + 128] = value.astype(BF)
                slope_out[pl.ds(at, 128), pair * 128 : pair * 128 + 128] = slope.astype(BF)
        return carry

    lax.fori_loop(0, 8, second_layer, 0)
    copies.append(move(active_out, active_hbm, done, 3))
    copies.append(move(slope_out, slope_out_hbm, done, 4))

    for frame in range(16):
        made = dot(active_out[frame * 128 : frame * 128 + 128], fwd_out[...])
        made = jnp.transpose(made)
        taps[frame + 1] = made[0:144]
    for frame in range(16):
        columns = []
        for col_off in range(3):
            value = None
            for time_off in range(3):
                at = (time_off * 3 + col_off) * 16
                piece = taps[frame + time_off, at : at + 16]
                value = piece if value is None else value + piece
            columns.append(value)
        result = previous_column(columns[0]) + columns[1] + next_column(columns[2])
        branch[frame * 16 : frame * 16 + 16] = result.astype(BF)
    for copy in copies:
        copy.wait()


def consistency_kernel(
    gathered, lines, stats, own, one, two, three, to_lines, to_rows, lines_again, spread, out, loss, target
):
    f, half, chip, core = place()
    for slot, source in enumerate((own, one, two, three)):
        for other in range(2):
            row = jnp.bitwise_xor(half * 4 + chip * 2 + core, other * 4 + slot) * 16
            row = pl.multiple_of(row, 16)
            at = other * 16
            for part in range(2):
                target[pl.ds(part * 128 + row, 16), :] = source[at : at + 16, part * 128 : part * 128 + 128]
    weight = stats[2:3, 0:128]
    free = jnp.transpose(jnp.zeros((128, 128), F32) + stats[0:1, 0:128])
    free = jnp.concatenate([free, free], axis=0)
    wanted = target[...]
    made = dot(to_lines[...], gathered[...])
    wanted_spectrum = dot(lines_again[...], wanted)
    held = lines[...].astype(F32)
    kept = free * (made + held) + held
    grad = (free * (kept - wanted_spectrum) * (2.0 * weight)).astype(BF)
    out[...] = dot(spread[...], grad).astype(BF)
    residual = dot(to_rows[...], kept.astype(BF)) - wanted.astype(F32)
    loss[...] = jnp.zeros((8, 128), F32) + jnp.sum(residual * residual * weight)


def backward_kernel(
    grads, bwd_out_hbm, slope_out_hbm, active_hbm, bwd_mid_hbm, slope_in_hbm, turned_hbm, natural_hbm,
    out,
    bwd_out, slope_out, active, bwd_mid, slope_in, turned, natural, came,
    stack, product, grad_mid, grad_in, sum_mid, sum_out, sum_in, patches, tall, tiles, line,
):
    sources = (bwd_out_hbm, slope_out_hbm, active_hbm, bwd_mid_hbm, slope_in_hbm, turned_hbm, natural_hbm)
    targets = (bwd_out, slope_out, active, bwd_mid, slope_in, turned, natural)
    loads = [move(source, to, came, at) for at, (source, to) in enumerate(zip(sources, targets))]
    zero32 = jnp.zeros((96, 128), BF)
    stack[0:96, 1920:2048] = zero32
    stack[192:288, 0:128] = zero32
    for frame in range(16):
        value = grads[frame * 32 : frame * 32 + 32].astype(F32)
        shifted = [next_column(value).astype(BF), value.astype(BF), previous_column(value).astype(BF)]
        for time_off in range(3):
            to = frame + time_off - 1
            if 0 <= to < 16:
                for col_off in range(3):
                    at = (time_off * 3 + col_off) * 32
                    stack[at : at + 32, to * 128 : to * 128 + 128] = shifted[col_off]
    loads[0].wait()
    loads[1].wait()
    grad_mid[0] = jnp.zeros((5, 10, 16, 128), BF)
    grad_mid[17] = jnp.zeros((5, 10, 16, 128), BF)
    for group in range(4):
        product[...] = dot_first(stack[:, group * 512 : group * 512 + 512], bwd_out[...])

        def finish_mid(step, carry):
            frame = group * 4 + step
            added = []
            for pair in range(5):
                chunk = product[pl.ds(step * 128, 128), pair * 128 : pair * 128 + 128]
                slope = slope_out[pl.ds(frame * 128, 128), pair * 128 : pair * 128 + 128]
                value = (chunk * slope.astype(F32)).astype(BF).astype(F32)
                added.append(jnp.sum(value, axis=0, keepdims=True))

                def store(slabs, values):
                    grad_mid[frame + 1, pair, slabs] = values

                put_slabs(store, value)
            lane = lax.broadcasted_iota(jnp.int32, (1, 128), 1)
            own = added[1] + added[2] + added[3]
            own = own + jnp.where(lane >= 64, added[0], 0.0) + jnp.where(lane < 64, added[4], 0.0)
            return carry + own

        if group == 0:
            bias_mid = jnp.zeros((1, 128), F32)
        bias_mid = lax.fori_loop(0, 4, finish_mid, bias_mid)

    loads[2].wait()
    result = dot(stack[...], active[...])
    for pair in range(5):
        sum_out[pair] = result[:, pair * 128 : pair * 128 + 128]

    loads[3].wait()
    loads[4].wait()

    def input_side(pair_of, carry):
        pieces = []
        for step in range(4):
            for col_off in range(3):
                pieces.append(two_rows(grad_mid, pair_of * 2 + step, 0, 4, col_off))
        result = dot(jnp.concatenate(pieces, axis=1), bwd_mid[...])
        for pair in range(4):
            for side in range(2):
                frame = pair_of * 2 + side
                chunk = result[pair * 128 : pair * 128 + 128, side * 128 : side * 128 + 128]
                slope = slope_in[pl.ds(pl.multiple_of(frame * 128, 128), 128), pair * 128 : pair * 128 + 128]
                value = (chunk * slope.astype(F32)).astype(BF)
                at = pl.multiple_of(frame * 512 + pair * 128, 128)
                grad_in[pl.ds(at, 128), :] = value
                carry = carry + jnp.sum(value.astype(F32), axis=0, keepdims=True)
        return carry

    bias_in = lax.fori_loop(0, 8, input_side, jnp.zeros((1, 128), F32))

    sum_mid[...] = jnp.zeros_like(sum_mid)
    loads[5].wait()

    def mid_weights(frame, carry):
        left = turned[pl.ds(frame, 3)].reshape(384, 512)
        for col_off in range(3):
            right = two_rows(grad_mid, frame + 1, 0, 4, 2 - col_off)
            sum_mid[col_off] = sum_mid[col_off] + dot(left, right)
        return carry

    lax.fori_loop(0, 16, mid_weights, 0)

    loads[6].wait()
    patches[0:96, 0:512] = jnp.zeros((96, 512), BF)
    patches[192:288, 7680:8192] = jnp.zeros((96, 512), BF)
    for frame in range(16):
        value = natural[frame].astype(F32)
        shifted = (previous_column(value).astype(BF), natural[frame], next_column(value).astype(BF))
        for col_off in range(3):
            for pair in range(4):
                piece = shifted[col_off][pair * 16 + 16 : pair * 16 + 48]
                for time_off in range(3):
                    to = frame - time_off + 1
                    if 0 <= to < 16:
                        at = (time_off * 3 + col_off) * 32
                        lane = (to * 4 + pair) * 128
                        patches[at : at + 32, lane : lane + 128] = piece
    sum_in[...] = dot(patches[...], grad_in[...])

    tall[...] = jnp.zeros_like(tall)
    for time_off in range(3):
        for row_off in range(3):
            for col_off in range(3):
                tap = (time_off * 3 + row_off) * 3 + col_off
                at = time_off * 128
                upper = sum_mid[col_off, at : at + 64, (2 - row_off) * 64 : (2 - row_off) * 64 + 64]
                lower = sum_mid[col_off, at + 64 : at + 128, (3 - row_off) * 64 : (3 - row_off) * 64 + 64]
                tall[tap * 64 : tap * 64 + 64, 0:64] = upper + lower
                at = (time_off * 3 + col_off) * 32 + row_off * 8
                upper = sum_in[at : at + 8, 0:64]
                lower = sum_in[at + 8 : at + 16, 64:128]
                tall[1792 + tap * 8 : 1792 + tap * 8 + 8, 0:64] = upper + lower
    tall[2008:2009, 0:64] = bias_in[:, 0:64] + bias_in[:, 64:128]
    tall[2009:2010, 0:64] = bias_mid[:, 0:64] + bias_mid[:, 64:128]
    for tile in range(16):
        tiles[tile] = jnp.transpose(tall[tile * 128 : tile * 128 + 128])[0:64]
    for row_off in range(3):
        value = None
        for row in range(2, 10):
            lane = (row - 2 + row_off) * 64
            piece = sum_out[lane // 128, pl.ds(row, 18, stride=16), :][:, lane % 128 : lane % 128 + 64]
            value = piece if value is None else value + piece
        for time_off in range(3):
            for col_off in range(3):
                tap = (time_off * 3 + row_off) * 3 + col_off
                for part in range(2):
                    row = (time_off * 3 + col_off) * 2 + part
                    line[part : part + 1, tap * 64 : tap * 64 + 64] = value[row : row + 1]
    for owner in range(8):
        for part in range(2):
            for piece in range(4):
                at = owner * 216 + piece * 54
                row = owner * 8 + part * 4 + piece
                tiles[13, row : row + 1, 64:118] = line[part : part + 1, at : at + 54]
    for quarter in range(4):
        for owner in range(8):
            value = tiles[quarter * 4 : quarter * 4 + 4, owner * 8 : owner * 8 + 8]
            out[quarter * 8 + owner] = value.reshape(32, 128).astype(BF)


def sum_kernel(parts, stats, loss, shard, shared):
    total = parts[0].astype(F32)
    for source in range(1, 32):
        total = total + parts[source].astype(F32)
    divisor = jnp.maximum(stats[1:2, 0:1] * (2.0 * 128 * 128), 1.0)
    total = total / divisor
    shard[...] = total
    lane = lax.broadcasted_iota(jnp.int32, (32, 128), 1)
    shared[...] = jnp.where(lane == 0, jnp.sum(total * total), loss[0:1] + jnp.zeros((32, 128), F32))


def update_kernel(
    own, near, mid, far, messages, stats,
    w_in, w_mid, w_out, w_bias, f_in, f_mid, f_out, f_bias, s_in, s_mid, s_out, s_bias,
    loss_sum, valid_count, grad_norm, mf_in, mf_mid, mf_out, mf_bias, ms_in, ms_mid, ms_out, ms_bias,
    mw_in, mw_mid, mw_out, mw_bias, mc_in, mc_mid, mc_out, mc_bias,
    shards, g_mid, g_in, g_out, g_bias,
):
    f, half, chip, core = place()
    for slot, source in enumerate((own, near, mid, far)):
        shards[jnp.bitwise_xor(f, slot)] = source[...]
    message = jnp.sum(messages[...], axis=0, keepdims=True)
    norm = jnp.sqrt(message[:, 0:1])
    loss_sum[0, 0] = jnp.sum(message[:, 1:2])
    valid_count[0, 0] = jnp.sum(stats[1:2, 0:1]) * (2.0 * 128 * 128)
    grad_norm[0, 0] = jnp.sum(norm)
    factor = jnp.minimum(1.0, CLIP / (norm + 1e-06))

    def tile_of(tile):
        at = (tile % 4) * 8
        return shards[tile // 4, at : at + 8]

    for tile in range(13):
        g_mid[:, tile * 128 : tile * 128 + 128] = tile_of(tile)
    mixed = tile_of(13)
    g_mid[:, 1664:1728] = mixed[:, 0:64]
    for part in range(2):
        for piece in range(4):
            row = part * 4 + piece
            g_out[part : part + 1, piece * 54 : piece * 54 + 54] = mixed[row : row + 1, 64:118]
    g_in[:, 0:128] = tile_of(14)
    mixed = tile_of(15)
    g_in[:, 128:216] = mixed[:, 0:88]
    square = jnp.concatenate([mixed, jnp.zeros((120, 128), F32)], axis=0)
    g_bias[...] = jnp.transpose(square)[88:90, 0:8]
    for grad, weight, one, two, new_one, new_two, new_weight, new_copy in (
        (g_in, w_in, f_in, s_in, mf_in, ms_in, mw_in, mc_in),
        (g_mid, w_mid, f_mid, s_mid, mf_mid, ms_mid, mw_mid, mc_mid),
        (g_out, w_out, f_out, s_out, mf_out, ms_out, mw_out, mc_out),
        (g_bias, w_bias, f_bias, s_bias, mf_bias, ms_bias, mw_bias, mc_bias),
    ):
        results = adamw(weight[...], grad[...] * factor, one[...], two[...])
        for ref, value in zip((new_one, new_two, new_weight, new_copy), results):
            ref[...] = value


VECTOR = pl.BlockSpec(memory_space=pltpu.VMEM)
SCALAR = pl.BlockSpec(memory_space=pltpu.SMEM)
LEFT = pl.BlockSpec(memory_space=pl.ANY)


def shape(*dims, dtype=BF):
    return jax.ShapeDtypeStruct(dims, dtype)


def kernel_call(kernel, name, micros, operands, results, scratch, in_specs=None, out_specs=None):
    return pl.pallas_call(
        kernel,
        name=name,
        out_shape=results,
        in_specs=in_specs or [VECTOR] * len(operands),
        out_specs=out_specs or [VECTOR] * len(results),
        scratch_shapes=scratch,
        cost_estimate=pl.CostEstimate(flops=int(micros * 1e9), bytes_accessed=0, transcendentals=0),
        compiler_params=pltpu.CompilerParams(vmem_limit_bytes=VMEM),
    )(*operands)


def swap(value, axis, bit):
    return lax.ppermute(value, axis, [(i, i ^ bit) for i in range(lax.axis_size(axis))])


def by_rows(
    kspace, line_mask, valid_flags, target, conv_in, conv_mid, conv_out, conv_bias,
    first_in, first_mid, first_out, first_bias, second_in, second_mid, second_out, second_bias,
):
    tables = make_tables()

    mine, theirs, mine_target, theirs_target = kernel_call(
        lines_kernel,
        "prepare_lines",
        2,
        [
            valid_flags, kspace.reshape(2, 4, 32, 128), line_mask.reshape(8, 16), target.reshape(2, 4, 32, 128),
            tables["permute"], conv_mid[0, 0].T, conv_in[0].T, conv_out[0], conv_bias[0],
        ],
        [shape(144, 256), shape(144, 256), shape(64, 256), shape(64, 256)],
        [pltpu.VMEM((2, 80, 256), BF), pltpu.VMEM((2, 64, 256), BF), pltpu.VMEM((16, 8, 128), F32)],
        in_specs=[SCALAR] + [VECTOR] * 8,
    )

    beside, other, far = (swap(value, ("half", "chip"), step) for value, step in ((mine, 1), (theirs, 2), (theirs, 3)))

    def two(one, another):
        return jnp.concatenate([one[0:64], another[0:64], one[64:80] + another[64:80]], axis=0)

    half_a, half_b = two(mine, beside), two(other, far)
    near_a, near_b = swap(half_a, "frames", 1), swap(half_b, "frames", 2)
    far_a = swap(jnp.concatenate([half_a, near_a], axis=0), "frames", 2)
    far_b = swap(jnp.concatenate([half_b, near_b], axis=0), "frames", 1)

    chips = jnp.concatenate([mine[80:144], beside[80:144], other[80:144], far[80:144]], axis=0)
    others = swap(chips, "core", 1)
    scratch = [pltpu.VMEM((16, 64, 128), F32), pltpu.VMEM((2, 1792), F32), pltpu.VMEM((64, 128), F32)]
    fwd_in, fwd_mid, fwd_out, bias = kernel_call(
        forward_weight_kernel,
        "lay_out_forward_weights",
        4,
        [chips, others, tables["pick_out"]],
        [shape(1152, 768), shape(3072, 256), shape(640, 256), shape(8, 768, dtype=F32)],
        scratch,
    )
    far_a, far_b, bias = lax.optimization_barrier((far_a, far_b, bias))
    gathered = [half_a, half_b, near_a, near_b, far_a, far_b]
    gathered += [swap(piece, "core", 1) for piece in gathered]
    bias, theirs_target = lax.optimization_barrier((bias, theirs_target))
    theirs_target = swap(theirs_target, "half", 1)
    kept = [(16, 128, 128), (18, 128, 512), (2048, 640), (2048, 512), (2048, 640)]
    moved = [(144, 256)] * 4 + [(288, 256)] * 2 + [(144, 256)] * 4 + [(288, 256)] * 2 + [(128, 256), (1152, 768), (3072, 256)]
    branch, stats, lines, natural, turned, active, slope_in, slope_out = kernel_call(
        forward_kernel,
        "features_and_branch",
        27,
        [*gathered, tables["feature"], tables["columns"], fwd_in, fwd_mid, fwd_out, bias],
        [shape(256, 128), shape(8, 256, dtype=F32), shape(256, 128)] + [shape(*dims) for dims in kept],
        [pltpu.VMEM(dims, BF) for dims in moved]
        + [pltpu.SemaphoreType.DMA((15,))]
        + [
            pltpu.VMEM((20, 128, 256), BF),
            pltpu.VMEM((4, 8, 128), F32),
            pltpu.VMEM((24, 128), F32),
            pltpu.VMEM((18, 10, 16, 128), BF),
            pltpu.VMEM((18, 6, 10, 16, 128), BF),
            pltpu.VMEM((512, 768), F32),
            pltpu.VMEM((18, 144, 128), F32),
        ]
        + [pltpu.VMEM(dims, BF) for dims in kept]
        + [pltpu.SemaphoreType.DMA((5,))],
        in_specs=[LEFT] * 13 + [VECTOR] + [LEFT] * 2 + [VECTOR] * 2,
        out_specs=[VECTOR] * 3 + [LEFT] * 5,
    )
    branch, chips, others, mine_target, theirs_target = lax.optimization_barrier(
        (branch, chips, others, mine_target, theirs_target)
    )
    wanted = []
    for step in range(4):
        at = 16 * step
        image = jnp.concatenate([mine_target[at : at + 16], theirs_target[at : at + 16]], axis=0)
        wanted.append(swap(image, ("chip", "core"), step) if step else image)
    bwd_mid, bwd_out = kernel_call(
        backward_weight_kernel,
        "lay_out_backward_weights",
        3,
        [chips, others, tables["pick_back"]],
        [shape(3072, 256), shape(288, 640)],
        scratch,
    )
    by_frame = lax.all_to_all(branch.reshape(16, 16, 128), ("frames", "chip", "core"), 0, 0, tiled=True)
    grads, loss = kernel_call(
        consistency_kernel,
        "data_consistency",
        2.5,
        [
            by_frame.reshape(256, 128), lines, stats, *wanted,
            tables["to_lines"], tables["to_rows"], tables["lines_again"], tables["spread"],
        ],
        [shape(512, 128), shape(8, 128, dtype=F32)],
        [pltpu.VMEM((256, 128), BF)],
    )
    by_block = lax.all_to_all(grads.reshape(16, 32, 128), ("frames", "chip", "core"), 0, 0, tiled=True)
    moved = [(288, 640), (2048, 640), (2048, 640), (3072, 256), (2048, 512), (18, 128, 512), (16, 128, 128)]
    (parts,) = kernel_call(
        backward_kernel,
        "weight_gradients",
        27,
        [by_block.reshape(512, 128), bwd_out, slope_out, active, bwd_mid, slope_in, turned, natural],
        [shape(32, 32, 128)],
        [pltpu.VMEM(dims, BF) for dims in moved]
        + [pltpu.SemaphoreType.DMA((7,))]
        + [
            pltpu.VMEM((288, 2048), BF),
            pltpu.VMEM((512, 640), F32),
            pltpu.VMEM((18, 5, 10, 16, 128), BF),
            pltpu.VMEM((8192, 128), BF),
            pltpu.VMEM((3, 384, 256), F32),
            pltpu.VMEM((5, 288, 128), F32),
            pltpu.VMEM((288, 128), F32),
            pltpu.VMEM((288, 8192), BF),
            pltpu.VMEM((2048, 128), F32),
            pltpu.VMEM((16, 64, 128), F32),
            pltpu.VMEM((2, 1792), F32),
        ],
        in_specs=[VECTOR] + [LEFT] * 7,
    )
    parts = lax.all_to_all(parts, ("frames", "half", "chip", "core"), 0, 0, tiled=True)
    shard, messages = kernel_call(
        sum_kernel,
        "sum_gradients",
        2,
        [parts, stats, loss],
        [shape(32, 128, dtype=F32), shape(32, 128, dtype=F32)],
        [],
    )
    shards = [shard] + [swap(shard, "frames", step) for step in (1, 2, 3)]
    messages = lax.all_to_all(messages, ("frames", "half", "chip", "core"), 0, 0, tiled=True)
    groups = (
        (conv_in, conv_mid, conv_out, conv_bias),
        (first_in, first_mid, first_out, first_bias),
        (second_in, second_mid, second_out, second_bias),
    )
    state = []
    for of_in, of_mid, of_out, of_bias in groups:
        state += [of_in[0].T, of_mid[0, 0].T, of_out[0], of_bias[0]]
    shapes = [(8, 216), (8, 1728), (2, 216), (2, 8)]
    results = kernel_call(
        update_kernel,
        "adamw",
        2,
        [*shards, messages, stats, *state],
        [shape(1, 1, dtype=F32)] * 3
        + [shape(*dims, dtype=F32) for dims in shapes * 3]
        + [shape(*dims, dtype=BF) for dims in shapes],
        [pltpu.VMEM((4, 32, 128), F32)] + [pltpu.VMEM(shapes[at], F32) for at in (1, 0, 2, 3)],
        out_specs=[SCALAR] * 3 + [VECTOR] * 16,
    )
    outputs = [result[0, 0] for result in results[0:3]]
    for at in range(3, 19, 4):
        of_in, of_mid, of_out, of_bias = results[at : at + 4]
        outputs += [of_in.T[None], of_mid.T[None, None], of_out[None], of_bias[None]]
    return tuple(outputs)


def specs_for(rows):
    lines = P(None, "frames", rows)
    images = P(None, "frames", rows, None, None)
    weights = [P(None, None, rows), P(None, None, None, rows), P(None, None, rows), P(None, None, rows)]
    in_specs = (images, lines, P(None, "frames"), images, *(weights * 3))
    out_specs = (P(), P(), P(), *(weights * 4))
    return in_specs, out_specs


def solution(mesh):
    frames, rows = (mesh.shape[axis] for axis in ("frames", "rows"))
    if (frames, rows) != (4, 8):
        in_specs, out_specs = specs_for("rows")
        return jax.shard_map(local, mesh=mesh, in_specs=in_specs, out_specs=out_specs, check_vma=False)
    chips = Mesh(mesh.devices.reshape(frames, 2, rows // 4, 2), ("frames", "half", "chip", "core"))
    in_specs, out_specs = specs_for(("half", "chip", "core"))
    return jax.shard_map(by_rows, mesh=chips, in_specs=in_specs, out_specs=out_specs, check_vma=False)
```

```python
import jax
import jax.numpy as jnp
import ml_dtypes
import numpy as np
from jax import lax
from jax.experimental import pallas as pl
from jax.experimental.pallas import tpu as pltpu
from jax.sharding import Mesh
from jax.sharding import PartitionSpec as P

NX = 128
CAS = 1
MIDS = 1
STEP = 10


CLIP = 0.05
RATE = 0.03
BETA_ONE = 0.9
BETA_TWO = 0.999
EPSILON = 1e-08
DECAY = 0.01
HIGHEST = lax.Precision.HIGHEST


def with_halo(shard, sides, width):
    for axis, dim in sides:
        size, length = (lax.axis_size(axis), shard.shape[dim])
        up = [(i, (i + 1) % size) for i in range(size - 1)]
        down = [(j, i) for i, j in up]
        last = lax.slice_in_dim(shard, length - width, length, axis=dim)
        first = lax.slice_in_dim(shard, 0, width, axis=dim)
        before = lax.ppermute(last, axis, up)
        after = lax.ppermute(first, axis, down)
        shard = jnp.concatenate([before, shard, after], axis=dim)
    return shard


def from_behind(block, axis, distance):
    devices = range(lax.axis_size(axis))
    route = [(i - distance, i) for i in devices if i - distance in devices]
    return lax.ppermute(block, axis, route)


def dft_blocks(length, sign):
    counter = jnp.arange(length, dtype=jnp.int32)
    turns = counter[:, None] * counter[None, :] % length
    angle = turns.astype(jnp.float32) * (2.0 * jnp.pi / length)
    norm_factor = 1.0 / jnp.sqrt(jnp.float32(length))
    cosine = jnp.cos(angle) * norm_factor
    sine = sign * jnp.sin(angle) * norm_factor
    return jnp.stack([jnp.stack([cosine, -sine]), jnp.stack([sine, cosine])])


def transform(image, sign):
    rows_here = image.shape[1]
    rows_all = rows_here * lax.axis_size("rows")
    first_row = lax.axis_index("rows") * rows_here
    across = jnp.einsum(
        "byix,oikx->byok", image, dft_blocks(image.shape[3], sign), precision=HIGHEST
    )
    table = dft_blocks(rows_all, sign)
    window = lax.dynamic_slice(
        table, (0, 0, 0, first_row), (2, 2, lax.axis_size("rows") * rows_here, rows_here)
    )
    return lax.psum_scatter(
        jnp.einsum("byix,oiky->kbox", across, window, precision=HIGHEST),
        "rows",
        scatter_dimension=0,
        tiled=True,
    ).transpose(1, 0, 2, 3)


def taps(widened, offset, frames, rows_here, columns):
    time_off = offset // 3
    row_off = offset % 3
    return jnp.concatenate(
        [
            widened[
                time_off : time_off + frames,
                row_off : row_off + rows_here,
                :,
                col_off : col_off + columns,
            ]
            for col_off in range(3)
        ],
        axis=2,
    )


def convolve(padded, kernel):
    frames = padded.shape[0] - 2
    rows_here = padded.shape[1] - 2
    width_in = padded.shape[2]
    columns = padded.shape[3]
    widened = jnp.pad(padded, ((0, 0), (0, 0), (0, 0), (1, 1)))
    blocks = kernel.reshape(9, 3 * width_in, kernel.shape[1])
    summed = jnp.zeros((frames, rows_here, kernel.shape[1], columns), jnp.float32)
    for offset in range(9):
        gathered = taps(widened, offset, frames, rows_here, columns)
        summed = summed + jnp.einsum(
            "tykx,kj->tyjx", gathered, blocks[offset], preferred_element_type=jnp.float32
        )
    return summed


def kernel_grad(padded, grad_out):
    frames, rows_here, columns = (grad_out.shape[0], grad_out.shape[1], grad_out.shape[3])
    widened = jnp.pad(padded, ((0, 0), (0, 0), (0, 0), (1, 1)))
    pieces = [
        jnp.einsum(
            "tykx,tyjx->kj",
            taps(widened, offset, frames, rows_here, columns),
            grad_out,
            preferred_element_type=jnp.float32,
        )
        for offset in range(9)
    ]
    return jnp.concatenate(pieces, axis=0)


def flipped(kernel):
    width_in = kernel.shape[0] // 27
    shaped = kernel.reshape(3, 3, 3, width_in, kernel.shape[1])[::-1, ::-1, ::-1]
    return shaped.transpose(0, 1, 2, 4, 3).reshape(27 * kernel.shape[1], width_in)


def activation_rim(values):
    return with_halo(values, (("frames", 0), ("rows", 1)), 1)


def gradient_rim(values):
    return with_halo(values, (("frames", 0), ("rows", 1)), 1)


def layer_forward(inputs, kernel, bias_row):
    padded = activation_rim(inputs)
    return (padded, convolve(padded, kernel) + bias_row.astype(jnp.float32)[None, None, :, None])


def layer_backward(padded, kernel, grad_hidden, needs_input):
    kernel_delta = kernel_grad(padded, grad_hidden)
    bias_delta = jnp.sum(grad_hidden, axis=(0, 1, 3), dtype=jnp.float32)
    input_delta = None
    if needs_input:
        input_delta = convolve(gradient_rim(grad_hidden), flipped(kernel))
    return (kernel_delta, bias_delta, input_delta)


def share(measured, sampled):
    frames = measured.shape[0]
    reach = (frames + 1) // frames
    before = []
    after = []
    for distance in range(1, reach + 1):
        for direction in (1, -1):
            moved = from_behind((measured, sampled), "frames", direction * distance)
            if direction == 1:
                before.insert(0, moved)
            else:
                after.append(moved)
    data_line = jnp.concatenate(
        [moved_pair[0] for moved_pair in before]
        + [measured]
        + [moved_pair[0] for moved_pair in after],
        axis=0,
    )
    mask_line = jnp.concatenate(
        [moved_pair[1] for moved_pair in before]
        + [sampled]
        + [moved_pair[1] for moved_pair in after],
        axis=0,
    )
    centre = reach * frames
    windows = []
    for radius in range(3):
        data_sum = data_line[centre - radius : centre - radius + frames]
        mask_sum = mask_line[centre - radius : centre - radius + frames]
        for offset in range(1 - radius, radius + 1):
            data_sum = data_sum + data_line[centre + offset : centre + offset + frames]
            mask_sum = mask_sum + mask_line[centre + offset : centre + offset + frames]
        windows.append(data_sum / jnp.maximum(mask_sum, 1.0)[:, :, None, None])
    return jnp.stack(windows, 1)


def adamw(weight, grad_piece, moment_one, moment_two):
    first_new = BETA_ONE * moment_one + (1.0 - BETA_ONE) * grad_piece
    second_new = BETA_TWO * moment_two + (1.0 - BETA_TWO) * grad_piece * grad_piece
    ascent = (
        first_new
        / (1.0 - BETA_ONE**STEP)
        / (jnp.sqrt(second_new / (1.0 - BETA_TWO**STEP)) + EPSILON)
    )
    weight_new = weight - RATE * (ascent + DECAY * weight)
    return (first_new, second_new, weight_new, weight_new.astype(jnp.bfloat16))


def local(
    kspace,
    line_mask,
    valid_flags,
    target,
    conv_in,
    conv_mid,
    conv_out,
    conv_bias,
    first_in,
    first_mid,
    first_out,
    first_bias,
    second_in,
    second_mid,
    second_out,
    second_bias,
):
    masters = (conv_in, conv_mid, conv_out, conv_bias)

    def reduce_grads(grads):
        shards = (
            lax.psum_scatter(
                grads[0].astype(jnp.bfloat16), "rows", scatter_dimension=2, tiled=True
            ).astype(jnp.float32),
            lax.psum_scatter(
                grads[1].astype(jnp.bfloat16), "rows", scatter_dimension=3, tiled=True
            ).astype(jnp.float32),
            lax.psum_scatter(
                grads[2].astype(jnp.bfloat16), "rows", scatter_dimension=2, tiled=True
            ).astype(jnp.float32),
            lax.psum_scatter(
                grads[3].astype(jnp.bfloat16), "rows", scatter_dimension=2, tiled=True
            ).astype(jnp.float32),
        )
        return lax.psum((shards[0], shards[1], shards[2], shards[3]), "frames")

    def micro_batch(carry, batch_data):
        grad_carry, loss_carry, count_carry = carry
        measured_full, mask_rows, frame_flags, wanted = batch_data
        full_in, full_mid, full_out, full_bias = (
            lax.all_gather(conv_in.astype(jnp.bfloat16), "rows", axis=2, tiled=True),
            lax.all_gather(conv_mid.astype(jnp.bfloat16), "rows", axis=3, tiled=True),
            lax.all_gather(conv_out.astype(jnp.bfloat16), "rows", axis=2, tiled=True),
            lax.all_gather(conv_bias.astype(jnp.bfloat16), "rows", axis=2, tiled=True),
        )
        sampled = mask_rows.astype(jnp.float32)
        measured = measured_full * sampled[:, :, None, None]
        shared = share(measured, sampled)
        frames, rows_here = (measured.shape[0], measured.shape[1])
        images = transform(shared.reshape(frames * 3, rows_here, 2, NX), 1.0).reshape(
            frames, 3, rows_here, 2, NX
        )
        shared_images = images.transpose(0, 2, 1, 3, 4).reshape(frames, rows_here, 6, NX)
        current = images[:, 0]
        unsampled = (1.0 - sampled)[:, :, None, None]
        no_bias = jnp.zeros((2,), jnp.bfloat16)

        def kernels_of(cascade):
            return [full_in[cascade]] + [full_mid[cascade, 0]] + [full_out[cascade].T]

        cascade = 0
        kernels = kernels_of(cascade)
        biases = [full_bias[cascade, layer_at] for layer_at in range(MIDS + 1)] + [no_bias]
        inputs = jnp.concatenate([current, shared_images], axis=2).astype(jnp.bfloat16)
        saved = []
        for layer_at in range(MIDS + 2):
            padded, hidden = layer_forward(inputs, kernels[layer_at], biases[layer_at])
            saved.append((padded, hidden))
            if layer_at < MIDS + 1:
                inputs = jax.nn.gelu(hidden).astype(jnp.bfloat16)
        current = transform(unsampled * transform(current + hidden, -1.0) + measured, 1.0)
        kept = [saved]
        frame_weight = frame_flags.astype(jnp.float32)[:, None, None, None]
        residual_error = current - wanted
        loss_part = jnp.sum(frame_weight * residual_error * residual_error)
        count_part = 2.0 * rows_here * NX * jnp.sum(frame_flags.astype(jnp.float32))
        grad_current = 2.0 * frame_weight * residual_error
        delta_in = [None] * CAS
        delta_mid = [None] * CAS
        delta_out = [None] * CAS
        delta_bias = [None] * CAS
        for cascade in reversed(range(CAS)):
            kernels = kernels_of(cascade)
            grad_sum = transform(unsampled * transform(grad_current, -1.0), 1.0)
            grad_hidden = grad_sum.astype(jnp.bfloat16)
            kernel_deltas = [None] * (MIDS + 2)
            bias_deltas = [None] * (MIDS + 2)
            grad_input = None
            for layer_at in reversed(range(MIDS + 2)):
                padded, hidden = kept[cascade][layer_at]
                if layer_at < MIDS + 1:
                    pullback = jax.vjp(jax.nn.gelu, hidden)[1]
                    grad_hidden = pullback(grad_input)[0].astype(jnp.bfloat16)
                needs_input = cascade > 0 or layer_at > 0
                kernel_deltas[layer_at], bias_deltas[layer_at], grad_input = layer_backward(
                    padded, kernels[layer_at], grad_hidden, needs_input
                )
            delta_in[cascade] = kernel_deltas[0]
            delta_mid[cascade] = jnp.stack(kernel_deltas[1 : MIDS + 1])
            delta_out[cascade] = kernel_deltas[MIDS + 1].T
            delta_bias[cascade] = jnp.stack(bias_deltas[0 : MIDS + 1])
        grads = (
            jnp.stack(delta_in),
            jnp.stack(delta_mid),
            jnp.stack(delta_out),
            jnp.stack(delta_bias),
        )
        grads = reduce_grads(grads)
        grad_carry = jax.tree.map(jnp.add, grad_carry, grads)
        return ((grad_carry, loss_carry + loss_part, count_carry + count_part), None)

    start_grads = jax.tree.map(jnp.zeros_like, masters)
    start = (start_grads, jnp.zeros((), jnp.float32), jnp.zeros((), jnp.float32))
    (summed, loss_local, count_local), unused = lax.scan(
        micro_batch, start, (kspace, line_mask, valid_flags, target)
    )
    summed = tuple(summed)
    loss_sum, valid_count = lax.psum((loss_local, count_local), ("frames", "rows"))
    divisor = jnp.maximum(valid_count, 1.0)
    grads = [grad_piece / divisor for grad_piece in summed]
    squares = sum((jnp.sum(grad_piece * grad_piece) for grad_piece in grads))
    grad_norm = jnp.sqrt(lax.psum(squares, "rows"))
    factor = jnp.minimum(1.0, CLIP / (grad_norm + 1e-06))
    firsts = (first_in, first_mid, first_out, first_bias)
    seconds = (second_in, second_mid, second_out, second_bias)
    results = [
        adamw(masters[which], grads[which] * factor, firsts[which], seconds[which])
        for which in range(4)
    ]
    return (
        loss_sum,
        valid_count,
        grad_norm,
        results[0][0],
        results[1][0],
        results[2][0],
        results[3][0],
        results[0][1],
        results[1][1],
        results[2][1],
        results[3][1],
        results[0][2],
        results[1][2],
        results[2][2],
        results[3][2],
        results[0][3],
        results[1][3],
        results[2][3],
        results[3][3],
    )


BF = jnp.bfloat16
F32 = jnp.float32
SQRT_TWO_OVER_PI = 0.7978845608028654
CUBIC = 0.044715 * SQRT_TWO_OVER_PI
UNITS = 16
VMEM = 56 * 2**20


def column_order():
    lanes = np.arange(128)
    return (lanes % 16) * 8 + lanes // 16


def dft_tables(sign):
    counter = np.arange(128)
    angle = (counter[:, None] * counter[None, :] % 128) * (2.0 * np.pi / 128)
    cosine, sine = np.cos(angle) / np.sqrt(128.0), sign * np.sin(angle) / np.sqrt(128.0)
    return np.stack([np.stack([cosine, -sine]), np.stack([sine, cosine])])


def make_tables():
    inverse, forward = dft_tables(1.0), dft_tables(-1.0)
    order = column_order()
    columns = inverse[:, :, :, order].transpose(1, 2, 0, 3).reshape(256, 256)
    blocks = np.arange(UNITS)[:, None] * 8

    def rows_of(first, kept):
        rows = blocks + first + np.arange(16)[None, :]
        inside = (rows >= 0) & (rows < 128) & (np.arange(16)[None, :] < kept)
        return np.clip(rows, 0, 127), inside

    rows, inside = rows_of(-3, 14)
    feature = inverse[:, :, rows, :] * inside[None, None, :, :, None]
    feature = feature.transpose(2, 3, 0, 1, 4).reshape(UNITS, 16, 2, 256)
    feature = np.tile(feature, (1, 1, 4, 1)).reshape(UNITS, 128, 256)
    to_lines = forward.reshape(2, 2, 128, UNITS, 8).transpose(0, 2, 3, 1, 4).reshape(256, 256)
    to_rows = inverse.transpose(0, 2, 1, 3).reshape(256, 256)
    lines_again = forward.transpose(0, 2, 1, 3).reshape(256, 256)
    rows, inside = rows_of(-2, 12)
    spread = inverse[:, :, rows, :] * inside[None, None, :, :, None]
    spread = spread.transpose(2, 0, 3, 1, 4).reshape(UNITS * 32, 256)
    permute = np.zeros((128, 128))
    permute[order, np.arange(128)] = 1.0
    pick_out = np.zeros((64, 10, 256))
    pick_back = np.zeros((10, 288, 64))
    for time_off in range(3):
        for row_off in range(3):
            for col_off in range(3):
                tap = (time_off * 3 + row_off) * 3 + col_off
                for part in range(2):
                    for row in range(8):
                        lane = (time_off * 3 + col_off) * 16 + part * 8 + row
                        pick_out[tap * 2 + part, row + row_off, lane] = 1.0
                    for row in range(12):
                        into = row + row_off - 2
                        if 0 <= into < 10:
                            at = (time_off * 3 + col_off) * 32 + part * 16 + row
                            pick_back[into, at, tap * 2 + part] = 1.0
    made = dict(
        columns=columns,
        feature=feature,
        to_lines=to_lines,
        lines_again=lines_again,
        to_rows=to_rows,
        spread=spread,
        permute=permute,
        pick_out=pick_out.reshape(64, 2560),
        pick_back=pick_back.reshape(2880, 64),
    )
    return {name: jnp.asarray(table.astype(ml_dtypes.bfloat16)) for name, table in made.items()}


def dot(left, right):
    return jnp.dot(left, right, preferred_element_type=F32)


def dot_first(left, right):
    return lax.dot_general(left, right, (((0,), (0,)), ((), ())), preferred_element_type=F32)


def next_column(values):
    lane = lax.broadcasted_iota(jnp.int32, values.shape, 1)
    inner = pltpu.roll(values, 112, 1)
    wrapped = jnp.where(lane == 127, 0.0, pltpu.roll(values, 111, 1))
    return jnp.where(lane < 112, inner, wrapped)


def previous_column(values):
    lane = lax.broadcasted_iota(jnp.int32, values.shape, 1)
    inner = pltpu.roll(values, 16, 1)
    wrapped = jnp.where(lane == 0, 0.0, pltpu.roll(values, 17, 1))
    return jnp.where(lane >= 16, inner, wrapped)


def put_slabs(store, values):
    store(slice(1, 9), values.astype(BF).reshape(8, 16, 128))
    first, last = values[0:16], values[112:128]
    at = lax.broadcasted_iota(jnp.int32, (16, 128), 0)
    before = jnp.where(at == 0, 0.0, pltpu.roll(last, 1, 0))
    after = jnp.where(at == 15, 0.0, pltpu.roll(first, 15, 0))
    store(slice(0, 1), before.astype(BF).reshape(1, 16, 128))
    store(slice(9, 10), after.astype(BF).reshape(1, 16, 128))


def two_rows(ref, frame, pair, count, first_slab):
    upper = ref[frame, pair : pair + count, first_slab : first_slab + 8]
    lower = ref[frame, pair + 1 : pair + 1 + count, first_slab : first_slab + 8]
    rows = count * 128
    return jnp.concatenate([upper.reshape(rows, 128), lower.reshape(rows, 128)], axis=1)


def gelu_and_slope(hidden):
    square = hidden * hidden
    half = 0.5 * jnp.tanh(hidden * (CUBIC * square + SQRT_TWO_OVER_PI)) + 0.5
    active = hidden * half
    slope = half + active * (1.0 - half) * (6.0 * CUBIC * square + 2.0 * SQRT_TWO_OVER_PI)
    return active, slope


def place():
    return tuple(lax.axis_index(name) for name in ("frames", "half", "chip", "core"))


def lines_kernel(
    valid, kspace, line_mask, target, columns_table, permute, conv_mid, conv_in, conv_out, conv_bias,
    mine, theirs, theirs_and_target, mine_target, both, images, tiles,
):
    f, half, chip, core = place()
    quarter = chip * 2 + core
    sampled = line_mask[...].astype(F32)
    wide = jnp.concatenate([sampled, jnp.zeros((8, 112), F32)], axis=1)
    column = jnp.transpose(jnp.concatenate([wide, jnp.zeros((120, 128), F32)], axis=0))
    placed = pltpu.roll(wide, (half * 4 + quarter) * 16, 1)
    total = jnp.zeros((1, 128), F32)
    flags = []
    for batch in range(2):
        for frame in range(4):
            flag = jnp.zeros((1, 128), F32) + valid[batch, frame].astype(F32)
            flags.append(flag)
            total = total + flag
    for batch in range(2):
        shown = [[], []]
        sampled_lines = []
        for frame in range(4):
            at = batch * 4 + frame
            own = column[0:16, at : at + 1]
            lines = [kspace[batch, frame, pl.ds(part, 16, stride=2), :] * own for part in range(2)]
            sampled_lines.append(jnp.concatenate(lines, axis=1).astype(BF))
            for part in range(2):
                shown[part].append(target[batch, frame, pl.ds(part, 16, stride=2), :])
        both[batch, 0:64] = dot(jnp.concatenate(sampled_lines, axis=0), columns_table[...]).astype(BF)
        rows = [placed[batch * 4 : batch * 4 + 4]] + flags[batch * 4 : batch * 4 + 4] + [total, jnp.zeros((7, 128), F32)]
        both[batch, 64:80, 0:128] = jnp.concatenate(rows, axis=0).astype(BF)
        both[batch, 64:80, 128:256] = jnp.zeros((16, 128), BF)
        for part in range(2):
            image = jnp.concatenate(shown[part], axis=0).astype(BF)
            image = dot(image, permute[...]).astype(BF)
            for frame in range(4):
                row = pl.multiple_of(16 * jnp.bitwise_xor(quarter, frame), 16)
                images[batch, pl.ds(row, 16), part * 128 : part * 128 + 128] = image[frame * 16 : frame * 16 + 16]
    mine[0:80] = both[half]
    theirs[0:80] = both[1 - half]
    theirs_and_target[0:80] = both[1 - half]
    mine_target[...] = images[half]
    theirs_and_target[144:208] = images[1 - half]
    tiles[...] = jnp.zeros_like(tiles)
    for tile in range(13):
        tiles[tile] = conv_mid[:, tile * 128 : tile * 128 + 128]
    tiles[13, :, 0:64] = conv_mid[:, 1664:1728]
    for part in range(2):
        for piece in range(4):
            row = part * 4 + piece
            tiles[13, row : row + 1, 64:118] = conv_out[part : part + 1, piece * 54 : piece * 54 + 54]
    tiles[14] = conv_in[:, 0:128]
    tiles[15, :, 0:88] = conv_in[:, 128:216]
    wide = jnp.concatenate([conv_bias[...], jnp.zeros((2, 120), F32)], axis=1)
    wide = jnp.transpose(jnp.concatenate([wide, jnp.zeros((126, 128), F32)], axis=0))
    tiles[15, :, 88:90] = wide[0:8, 0:2]
    packed = tiles[...].reshape(128, 128).astype(BF)
    packed = jnp.concatenate([packed[0:64], packed[64:128]], axis=1)
    mine[80:144] = packed
    theirs[80:144] = packed
    theirs_and_target[80:144] = packed


def unpack_weights(own, other, whole):
    f, half, chip, core = place()
    for side, source in enumerate((own, other)):
        for slot in range(4):
            row = jnp.bitwise_xor(half * 4 + chip * 2 + core, slot * 2 + side)
            row = pl.multiple_of(row * 8, 8)
            values = source[slot * 64 : slot * 64 + 64].astype(F32)
            for part in range(2):
                half_of = values[:, part * 128 : part * 128 + 128].reshape(8, 8, 128)
                whole[part * 8 : part * 8 + 8, pl.ds(row, 8), :] = half_of


def unpack_last(whole, line, taps):
    for owner in range(8):
        for part in range(2):
            for piece in range(4):
                at = owner * 216 + piece * 54
                row = owner * 8 + part * 4 + piece
                line[part : part + 1, at : at + 54] = whole[13, row : row + 1, 64:118]
    taps[...] = jnp.zeros_like(taps)
    for tap in range(27):
        for part in range(2):
            row = tap * 2 + part
            taps[row : row + 1, 0:64] = line[part : part + 1, tap * 64 : tap * 64 + 64]
    return taps[...].astype(BF)[:, 0:64]


def forward_weight_kernel(own, other, pick_out, fwd_in, fwd_mid, fwd_out, bias, whole, line, taps):
    unpack_weights(own, other, whole)
    zero = jnp.zeros((64, 64), F32)
    turned = [jnp.transpose(whole[tile]) for tile in range(16)]

    def of_tap(time_off, row_off, col_off):
        tap = (time_off * 3 + row_off) * 3 + col_off
        return turned[tap // 2][(tap % 2) * 64 : (tap % 2) * 64 + 64]

    for time_off in range(4):
        for col_off in range(3):
            at = (time_off * 3 + col_off) * 256
            if time_off == 0:
                fwd_mid[at : at + 256, 128:256] = jnp.zeros((256, 128), BF)
            if time_off == 3:
                fwd_mid[at : at + 256, 0:128] = jnp.zeros((256, 128), BF)
    for time_off in range(3):
        for col_off in range(3):
            for level in range(4):
                left = of_tap(time_off, level, col_off) if level < 3 else zero
                right = of_tap(time_off, level - 1, col_off) if level > 0 else zero
                strip = jnp.concatenate([left, right], axis=1).astype(BF)
                for pair in range(2):
                    at = ((time_off + pair) * 3 + col_off) * 256 + level * 64
                    fwd_mid[at : at + 64, pair * 128 : pair * 128 + 128] = strip
    first = jnp.concatenate([turned[14], turned[15]], axis=0)
    fwd_in[...] = jnp.zeros_like(fwd_in)
    pad = jnp.zeros((8, 64), F32)
    for time_off in range(3):
        for col_off in range(3):
            three = []
            for row_off in range(3):
                tap = (time_off * 3 + row_off) * 3 + col_off
                three.append(first[tap * 8 : tap * 8 + 8, 0:64])
            left = jnp.concatenate(three + [pad], axis=0)
            right = jnp.concatenate([pad] + three, axis=0)
            strip = jnp.concatenate([left, right], axis=1).astype(BF)
            at = (time_off * 3 + col_off) * 128
            for pair in range(6):
                fwd_in[at + pair * 16 : at + pair * 16 + 32, pair * 128 : pair * 128 + 128] = strip
    bias[...] = jnp.zeros_like(bias)
    for layer in range(2):
        row = turned[15][88 + layer : 89 + layer, 0:64]
        row = jnp.concatenate([row, row], axis=1)
        for pair in range(6):
            bias[layer : layer + 1, pair * 128 : pair * 128 + 128] = row
    spread = dot_first(unpack_last(whole, line, taps), pick_out[...]).astype(BF)
    for row in range(10):
        fwd_out[row * 64 : row * 64 + 64, :] = spread[:, row * 256 : row * 256 + 256]


def backward_weight_kernel(own, other, pick_back, bwd_mid, bwd_out, whole, line, taps):
    unpack_weights(own, other, whole)
    zero = jnp.zeros((64, 64), F32)
    plain = [whole[tile] for tile in range(14)]

    def of_tap(time_off, row_off, col_off):
        tap = (time_off * 3 + row_off) * 3 + col_off
        return plain[tap // 2][:, (tap % 2) * 64 : (tap % 2) * 64 + 64]

    for time_off in range(4):
        for col_off in range(3):
            at = (time_off * 3 + col_off) * 256
            if time_off == 0:
                bwd_mid[at : at + 256, 128:256] = jnp.zeros((256, 128), BF)
            if time_off == 3:
                bwd_mid[at : at + 256, 0:128] = jnp.zeros((256, 128), BF)
    for time_off in range(3):
        for col_off in range(3):
            for level in range(4):
                left = of_tap(time_off, 2 - level, col_off) if level < 3 else zero
                right = of_tap(time_off, 3 - level, col_off) if level > 0 else zero
                strip = jnp.concatenate([left, right], axis=1).astype(BF)
                for pair in range(2):
                    at = ((2 + pair - time_off) * 3 + 2 - col_off) * 256 + level * 64
                    bwd_mid[at : at + 64, pair * 128 : pair * 128 + 128] = strip
    back = dot(pick_back[...], unpack_last(whole, line, taps)).astype(BF)
    for pair in range(5):
        at = pair * 2 * 288
        bwd_out[:, pair * 128 : pair * 128 + 128] = jnp.concatenate(
            [back[at : at + 288], back[at + 288 : at + 576]], axis=1
        )


def move(source, target, semaphores, at):
    copy = pltpu.make_async_copy(source, target, semaphores.at[at])
    copy.start()
    return copy


def forward_kernel(*refs):
    gathered, refs = refs[0:12], refs[12:]
    row_tables, fwd_in_hbm, fwd_mid_hbm, fwd_out, bias = refs[0:5]
    branch, stats, lines, natural_hbm, turned_hbm, active_hbm, slope_in_hbm, slope_out_hbm = refs[5:13]
    rows_table, fwd_in, fwd_mid, came = refs[13:17]
    spectrum, masks, seen, feature, active, hidden, second, taps, natural, turned, active_out, slope_in, slope_out, done = refs[17:]
    f, half, chip, core = place()
    quarter = chip * 2 + core
    block = f * 4 + quarter
    loads = [move(row_tables.at[block], rows_table, came, 0), move(fwd_in_hbm, fwd_in, came, 1)]
    spectrum[0:2] = jnp.zeros((2, 128, 256), BF)
    spectrum[18:20] = jnp.zeros((2, 128, 256), BF)
    feature[0] = jnp.zeros((10, 16, 128), BF)
    feature[17] = jnp.zeros((10, 16, 128), BF)
    active[0] = jnp.zeros((6, 10, 16, 128), BF)
    active[17] = jnp.zeros((6, 10, 16, 128), BF)
    turned[0] = jnp.zeros((128, 512), BF)
    turned[17] = jnp.zeros((128, 512), BF)
    taps[0] = jnp.zeros((144, 128), F32)
    taps[17] = jnp.zeros((144, 128), F32)
    total = jnp.zeros((1, 128), F32)
    masks[...] = jnp.zeros_like(masks)
    for at in range(12):
        side, which = at // 6, at % 6
        held = ((0,), (0,), (1,), (2,), (2, 3), (1, 3))[which]
        for piece, turn in enumerate(held):
            group = jnp.bitwise_xor(f, turn)
            rows = gathered[at][piece * 144 : piece * 144 + 144]
            for other in range(2):
                chips_away = which % 2 * 2 + other
                row = jnp.bitwise_xor(half * 4 + quarter, chips_away * 2 + side) * 16
                row = pl.multiple_of(row, 16)
                for frame in range(4):
                    line = rows[other * 64 + frame * 16 : other * 64 + frame * 16 + 16]
                    spectrum[2 + group * 4 + frame, pl.ds(row, 16), :] = line
            flags = rows[128:144, 0:128].astype(F32)
            if side == 0 and which % 2 == 0:
                total = total + 0.5 * flags[8:9]
                masks[group] = masks[group] + flags[0:8]
            else:
                masks[group, 0:4] = masks[group, 0:4] + flags[0:4]
    seen[...] = jnp.zeros_like(seen)
    for group in range(4):
        seen[2 + group * 4 : 6 + group * 4] = masks[group, 0:4]
    stats[...] = jnp.zeros_like(stats)
    for part in range(2):
        stats[0:1, part * 128 : part * 128 + 128] = 1.0 - masks[f, pl.ds(quarter, 1), :]
    stats[1:2, 0:128] = total
    stats[2:3, 0:128] = 0.5 * masks[f, pl.ds(4 + quarter, 1), :]
    mine = spectrum[2 + block]
    lines[0:128] = mine[:, 0:128]
    lines[128:256] = mine[:, 128:256]
    sampled = seen[0:20]
    reach = [sampled[2:18]]
    reach.append(sampled[1:17] + sampled[2:18] + sampled[3:19])
    reach.append(reach[1] + sampled[0:16] + sampled[4:20])
    scales = [1.0 / jnp.maximum(count, 1.0) for count in reach]
    scales = [jnp.concatenate([scale, scale], axis=1) for scale in scales]

    loads[0].wait()
    channel = lax.rem(lax.broadcasted_iota(jnp.int32, (128, 256), 0), 8)
    table = rows_table[...].astype(F32)
    tables = [
        jnp.where(channel < 4, table, 0.0),
        jnp.where((channel == 4) | (channel == 5), table, 0.0),
        jnp.where(channel > 5, table, 0.0),
    ]
    for frame in range(16):
        near = [spectrum[frame + step].astype(F32) for step in range(5)]
        sums = [near[2]]
        sums.append(near[1] + near[2] + near[3])
        sums.append(sums[1] + near[0] + near[4])
        left = [(tables[radius] * scales[radius][frame : frame + 1]).astype(BF) for radius in range(3)]
        right = []
        for radius in range(3):
            value = sums[radius].astype(BF)
            right += [value[:, 0:128], value[:, 128:256]]
        image = dot(jnp.concatenate(left, axis=1), jnp.concatenate(right, axis=0))
        natural[frame] = image.astype(BF)

        def store(slabs, values, frame=frame):
            feature[frame + 1, slabs] = values

        put_slabs(store, jnp.transpose(image))
    move(natural, natural_hbm, done, 0)
    loads.append(move(fwd_mid_hbm, fwd_mid, came, 2))
    loads[1].wait()
    half_lane = lax.broadcasted_iota(jnp.int32, (1, 128), 1) // 64

    def finish_first(frame, pair, at):
        chunk = hidden[at : at + 128, pair * 128 : pair * 128 + 128]
        value, slope = gelu_and_slope(chunk + bias[0:1, pair * 128 : pair * 128 + 128])
        if pair in (0, 5):
            row = block * 8 - 2 + 2 * pair + half_lane
            value = jnp.where((row >= 0) & (row < 128), value, 0.0)
        else:
            at = (pair - 1) * 128
            slope_in[pl.ds(pl.multiple_of(frame * 128, 128), 128), at : at + 128] = slope.astype(BF)
            turned[frame + 1, :, at : at + 128] = jnp.transpose(value.astype(BF))

        def store(slabs, values):
            active[frame + 1, pair, slabs] = values

        put_slabs(store, value)

    def first_layer(group, carry):
        for step in range(4):
            for pair in range(6):
                finish_first((group - 1) * 4 + step, pair, step * 128)
        pieces = []
        for time_off in range(3):
            for col_off in range(3):
                piece = feature[pl.ds(group * 4 + time_off, 4), col_off : col_off + 8]
                pieces.append(piece.reshape(512, 128))
        made = dot(jnp.concatenate(pieces, axis=1), fwd_in[...])
        hidden[...] = made
        return carry

    group = 0
    pieces = []
    for time_off in range(3):
        for col_off in range(3):
            piece = feature[pl.ds(group * 4 + time_off, 4), col_off : col_off + 8]
            pieces.append(piece.reshape(512, 128))
    made = dot(jnp.concatenate(pieces, axis=1), fwd_in[...])
    hidden[...] = made
    lax.fori_loop(1, 4, first_layer, 0)
    for step in range(4):
        for pair in range(6):
            finish_first(12 + step, pair, step * 128)
    move(slope_in, slope_in_hbm, done, 2)
    move(turned, turned_hbm, done, 1)
    loads[2].wait()

    def finish_second(pair_of, pair, at):
        for side in range(2):
            chunk = second[at : at + 128, side * 128 : side * 128 + 128]
            value, slope = gelu_and_slope(chunk + bias[1:2, 0:128])
            if pair in (0, 4):
                row = block * 8 - 1 + 2 * pair + half_lane
                inside = (row >= 0) & (row < 128)
                value = jnp.where(inside, value, 0.0)
                slope = jnp.where(inside, slope, 0.0)
            row = pl.multiple_of((pair_of * 2 + side) * 128, 128)
            active_out[pl.ds(row, 128), pair * 128 : pair * 128 + 128] = value.astype(BF)
            slope_out[pl.ds(row, 128), pair * 128 : pair * 128 + 128] = slope.astype(BF)

    def finish_group(group):
        for step in range(2):
            for pair in range(5):
                finish_second(group * 2 + step, pair, step * 640 + pair * 128)
        rows = pl.ds(pl.multiple_of(group * 512, 512), 512)
        made = dot(active_out[rows], fwd_out[...])
        for frame in range(4):
            taps[group * 4 + frame + 1] = jnp.transpose(made[frame * 128 : frame * 128 + 128])[0:144]
        move(active_out.at[rows], active_hbm.at[rows], done, 3)
        move(slope_out.at[rows], slope_out_hbm.at[rows], done, 4)

    def second_product(group):
        rows = []
        for half_of in range(2):
            pieces = []
            for step in range(4):
                for col_off in range(3):
                    pieces.append(two_rows(active, group * 4 + half_of * 2 + step, 0, 5, col_off))
            rows.append(jnp.concatenate(pieces, axis=1))
        return dot(jnp.concatenate(rows, axis=0), fwd_mid[...])

    def second_layer(group, carry):
        finish_group(group - 1)
        second[...] = second_product(group)
        return carry

    second[...] = second_product(0)
    lax.fori_loop(1, 4, second_layer, 0)
    finish_group(3)
    for frame in range(16):
        columns = []
        for col_off in range(3):
            value = None
            for time_off in range(3):
                at = (time_off * 3 + col_off) * 16
                piece = taps[frame + time_off, at : at + 16]
                value = piece if value is None else value + piece
            columns.append(value)
        result = previous_column(columns[0]) + columns[1] + next_column(columns[2])
        branch[frame * 16 : frame * 16 + 16] = result.astype(BF)
    stored = (natural, turned, slope_in, active_out, slope_out)
    homes = (natural_hbm, turned_hbm, slope_in_hbm, active_hbm, slope_out_hbm)
    for at, (source, to) in enumerate(zip(stored, homes)):
        pltpu.make_async_copy(source, to, done.at[at]).wait()


def consistency_kernel(
    gathered, lines, stats, own, one, two, three, to_lines, to_rows, lines_again, spread, out, loss, target
):
    f, half, chip, core = place()
    for slot, source in enumerate((own, one, two, three)):
        for other in range(2):
            row = jnp.bitwise_xor(half * 4 + chip * 2 + core, other * 4 + slot) * 16
            row = pl.multiple_of(row, 16)
            at = other * 16
            for part in range(2):
                target[pl.ds(part * 128 + row, 16), :] = source[at : at + 16, part * 128 : part * 128 + 128]
    weight = stats[2:3, 0:128]
    free = jnp.transpose(jnp.zeros((128, 128), F32) + stats[0:1, 0:128])
    free = jnp.concatenate([free, free], axis=0)
    wanted = target[...]
    made = dot(to_lines[...], gathered[...])
    wanted_spectrum = dot(lines_again[...], wanted)
    held = lines[...].astype(F32)
    kept = free * (made + held) + held
    grad = (free * (kept - wanted_spectrum) * (2.0 * weight)).astype(BF)
    out[...] = dot(spread[...], grad).astype(BF)
    residual = dot(to_rows[...], kept.astype(BF)) - wanted.astype(F32)
    loss[...] = jnp.zeros((8, 128), F32) + jnp.sum(residual * residual * weight)


def backward_kernel(
    grads, bwd_out_hbm, slope_out_hbm, active_hbm, bwd_mid_hbm, slope_in_hbm, turned_hbm, natural_hbm,
    out,
    bwd_out, slope_out, active, bwd_mid, slope_in, turned, natural, came,
    stack, product, grad_mid, grad_in, sum_mid, sum_out, sum_in, patches, tall, tiles, line,
):
    sources = (bwd_out_hbm, slope_out_hbm, active_hbm, bwd_mid_hbm, slope_in_hbm, turned_hbm, natural_hbm)
    targets = (bwd_out, slope_out, active, bwd_mid, slope_in, turned, natural)
    loads = [move(source, to, came, at) for at, (source, to) in enumerate(zip(sources[0:3], targets[0:3]))]
    zero32 = jnp.zeros((96, 128), BF)
    stack[0:96, 1920:2048] = zero32
    stack[192:288, 0:128] = zero32
    for frame in range(16):
        value = grads[frame * 32 : frame * 32 + 32].astype(F32)
        shifted = [next_column(value).astype(BF), value.astype(BF), previous_column(value).astype(BF)]
        for time_off in range(3):
            to = frame + time_off - 1
            if 0 <= to < 16:
                for col_off in range(3):
                    at = (time_off * 3 + col_off) * 32
                    stack[at : at + 32, to * 128 : to * 128 + 128] = shifted[col_off]
    loads[0].wait()
    loads[1].wait()
    loads += [move(sources[at], targets[at], came, at) for at in (3, 4)]
    grad_mid[0] = jnp.zeros((5, 10, 16, 128), BF)
    grad_mid[17] = jnp.zeros((5, 10, 16, 128), BF)
    for group in range(4):
        product[...] = dot_first(stack[:, group * 512 : group * 512 + 512], bwd_out[...])

        def finish_mid(step, carry):
            frame = group * 4 + step
            added = []
            for pair in range(5):
                chunk = product[pl.ds(step * 128, 128), pair * 128 : pair * 128 + 128]
                slope = slope_out[pl.ds(frame * 128, 128), pair * 128 : pair * 128 + 128]
                value = (chunk * slope.astype(F32)).astype(BF).astype(F32)
                added.append(jnp.sum(value, axis=0, keepdims=True))

                def store(slabs, values):
                    grad_mid[frame + 1, pair, slabs] = values

                put_slabs(store, value)
            lane = lax.broadcasted_iota(jnp.int32, (1, 128), 1)
            own = added[1] + added[2] + added[3]
            own = own + jnp.where(lane >= 64, added[0], 0.0) + jnp.where(lane < 64, added[4], 0.0)
            return carry + own

        if group == 0:
            bias_mid = jnp.zeros((1, 128), F32)
        bias_mid = lax.fori_loop(0, 4, finish_mid, bias_mid)

    loads[2].wait()
    loads += [move(sources[at], targets[at], came, at) for at in (5, 6)]
    result = dot(stack[...], active[...])
    for pair in range(5):
        sum_out[pair] = result[:, pair * 128 : pair * 128 + 128]

    loads[3].wait()
    loads[4].wait()

    def input_side(group, carry):
        rows = []
        for half_of in range(2):
            pieces = []
            for step in range(4):
                for col_off in range(3):
                    pieces.append(two_rows(grad_mid, group * 4 + half_of * 2 + step, 0, 4, col_off))
            rows.append(jnp.concatenate(pieces, axis=1))
        result = dot(jnp.concatenate(rows, axis=0), bwd_mid[...])
        for half_of in range(2):
            for pair in range(4):
                for side in range(2):
                    frame = group * 4 + half_of * 2 + side
                    at = half_of * 512 + pair * 128
                    chunk = result[at : at + 128, side * 128 : side * 128 + 128]
                    slope = slope_in[pl.ds(pl.multiple_of(frame * 128, 128), 128), pair * 128 : pair * 128 + 128]
                    value = (chunk * slope.astype(F32)).astype(BF)
                    at = pl.multiple_of(frame * 512 + pair * 128, 128)
                    grad_in[pl.ds(at, 128), :] = value
                    carry = carry + jnp.sum(value.astype(F32), axis=0, keepdims=True)
        return carry

    bias_in = lax.fori_loop(0, 4, input_side, jnp.zeros((1, 128), F32))

    sum_mid[...] = jnp.zeros_like(sum_mid)
    loads[5].wait()

    def mid_weights(group, carry):
        frames = [group * 4 + step for step in range(4)]
        left = jnp.concatenate([turned[pl.ds(frame, 3)].reshape(384, 512) for frame in frames], axis=1)
        right = []
        for col_off in range(3):
            right.append(jnp.concatenate([two_rows(grad_mid, frame + 1, 0, 4, 2 - col_off) for frame in frames], axis=0))
        sum_mid[...] = sum_mid[...] + dot(left, jnp.concatenate(right, axis=1))
        return carry

    lax.fori_loop(0, 4, mid_weights, 0)

    loads[6].wait()
    patches[0:96, 0:512] = jnp.zeros((96, 512), BF)
    patches[192:288, 7680:8192] = jnp.zeros((96, 512), BF)
    for frame in range(16):
        value = natural[frame].astype(F32)
        shifted = (previous_column(value).astype(BF), natural[frame], next_column(value).astype(BF))
        for col_off in range(3):
            for pair in range(4):
                piece = shifted[col_off][pair * 16 + 16 : pair * 16 + 48]
                for time_off in range(3):
                    to = frame - time_off + 1
                    if 0 <= to < 16:
                        at = (time_off * 3 + col_off) * 32
                        lane = (to * 4 + pair) * 128
                        patches[at : at + 32, lane : lane + 128] = piece
    sum_in[...] = dot(patches[...], grad_in[...])

    tall[...] = jnp.zeros_like(tall)
    for time_off in range(3):
        for row_off in range(3):
            for col_off in range(3):
                tap = (time_off * 3 + row_off) * 3 + col_off
                at, lane = time_off * 128, col_off * 256
                upper = sum_mid[at : at + 64, lane + (2 - row_off) * 64 : lane + (2 - row_off) * 64 + 64]
                lower = sum_mid[at + 64 : at + 128, lane + (3 - row_off) * 64 : lane + (3 - row_off) * 64 + 64]
                tall[tap * 64 : tap * 64 + 64, 0:64] = upper + lower
                at = (time_off * 3 + col_off) * 32 + row_off * 8
                upper = sum_in[at : at + 8, 0:64]
                lower = sum_in[at + 8 : at + 16, 64:128]
                tall[1792 + tap * 8 : 1792 + tap * 8 + 8, 0:64] = upper + lower
    tall[2008:2009, 0:64] = bias_in[:, 0:64] + bias_in[:, 64:128]
    tall[2009:2010, 0:64] = bias_mid[:, 0:64] + bias_mid[:, 64:128]
    for tile in range(16):
        tiles[tile] = jnp.transpose(tall[tile * 128 : tile * 128 + 128])[0:64]
    for row_off in range(3):
        value = None
        for row in range(2, 10):
            lane = (row - 2 + row_off) * 64
            piece = sum_out[lane // 128, pl.ds(row, 18, stride=16), :][:, lane % 128 : lane % 128 + 64]
            value = piece if value is None else value + piece
        for time_off in range(3):
            for col_off in range(3):
                tap = (time_off * 3 + row_off) * 3 + col_off
                for part in range(2):
                    row = (time_off * 3 + col_off) * 2 + part
                    line[part : part + 1, tap * 64 : tap * 64 + 64] = value[row : row + 1]
    for owner in range(8):
        for part in range(2):
            for piece in range(4):
                at = owner * 216 + piece * 54
                row = owner * 8 + part * 4 + piece
                tiles[13, row : row + 1, 64:118] = line[part : part + 1, at : at + 54]
    for quarter in range(4):
        for owner in range(8):
            value = tiles[quarter * 4 : quarter * 4 + 4, owner * 8 : owner * 8 + 8]
            out[quarter * 8 + owner] = value.reshape(32, 128).astype(BF)


def sum_kernel(parts, stats, loss, shard, shared):
    total = parts[0].astype(F32)
    for source in range(1, 32):
        total = total + parts[source].astype(F32)
    divisor = jnp.maximum(stats[1:2, 0:1] * (2.0 * 128 * 128), 1.0)
    total = total / divisor
    shard[...] = total
    lane = lax.broadcasted_iota(jnp.int32, (32, 128), 1)
    shared[...] = jnp.where(lane == 0, jnp.sum(total * total), loss[0:1] + jnp.zeros((32, 128), F32))


def update_kernel(
    own, near, mid, far, messages, stats,
    w_in, w_mid, w_out, w_bias, f_in, f_mid, f_out, f_bias, s_in, s_mid, s_out, s_bias,
    loss_sum, valid_count, grad_norm, mf_in, mf_mid, mf_out, mf_bias, ms_in, ms_mid, ms_out, ms_bias,
    mw_in, mw_mid, mw_out, mw_bias, mc_in, mc_mid, mc_out, mc_bias,
    shards, g_mid, g_in, g_out, g_bias,
):
    f, half, chip, core = place()
    for slot, source in enumerate((own, near, mid, far)):
        shards[jnp.bitwise_xor(f, slot)] = source[...]
    message = jnp.sum(messages[...], axis=0, keepdims=True)
    norm = jnp.sqrt(message[:, 0:1])
    loss_sum[0, 0] = jnp.sum(message[:, 1:2])
    valid_count[0, 0] = jnp.sum(stats[1:2, 0:1]) * (2.0 * 128 * 128)
    grad_norm[0, 0] = jnp.sum(norm)
    factor = jnp.minimum(1.0, CLIP / (norm + 1e-06))

    def tile_of(tile):
        at = (tile % 4) * 8
        return shards[tile // 4, at : at + 8]

    for tile in range(13):
        g_mid[:, tile * 128 : tile * 128 + 128] = tile_of(tile)
    mixed = tile_of(13)
    g_mid[:, 1664:1728] = mixed[:, 0:64]
    for part in range(2):
        for piece in range(4):
            row = part * 4 + piece
            g_out[part : part + 1, piece * 54 : piece * 54 + 54] = mixed[row : row + 1, 64:118]
    g_in[:, 0:128] = tile_of(14)
    mixed = tile_of(15)
    g_in[:, 128:216] = mixed[:, 0:88]
    square = jnp.concatenate([mixed, jnp.zeros((120, 128), F32)], axis=0)
    g_bias[...] = jnp.transpose(square)[88:90, 0:8]
    for grad, weight, one, two, new_one, new_two, new_weight, new_copy in (
        (g_in, w_in, f_in, s_in, mf_in, ms_in, mw_in, mc_in),
        (g_mid, w_mid, f_mid, s_mid, mf_mid, ms_mid, mw_mid, mc_mid),
        (g_out, w_out, f_out, s_out, mf_out, ms_out, mw_out, mc_out),
        (g_bias, w_bias, f_bias, s_bias, mf_bias, ms_bias, mw_bias, mc_bias),
    ):
        results = adamw(weight[...], grad[...] * factor, one[...], two[...])
        for ref, value in zip((new_one, new_two, new_weight, new_copy), results):
            ref[...] = value


VECTOR = pl.BlockSpec(memory_space=pltpu.VMEM)
SCALAR = pl.BlockSpec(memory_space=pltpu.SMEM)
LEFT = pl.BlockSpec(memory_space=pl.ANY)


def shape(*dims, dtype=BF):
    return jax.ShapeDtypeStruct(dims, dtype)


def kernel_call(kernel, name, micros, operands, results, scratch, in_specs=None, out_specs=None):
    return pl.pallas_call(
        kernel,
        name=name,
        out_shape=results,
        in_specs=in_specs or [VECTOR] * len(operands),
        out_specs=out_specs or [VECTOR] * len(results),
        scratch_shapes=scratch,
        cost_estimate=pl.CostEstimate(flops=int(micros * 1e9), bytes_accessed=0, transcendentals=0),
        compiler_params=pltpu.CompilerParams(vmem_limit_bytes=VMEM),
    )(*operands)


def swap(value, axis, bit):
    return lax.ppermute(value, axis, [(i, i ^ bit) for i in range(lax.axis_size(axis))])


def by_rows(
    kspace, line_mask, valid_flags, target, conv_in, conv_mid, conv_out, conv_bias,
    first_in, first_mid, first_out, first_bias, second_in, second_mid, second_out, second_bias,
):
    tables = make_tables()

    mine, theirs, theirs_and_target, mine_target = kernel_call(
        lines_kernel,
        "prepare_lines",
        2,
        [
            valid_flags, kspace.reshape(2, 4, 32, 128), line_mask.reshape(8, 16), target.reshape(2, 4, 32, 128),
            tables["columns"], tables["permute"], conv_mid[0, 0].T, conv_in[0].T, conv_out[0], conv_bias[0],
        ],
        [shape(144, 256), shape(144, 256), shape(208, 256), shape(64, 256)],
        [pltpu.VMEM((2, 80, 256), BF), pltpu.VMEM((2, 64, 256), BF), pltpu.VMEM((16, 8, 128), F32)],
        in_specs=[SCALAR] + [VECTOR] * 9,
    )

    sent = ((mine, 1), (theirs_and_target, 2), (theirs, 3))
    beside, other, far = (swap(value, ("half", "chip"), step) for value, step in sent)

    def two(one, another):
        return jnp.concatenate([one[0:64], another[0:64], one[64:80] + another[64:80]], axis=0)

    half_a, half_b = two(mine, beside), two(other, far)
    near_a, near_b = swap(half_a, "frames", 1), swap(half_b, "frames", 2)
    both_a = jnp.concatenate([half_a, near_a], axis=0)
    both_a, theirs_target = lax.optimization_barrier((both_a, other[144:208]))
    far_a = swap(both_a, "frames", 2)
    far_b = swap(jnp.concatenate([half_b, near_b], axis=0), "frames", 1)

    wanted = []
    for step in range(4):
        at = 16 * step
        image = jnp.concatenate([mine_target[at : at + 16], theirs_target[at : at + 16]], axis=0)
        wanted.append(swap(image, ("chip", "core"), step) if step else image)

    chips = jnp.concatenate([mine[80:144], beside[80:144], other[80:144], far[80:144]], axis=0)
    others = swap(chips, "core", 1)
    scratch = [pltpu.VMEM((16, 64, 128), F32), pltpu.VMEM((2, 1792), F32), pltpu.VMEM((64, 128), F32)]
    fwd_in, fwd_mid, fwd_out, bias = kernel_call(
        forward_weight_kernel,
        "lay_out_forward_weights",
        4,
        [chips, others, tables["pick_out"]],
        [shape(1152, 768), shape(3072, 256), shape(640, 256), shape(8, 768, dtype=F32)],
        scratch,
    )
    far_a, far_b, bias = lax.optimization_barrier((far_a, far_b, bias))
    gathered = [half_a, half_b, near_a, near_b, far_a, far_b]
    gathered += [swap(piece, "core", 1) for piece in gathered]
    kept = [(16, 128, 128), (18, 128, 512), (2048, 640), (2048, 512), (2048, 640)]
    moved = [(128, 256), (1152, 768), (3072, 256)]
    branch, stats, lines, natural, turned, active, slope_in, slope_out = kernel_call(
        forward_kernel,
        "features_and_branch",
        27,
        [*gathered, tables["feature"], fwd_in, fwd_mid, fwd_out, bias],
        [shape(256, 128), shape(8, 256, dtype=F32), shape(256, 128)] + [shape(*dims) for dims in kept],
        [pltpu.VMEM(dims, BF) for dims in moved]
        + [pltpu.SemaphoreType.DMA((3,))]
        + [
            pltpu.VMEM((20, 128, 256), BF),
            pltpu.VMEM((4, 8, 128), F32),
            pltpu.VMEM((24, 128), F32),
            pltpu.VMEM((18, 10, 16, 128), BF),
            pltpu.VMEM((18, 6, 10, 16, 128), BF),
            pltpu.VMEM((512, 768), F32),
            pltpu.VMEM((1280, 256), F32),
            pltpu.VMEM((18, 144, 128), F32),
        ]
        + [pltpu.VMEM(dims, BF) for dims in kept]
        + [pltpu.SemaphoreType.DMA((5,))],
        in_specs=[VECTOR] * 12 + [LEFT] * 3 + [VECTOR] * 2,
        out_specs=[VECTOR] * 3 + [LEFT] * 5,
    )
    branch, chips, others = lax.optimization_barrier((branch, chips, others))
    bwd_mid, bwd_out = kernel_call(
        backward_weight_kernel,
        "lay_out_backward_weights",
        3,
        [chips, others, tables["pick_back"]],
        [shape(3072, 256), shape(288, 640)],
        scratch,
    )
    lines, bwd_out = lax.optimization_barrier((lines, bwd_out))
    by_frame = lax.all_to_all(branch.reshape(16, 16, 128), ("frames", "chip", "core"), 0, 0, tiled=True)
    grads, loss = kernel_call(
        consistency_kernel,
        "data_consistency",
        2.5,
        [
            by_frame.reshape(256, 128), lines, stats, *wanted,
            tables["to_lines"], tables["to_rows"], tables["lines_again"], tables["spread"],
        ],
        [shape(512, 128), shape(8, 128, dtype=F32)],
        [pltpu.VMEM((256, 128), BF)],
    )
    by_block = lax.all_to_all(grads.reshape(16, 32, 128), ("frames", "chip", "core"), 0, 0, tiled=True)
    moved = [(288, 640), (2048, 640), (2048, 640), (3072, 256), (2048, 512), (18, 128, 512), (16, 128, 128)]
    (parts,) = kernel_call(
        backward_kernel,
        "weight_gradients",
        27,
        [by_block.reshape(512, 128), bwd_out, slope_out, active, bwd_mid, slope_in, turned, natural],
        [shape(32, 32, 128)],
        [pltpu.VMEM(dims, BF) for dims in moved]
        + [pltpu.SemaphoreType.DMA((7,))]
        + [
            pltpu.VMEM((288, 2048), BF),
            pltpu.VMEM((512, 640), F32),
            pltpu.VMEM((18, 5, 10, 16, 128), BF),
            pltpu.VMEM((8192, 128), BF),
            pltpu.VMEM((384, 768), F32),
            pltpu.VMEM((5, 288, 128), F32),
            pltpu.VMEM((288, 128), F32),
            pltpu.VMEM((288, 8192), BF),
            pltpu.VMEM((2048, 128), F32),
            pltpu.VMEM((16, 64, 128), F32),
            pltpu.VMEM((2, 1792), F32),
        ],
        in_specs=[VECTOR] + [LEFT] * 7,
    )
    parts = lax.all_to_all(parts, ("frames", "half", "chip", "core"), 0, 0, tiled=True)
    shard, messages = kernel_call(
        sum_kernel,
        "sum_gradients",
        2,
        [parts, stats, loss],
        [shape(32, 128, dtype=F32), shape(32, 128, dtype=F32)],
        [],
    )
    shards = [shard] + [swap(shard, "frames", step) for step in (1, 2, 3)]
    messages = lax.all_to_all(messages, ("frames", "half", "chip", "core"), 0, 0, tiled=True)
    groups = (
        (conv_in, conv_mid, conv_out, conv_bias),
        (first_in, first_mid, first_out, first_bias),
        (second_in, second_mid, second_out, second_bias),
    )
    state = []
    for of_in, of_mid, of_out, of_bias in groups:
        state += [of_in[0].T, of_mid[0, 0].T, of_out[0], of_bias[0]]
    shapes = [(8, 216), (8, 1728), (2, 216), (2, 8)]
    results = kernel_call(
        update_kernel,
        "adamw",
        2,
        [*shards, messages, stats, *state],
        [shape(1, 1, dtype=F32)] * 3
        + [shape(*dims, dtype=F32) for dims in shapes * 3]
        + [shape(*dims, dtype=BF) for dims in shapes],
        [pltpu.VMEM((4, 32, 128), F32)] + [pltpu.VMEM(shapes[at], F32) for at in (1, 0, 2, 3)],
        out_specs=[SCALAR] * 3 + [VECTOR] * 16,
    )
    outputs = [result[0, 0] for result in results[0:3]]
    for at in range(3, 19, 4):
        of_in, of_mid, of_out, of_bias = results[at : at + 4]
        outputs += [of_in.T[None], of_mid.T[None, None], of_out[None], of_bias[None]]
    return tuple(outputs)


def specs_for(rows):
    lines = P(None, "frames", rows)
    images = P(None, "frames", rows, None, None)
    weights = [P(None, None, rows), P(None, None, None, rows), P(None, None, rows), P(None, None, rows)]
    in_specs = (images, lines, P(None, "frames"), images, *(weights * 3))
    out_specs = (P(), P(), P(), *(weights * 4))
    return in_specs, out_specs


def solution(mesh):
    frames, rows = (mesh.shape[axis] for axis in ("frames", "rows"))
    if (frames, rows) != (4, 8):
        in_specs, out_specs = specs_for("rows")
        return jax.shard_map(local, mesh=mesh, in_specs=in_specs, out_specs=out_specs, check_vma=False)
    chips = Mesh(mesh.devices.reshape(frames, 2, rows // 4, 2), ("frames", "half", "chip", "core"))
    in_specs, out_specs = specs_for(("half", "chip", "core"))
    return jax.shard_map(by_rows, mesh=chips, in_specs=in_specs, out_specs=out_specs, check_vma=False)
```

```python
import jax
import jax.numpy as jnp
import ml_dtypes
import numpy as np
from jax import lax
from jax.experimental import pallas as pl
from jax.experimental.pallas import tpu as pltpu
from jax.sharding import Mesh
from jax.sharding import PartitionSpec as P

NX = 128
CAS = 1
MIDS = 1
STEP = 10


CLIP = 0.05
RATE = 0.03
BETA_ONE = 0.9
BETA_TWO = 0.999
EPSILON = 1e-08
DECAY = 0.01
HIGHEST = lax.Precision.HIGHEST


def with_halo(shard, sides, width):
    for axis, dim in sides:
        size, length = (lax.axis_size(axis), shard.shape[dim])
        up = [(i, (i + 1) % size) for i in range(size - 1)]
        down = [(j, i) for i, j in up]
        last = lax.slice_in_dim(shard, length - width, length, axis=dim)
        first = lax.slice_in_dim(shard, 0, width, axis=dim)
        before = lax.ppermute(last, axis, up)
        after = lax.ppermute(first, axis, down)
        shard = jnp.concatenate([before, shard, after], axis=dim)
    return shard


def from_behind(block, axis, distance):
    devices = range(lax.axis_size(axis))
    route = [(i - distance, i) for i in devices if i - distance in devices]
    return lax.ppermute(block, axis, route)


def dft_blocks(length, sign):
    counter = jnp.arange(length, dtype=jnp.int32)
    turns = counter[:, None] * counter[None, :] % length
    angle = turns.astype(jnp.float32) * (2.0 * jnp.pi / length)
    norm_factor = 1.0 / jnp.sqrt(jnp.float32(length))
    cosine = jnp.cos(angle) * norm_factor
    sine = sign * jnp.sin(angle) * norm_factor
    return jnp.stack([jnp.stack([cosine, -sine]), jnp.stack([sine, cosine])])


def transform(image, sign):
    rows_here = image.shape[1]
    rows_all = rows_here * lax.axis_size("rows")
    first_row = lax.axis_index("rows") * rows_here
    across = jnp.einsum(
        "byix,oikx->byok", image, dft_blocks(image.shape[3], sign), precision=HIGHEST
    )
    table = dft_blocks(rows_all, sign)
    window = lax.dynamic_slice(
        table, (0, 0, 0, first_row), (2, 2, lax.axis_size("rows") * rows_here, rows_here)
    )
    return lax.psum_scatter(
        jnp.einsum("byix,oiky->kbox", across, window, precision=HIGHEST),
        "rows",
        scatter_dimension=0,
        tiled=True,
    ).transpose(1, 0, 2, 3)


def taps(widened, offset, frames, rows_here, columns):
    time_off = offset // 3
    row_off = offset % 3
    return jnp.concatenate(
        [
            widened[
                time_off : time_off + frames,
                row_off : row_off + rows_here,
                :,
                col_off : col_off + columns,
            ]
            for col_off in range(3)
        ],
        axis=2,
    )


def convolve(padded, kernel):
    frames = padded.shape[0] - 2
    rows_here = padded.shape[1] - 2
    width_in = padded.shape[2]
    columns = padded.shape[3]
    widened = jnp.pad(padded, ((0, 0), (0, 0), (0, 0), (1, 1)))
    blocks = kernel.reshape(9, 3 * width_in, kernel.shape[1])
    summed = jnp.zeros((frames, rows_here, kernel.shape[1], columns), jnp.float32)
    for offset in range(9):
        gathered = taps(widened, offset, frames, rows_here, columns)
        summed = summed + jnp.einsum(
            "tykx,kj->tyjx", gathered, blocks[offset], preferred_element_type=jnp.float32
        )
    return summed


def kernel_grad(padded, grad_out):
    frames, rows_here, columns = (grad_out.shape[0], grad_out.shape[1], grad_out.shape[3])
    widened = jnp.pad(padded, ((0, 0), (0, 0), (0, 0), (1, 1)))
    pieces = [
        jnp.einsum(
            "tykx,tyjx->kj",
            taps(widened, offset, frames, rows_here, columns),
            grad_out,
            preferred_element_type=jnp.float32,
        )
        for offset in range(9)
    ]
    return jnp.concatenate(pieces, axis=0)


def flipped(kernel):
    width_in = kernel.shape[0] // 27
    shaped = kernel.reshape(3, 3, 3, width_in, kernel.shape[1])[::-1, ::-1, ::-1]
    return shaped.transpose(0, 1, 2, 4, 3).reshape(27 * kernel.shape[1], width_in)


def activation_rim(values):
    return with_halo(values, (("frames", 0), ("rows", 1)), 1)


def gradient_rim(values):
    return with_halo(values, (("frames", 0), ("rows", 1)), 1)


def layer_forward(inputs, kernel, bias_row):
    padded = activation_rim(inputs)
    return (padded, convolve(padded, kernel) + bias_row.astype(jnp.float32)[None, None, :, None])


def layer_backward(padded, kernel, grad_hidden, needs_input):
    kernel_delta = kernel_grad(padded, grad_hidden)
    bias_delta = jnp.sum(grad_hidden, axis=(0, 1, 3), dtype=jnp.float32)
    input_delta = None
    if needs_input:
        input_delta = convolve(gradient_rim(grad_hidden), flipped(kernel))
    return (kernel_delta, bias_delta, input_delta)


def share(measured, sampled):
    frames = measured.shape[0]
    reach = (frames + 1) // frames
    before = []
    after = []
    for distance in range(1, reach + 1):
        for direction in (1, -1):
            moved = from_behind((measured, sampled), "frames", direction * distance)
            if direction == 1:
                before.insert(0, moved)
            else:
                after.append(moved)
    data_line = jnp.concatenate(
        [moved_pair[0] for moved_pair in before]
        + [measured]
        + [moved_pair[0] for moved_pair in after],
        axis=0,
    )
    mask_line = jnp.concatenate(
        [moved_pair[1] for moved_pair in before]
        + [sampled]
        + [moved_pair[1] for moved_pair in after],
        axis=0,
    )
    centre = reach * frames
    windows = []
    for radius in range(3):
        data_sum = data_line[centre - radius : centre - radius + frames]
        mask_sum = mask_line[centre - radius : centre - radius + frames]
        for offset in range(1 - radius, radius + 1):
            data_sum = data_sum + data_line[centre + offset : centre + offset + frames]
            mask_sum = mask_sum + mask_line[centre + offset : centre + offset + frames]
        windows.append(data_sum / jnp.maximum(mask_sum, 1.0)[:, :, None, None])
    return jnp.stack(windows, 1)


def adamw(weight, grad_piece, moment_one, moment_two):
    first_new = BETA_ONE * moment_one + (1.0 - BETA_ONE) * grad_piece
    second_new = BETA_TWO * moment_two + (1.0 - BETA_TWO) * grad_piece * grad_piece
    ascent = (
        first_new
        / (1.0 - BETA_ONE**STEP)
        / (jnp.sqrt(second_new / (1.0 - BETA_TWO**STEP)) + EPSILON)
    )
    weight_new = weight - RATE * (ascent + DECAY * weight)
    return (first_new, second_new, weight_new, weight_new.astype(jnp.bfloat16))


def local(
    kspace,
    line_mask,
    valid_flags,
    target,
    conv_in,
    conv_mid,
    conv_out,
    conv_bias,
    first_in,
    first_mid,
    first_out,
    first_bias,
    second_in,
    second_mid,
    second_out,
    second_bias,
):
    masters = (conv_in, conv_mid, conv_out, conv_bias)

    def reduce_grads(grads):
        shards = (
            lax.psum_scatter(
                grads[0].astype(jnp.bfloat16), "rows", scatter_dimension=2, tiled=True
            ).astype(jnp.float32),
            lax.psum_scatter(
                grads[1].astype(jnp.bfloat16), "rows", scatter_dimension=3, tiled=True
            ).astype(jnp.float32),
            lax.psum_scatter(
                grads[2].astype(jnp.bfloat16), "rows", scatter_dimension=2, tiled=True
            ).astype(jnp.float32),
            lax.psum_scatter(
                grads[3].astype(jnp.bfloat16), "rows", scatter_dimension=2, tiled=True
            ).astype(jnp.float32),
        )
        return lax.psum((shards[0], shards[1], shards[2], shards[3]), "frames")

    def micro_batch(carry, batch_data):
        grad_carry, loss_carry, count_carry = carry
        measured_full, mask_rows, frame_flags, wanted = batch_data
        full_in, full_mid, full_out, full_bias = (
            lax.all_gather(conv_in.astype(jnp.bfloat16), "rows", axis=2, tiled=True),
            lax.all_gather(conv_mid.astype(jnp.bfloat16), "rows", axis=3, tiled=True),
            lax.all_gather(conv_out.astype(jnp.bfloat16), "rows", axis=2, tiled=True),
            lax.all_gather(conv_bias.astype(jnp.bfloat16), "rows", axis=2, tiled=True),
        )
        sampled = mask_rows.astype(jnp.float32)
        measured = measured_full * sampled[:, :, None, None]
        shared = share(measured, sampled)
        frames, rows_here = (measured.shape[0], measured.shape[1])
        images = transform(shared.reshape(frames * 3, rows_here, 2, NX), 1.0).reshape(
            frames, 3, rows_here, 2, NX
        )
        shared_images = images.transpose(0, 2, 1, 3, 4).reshape(frames, rows_here, 6, NX)
        current = images[:, 0]
        unsampled = (1.0 - sampled)[:, :, None, None]
        no_bias = jnp.zeros((2,), jnp.bfloat16)

        def kernels_of(cascade):
            return [full_in[cascade]] + [full_mid[cascade, 0]] + [full_out[cascade].T]

        cascade = 0
        kernels = kernels_of(cascade)
        biases = [full_bias[cascade, layer_at] for layer_at in range(MIDS + 1)] + [no_bias]
        inputs = jnp.concatenate([current, shared_images], axis=2).astype(jnp.bfloat16)
        saved = []
        for layer_at in range(MIDS + 2):
            padded, hidden = layer_forward(inputs, kernels[layer_at], biases[layer_at])
            saved.append((padded, hidden))
            if layer_at < MIDS + 1:
                inputs = jax.nn.gelu(hidden).astype(jnp.bfloat16)
        current = transform(unsampled * transform(current + hidden, -1.0) + measured, 1.0)
        kept = [saved]
        frame_weight = frame_flags.astype(jnp.float32)[:, None, None, None]
        residual_error = current - wanted
        loss_part = jnp.sum(frame_weight * residual_error * residual_error)
        count_part = 2.0 * rows_here * NX * jnp.sum(frame_flags.astype(jnp.float32))
        grad_current = 2.0 * frame_weight * residual_error
        delta_in = [None] * CAS
        delta_mid = [None] * CAS
        delta_out = [None] * CAS
        delta_bias = [None] * CAS
        for cascade in reversed(range(CAS)):
            kernels = kernels_of(cascade)
            grad_sum = transform(unsampled * transform(grad_current, -1.0), 1.0)
            grad_hidden = grad_sum.astype(jnp.bfloat16)
            kernel_deltas = [None] * (MIDS + 2)
            bias_deltas = [None] * (MIDS + 2)
            grad_input = None
            for layer_at in reversed(range(MIDS + 2)):
                padded, hidden = kept[cascade][layer_at]
                if layer_at < MIDS + 1:
                    pullback = jax.vjp(jax.nn.gelu, hidden)[1]
                    grad_hidden = pullback(grad_input)[0].astype(jnp.bfloat16)
                needs_input = cascade > 0 or layer_at > 0
                kernel_deltas[layer_at], bias_deltas[layer_at], grad_input = layer_backward(
                    padded, kernels[layer_at], grad_hidden, needs_input
                )
            delta_in[cascade] = kernel_deltas[0]
            delta_mid[cascade] = jnp.stack(kernel_deltas[1 : MIDS + 1])
            delta_out[cascade] = kernel_deltas[MIDS + 1].T
            delta_bias[cascade] = jnp.stack(bias_deltas[0 : MIDS + 1])
        grads = (
            jnp.stack(delta_in),
            jnp.stack(delta_mid),
            jnp.stack(delta_out),
            jnp.stack(delta_bias),
        )
        grads = reduce_grads(grads)
        grad_carry = jax.tree.map(jnp.add, grad_carry, grads)
        return ((grad_carry, loss_carry + loss_part, count_carry + count_part), None)

    start_grads = jax.tree.map(jnp.zeros_like, masters)
    start = (start_grads, jnp.zeros((), jnp.float32), jnp.zeros((), jnp.float32))
    (summed, loss_local, count_local), unused = lax.scan(
        micro_batch, start, (kspace, line_mask, valid_flags, target)
    )
    summed = tuple(summed)
    loss_sum, valid_count = lax.psum((loss_local, count_local), ("frames", "rows"))
    divisor = jnp.maximum(valid_count, 1.0)
    grads = [grad_piece / divisor for grad_piece in summed]
    squares = sum((jnp.sum(grad_piece * grad_piece) for grad_piece in grads))
    grad_norm = jnp.sqrt(lax.psum(squares, "rows"))
    factor = jnp.minimum(1.0, CLIP / (grad_norm + 1e-06))
    firsts = (first_in, first_mid, first_out, first_bias)
    seconds = (second_in, second_mid, second_out, second_bias)
    results = [
        adamw(masters[which], grads[which] * factor, firsts[which], seconds[which])
        for which in range(4)
    ]
    return (
        loss_sum,
        valid_count,
        grad_norm,
        results[0][0],
        results[1][0],
        results[2][0],
        results[3][0],
        results[0][1],
        results[1][1],
        results[2][1],
        results[3][1],
        results[0][2],
        results[1][2],
        results[2][2],
        results[3][2],
        results[0][3],
        results[1][3],
        results[2][3],
        results[3][3],
    )


BF = jnp.bfloat16
F32 = jnp.float32
SQRT_TWO_OVER_PI = 0.7978845608028654
CUBIC = 0.044715 * SQRT_TWO_OVER_PI
UNITS = 16
VMEM = 56 * 2**20


def column_order():
    lanes = np.arange(128)
    return (lanes % 16) * 8 + lanes // 16


def dft_tables(sign):
    counter = np.arange(128)
    angle = (counter[:, None] * counter[None, :] % 128) * (2.0 * np.pi / 128)
    cosine, sine = np.cos(angle) / np.sqrt(128.0), sign * np.sin(angle) / np.sqrt(128.0)
    return np.stack([np.stack([cosine, -sine]), np.stack([sine, cosine])])


def make_tables():
    inverse, forward = dft_tables(1.0), dft_tables(-1.0)
    order = column_order()
    columns = inverse[:, :, :, order].transpose(1, 2, 0, 3).reshape(256, 256)
    blocks = np.arange(UNITS)[:, None] * 8

    def rows_of(first, kept):
        rows = blocks + first + np.arange(16)[None, :]
        inside = (rows >= 0) & (rows < 128) & (np.arange(16)[None, :] < kept)
        return np.clip(rows, 0, 127), inside

    rows, inside = rows_of(-3, 14)
    feature = inverse[:, :, rows, :] * inside[None, None, :, :, None]
    feature = feature.transpose(2, 3, 0, 1, 4).reshape(UNITS, 16, 2, 256)
    feature = np.tile(feature, (1, 1, 4, 1)).reshape(UNITS, 128, 256)
    to_lines = forward.reshape(2, 2, 128, UNITS, 8).transpose(0, 2, 3, 1, 4).reshape(256, 256)
    to_rows = inverse.transpose(0, 2, 1, 3).reshape(256, 256)
    lines_again = forward.transpose(0, 2, 1, 3).reshape(256, 256)
    rows, inside = rows_of(-2, 12)
    spread = inverse[:, :, rows, :] * inside[None, None, :, :, None]
    spread = spread.transpose(2, 0, 3, 1, 4).reshape(UNITS * 32, 256)
    permute = np.zeros((128, 128))
    permute[order, np.arange(128)] = 1.0
    pick_out = np.zeros((64, 10, 256))
    pick_back = np.zeros((10, 288, 64))
    for time_off in range(3):
        for row_off in range(3):
            for col_off in range(3):
                tap = (time_off * 3 + row_off) * 3 + col_off
                for part in range(2):
                    for row in range(8):
                        lane = (time_off * 3 + col_off) * 16 + part * 8 + row
                        pick_out[tap * 2 + part, row + row_off, lane] = 1.0
                    for row in range(12):
                        into = row + row_off - 2
                        if 0 <= into < 10:
                            at = (time_off * 3 + col_off) * 32 + part * 16 + row
                            pick_back[into, at, tap * 2 + part] = 1.0
    made = dict(
        columns=columns,
        feature=feature,
        to_lines=to_lines,
        lines_again=lines_again,
        to_rows=to_rows,
        spread=spread,
        permute=permute,
        pick_out=pick_out.reshape(64, 2560),
        pick_back=pick_back.reshape(2880, 64),
    )
    return {name: jnp.asarray(table.astype(ml_dtypes.bfloat16)) for name, table in made.items()}


def dot(left, right):
    return jnp.dot(left, right, preferred_element_type=F32)


def dot_first(left, right):
    return lax.dot_general(left, right, (((0,), (0,)), ((), ())), preferred_element_type=F32)


def next_column(values):
    lane = lax.broadcasted_iota(jnp.int32, values.shape, 1)
    inner = pltpu.roll(values, 112, 1)
    wrapped = jnp.where(lane == 127, 0.0, pltpu.roll(values, 111, 1))
    return jnp.where(lane < 112, inner, wrapped)


def previous_column(values):
    lane = lax.broadcasted_iota(jnp.int32, values.shape, 1)
    inner = pltpu.roll(values, 16, 1)
    wrapped = jnp.where(lane == 0, 0.0, pltpu.roll(values, 17, 1))
    return jnp.where(lane >= 16, inner, wrapped)


def put_slabs(store, values):
    store(slice(1, 9), values.astype(BF).reshape(8, 16, 128))
    first, last = values[0:16], values[112:128]
    at = lax.broadcasted_iota(jnp.int32, (16, 128), 0)
    before = jnp.where(at == 0, 0.0, pltpu.roll(last, 1, 0))
    after = jnp.where(at == 15, 0.0, pltpu.roll(first, 15, 0))
    store(slice(0, 1), before.astype(BF).reshape(1, 16, 128))
    store(slice(9, 10), after.astype(BF).reshape(1, 16, 128))


def two_rows(ref, frame, pair, count, first_slab):
    upper = ref[frame, pair : pair + count, first_slab : first_slab + 8]
    lower = ref[frame, pair + 1 : pair + 1 + count, first_slab : first_slab + 8]
    rows = count * 128
    return jnp.concatenate([upper.reshape(rows, 128), lower.reshape(rows, 128)], axis=1)


def gelu_and_slope(hidden):
    square = hidden * hidden
    half = 0.5 * jnp.tanh(hidden * (CUBIC * square + SQRT_TWO_OVER_PI)) + 0.5
    active = hidden * half
    slope = half + active * (1.0 - half) * (6.0 * CUBIC * square + 2.0 * SQRT_TWO_OVER_PI)
    return active, slope


def place():
    return tuple(lax.axis_index(name) for name in ("frames", "half", "chip", "core"))


def lines_kernel(
    valid, kspace, line_mask, target, columns_table, permute, conv_mid, conv_in, conv_out, conv_bias,
    beside, other, far, mine_target, both, images, tiles,
):
    f, half, chip, core = place()
    quarter = chip * 2 + core
    sampled = line_mask[...].astype(F32)
    wide = jnp.concatenate([sampled, jnp.zeros((8, 112), F32)], axis=1)
    column = jnp.transpose(jnp.concatenate([wide, jnp.zeros((120, 128), F32)], axis=0))
    placed = pltpu.roll(wide, (half * 4 + quarter) * 16, 1)
    total = jnp.zeros((1, 128), F32)
    flags = []
    for batch in range(2):
        for frame in range(4):
            flag = jnp.zeros((1, 128), F32) + valid[batch, frame].astype(F32)
            flags.append(flag)
            total = total + flag
    for batch in range(2):
        shown = [[], []]
        sampled_lines = []
        for frame in range(4):
            at = batch * 4 + frame
            own = column[0:16, at : at + 1]
            lines = [kspace[batch, frame, pl.ds(part, 16, stride=2), :] * own for part in range(2)]
            sampled_lines.append(jnp.concatenate(lines, axis=1).astype(BF))
            for part in range(2):
                shown[part].append(target[batch, frame, pl.ds(part, 16, stride=2), :])
        both[batch, 0:64] = dot(jnp.concatenate(sampled_lines, axis=0), columns_table[...]).astype(BF)
        rows = [placed[batch * 4 : batch * 4 + 4]] + flags[batch * 4 : batch * 4 + 4] + [total, jnp.zeros((7, 128), F32)]
        both[batch, 64:80, 0:128] = jnp.concatenate(rows, axis=0).astype(BF)
        both[batch, 64:80, 128:256] = jnp.zeros((16, 128), BF)
        for part in range(2):
            image = jnp.concatenate(shown[part], axis=0).astype(BF)
            image = dot(image, permute[...]).astype(BF)
            for frame in range(4):
                images[batch, frame, :, part * 128 : part * 128 + 128] = image[frame * 16 : frame * 16 + 16]
    for step, to in ((1, beside), (2, other), (3, far)):
        batch = half if step == 1 else 1 - half
        to[0:80] = both[batch]
        for sibling in range(2):
            frame = jnp.bitwise_xor(quarter, (step % 2) * 2 + sibling)
            to[144 + sibling * 16 : 160 + sibling * 16] = images[batch, frame]
    for sibling in range(2):
        mine_target[sibling * 16 : sibling * 16 + 16] = images[half, jnp.bitwise_xor(quarter, sibling)]
    tiles[...] = jnp.zeros_like(tiles)
    for tile in range(13):
        tiles[tile] = conv_mid[:, tile * 128 : tile * 128 + 128]
    tiles[13, :, 0:64] = conv_mid[:, 1664:1728]
    for part in range(2):
        for piece in range(4):
            row = part * 4 + piece
            tiles[13, row : row + 1, 64:118] = conv_out[part : part + 1, piece * 54 : piece * 54 + 54]
    tiles[14] = conv_in[:, 0:128]
    tiles[15, :, 0:88] = conv_in[:, 128:216]
    wide = jnp.concatenate([conv_bias[...], jnp.zeros((2, 120), F32)], axis=1)
    wide = jnp.transpose(jnp.concatenate([wide, jnp.zeros((126, 128), F32)], axis=0))
    tiles[15, :, 88:90] = wide[0:8, 0:2]
    packed = tiles[...].reshape(128, 128).astype(BF)
    packed = jnp.concatenate([packed[0:64], packed[64:128]], axis=1)
    for to in (beside, other, far):
        to[80:144] = packed


def unpack_weights(own, other, whole):
    f, half, chip, core = place()
    for side, source in enumerate((own, other)):
        for slot in range(4):
            row = jnp.bitwise_xor(half * 4 + chip * 2 + core, slot * 2 + side)
            row = pl.multiple_of(row * 8, 8)
            values = source[slot * 64 : slot * 64 + 64].astype(F32)
            for part in range(2):
                half_of = values[:, part * 128 : part * 128 + 128].reshape(8, 8, 128)
                whole[part * 8 : part * 8 + 8, pl.ds(row, 8), :] = half_of


def unpack_last(whole, line, taps):
    for owner in range(8):
        for part in range(2):
            for piece in range(4):
                at = owner * 216 + piece * 54
                row = owner * 8 + part * 4 + piece
                line[part : part + 1, at : at + 54] = whole[13, row : row + 1, 64:118]
    taps[...] = jnp.zeros_like(taps)
    for tap in range(27):
        for part in range(2):
            row = tap * 2 + part
            taps[row : row + 1, 0:64] = line[part : part + 1, tap * 64 : tap * 64 + 64]
    return taps[...].astype(BF)[:, 0:64]


def forward_weight_kernel(own, other, pick_out, fwd_in, fwd_mid, fwd_out, bias, whole, line, taps):
    unpack_weights(own, other, whole)
    zero = jnp.zeros((64, 64), F32)
    turned = [jnp.transpose(whole[tile]) for tile in range(16)]

    def of_tap(time_off, row_off, col_off):
        tap = (time_off * 3 + row_off) * 3 + col_off
        return turned[tap // 2][(tap % 2) * 64 : (tap % 2) * 64 + 64]

    for time_off in range(4):
        for col_off in range(3):
            at = (time_off * 3 + col_off) * 256
            if time_off == 0:
                fwd_mid[at : at + 256, 128:256] = jnp.zeros((256, 128), BF)
            if time_off == 3:
                fwd_mid[at : at + 256, 0:128] = jnp.zeros((256, 128), BF)
    for time_off in range(3):
        for col_off in range(3):
            for level in range(4):
                left = of_tap(time_off, level, col_off) if level < 3 else zero
                right = of_tap(time_off, level - 1, col_off) if level > 0 else zero
                strip = jnp.concatenate([left, right], axis=1).astype(BF)
                for pair in range(2):
                    at = ((time_off + pair) * 3 + col_off) * 256 + level * 64
                    fwd_mid[at : at + 64, pair * 128 : pair * 128 + 128] = strip
    first = jnp.concatenate([turned[14], turned[15]], axis=0)
    fwd_in[...] = jnp.zeros_like(fwd_in)
    pad = jnp.zeros((8, 64), F32)
    for time_off in range(3):
        for col_off in range(3):
            three = []
            for row_off in range(3):
                tap = (time_off * 3 + row_off) * 3 + col_off
                three.append(first[tap * 8 : tap * 8 + 8, 0:64])
            left = jnp.concatenate(three + [pad], axis=0)
            right = jnp.concatenate([pad] + three, axis=0)
            strip = jnp.concatenate([left, right], axis=1).astype(BF)
            at = (time_off * 3 + col_off) * 128
            for pair in range(6):
                fwd_in[at + pair * 16 : at + pair * 16 + 32, pair * 128 : pair * 128 + 128] = strip
    bias[...] = jnp.zeros_like(bias)
    for layer in range(2):
        row = turned[15][88 + layer : 89 + layer, 0:64]
        row = jnp.concatenate([row, row], axis=1)
        for pair in range(6):
            bias[layer : layer + 1, pair * 128 : pair * 128 + 128] = row
    spread = dot_first(unpack_last(whole, line, taps), pick_out[...]).astype(BF)
    for row in range(10):
        fwd_out[row * 64 : row * 64 + 64, :] = spread[:, row * 256 : row * 256 + 256]


def backward_weight_kernel(own, other, pick_back, bwd_mid, bwd_out, whole, line, taps):
    unpack_weights(own, other, whole)
    zero = jnp.zeros((64, 64), F32)
    plain = [whole[tile] for tile in range(14)]

    def of_tap(time_off, row_off, col_off):
        tap = (time_off * 3 + row_off) * 3 + col_off
        return plain[tap // 2][:, (tap % 2) * 64 : (tap % 2) * 64 + 64]

    for time_off in range(4):
        for col_off in range(3):
            at = (time_off * 3 + col_off) * 256
            if time_off == 0:
                bwd_mid[at : at + 256, 128:256] = jnp.zeros((256, 128), BF)
            if time_off == 3:
                bwd_mid[at : at + 256, 0:128] = jnp.zeros((256, 128), BF)
    for time_off in range(3):
        for col_off in range(3):
            for level in range(4):
                left = of_tap(time_off, 2 - level, col_off) if level < 3 else zero
                right = of_tap(time_off, 3 - level, col_off) if level > 0 else zero
                strip = jnp.concatenate([left, right], axis=1).astype(BF)
                for pair in range(2):
                    at = ((2 + pair - time_off) * 3 + 2 - col_off) * 256 + level * 64
                    bwd_mid[at : at + 64, pair * 128 : pair * 128 + 128] = strip
    back = dot(pick_back[...], unpack_last(whole, line, taps)).astype(BF)
    for pair in range(5):
        at = pair * 2 * 288
        bwd_out[:, pair * 128 : pair * 128 + 128] = jnp.concatenate(
            [back[at : at + 288], back[at + 288 : at + 576]], axis=1
        )


def move(source, target, semaphores, at):
    copy = pltpu.make_async_copy(source, target, semaphores.at[at])
    copy.start()
    return copy


def forward_kernel(*refs):
    gathered, refs = refs[0:8], refs[8:]
    row_tables, fwd_in_hbm, fwd_mid_hbm, fwd_out, bias = refs[0:5]
    branch, stats, lines, natural_hbm, turned_hbm, active_hbm, slope_in_hbm, slope_out_hbm = refs[5:13]
    rows_table, fwd_in, fwd_mid, came = refs[13:17]
    spectrum, masks, seen, feature, active, hidden, hidden_other, second, second_other, taps, natural, turned, active_out, slope_in, slope_out, done = refs[17:]
    f, half, chip, core = place()
    quarter = chip * 2 + core
    block = f * 4 + quarter
    loads = [move(row_tables.at[block], rows_table, came, 0), move(fwd_in_hbm, fwd_in, came, 1)]
    spectrum[0:2] = jnp.zeros((2, 128, 256), BF)
    spectrum[18:20] = jnp.zeros((2, 128, 256), BF)
    feature[0] = jnp.zeros((10, 16, 128), BF)
    feature[17] = jnp.zeros((10, 16, 128), BF)
    active[0] = jnp.zeros((6, 10, 16, 128), BF)
    active[17] = jnp.zeros((6, 10, 16, 128), BF)
    turned[0] = jnp.zeros((128, 512), BF)
    turned[17] = jnp.zeros((128, 512), BF)
    taps[0] = jnp.zeros((144, 128), F32)
    taps[17] = jnp.zeros((144, 128), F32)
    total = jnp.zeros((1, 128), F32)
    masks[...] = jnp.zeros_like(masks)
    for at in range(8):
        side, which = at // 4, at % 4
        for piece in range(2):
            turn = which
            group = jnp.bitwise_xor(f, turn)
            rows = gathered[at][piece * 144 : piece * 144 + 144]
            for other in range(2):
                chips_away = piece * 2 + other
                row = jnp.bitwise_xor(half * 4 + quarter, chips_away * 2 + side) * 16
                row = pl.multiple_of(row, 16)
                for frame in range(4):
                    line = rows[other * 64 + frame * 16 : other * 64 + frame * 16 + 16]
                    spectrum[2 + group * 4 + frame, pl.ds(row, 16), :] = line
            flags = rows[128:144, 0:128].astype(F32)
            if side == 0 and piece == 0:
                total = total + 0.5 * flags[8:9]
                masks[group] = masks[group] + flags[0:8]
            else:
                masks[group, 0:4] = masks[group, 0:4] + flags[0:4]
    seen[...] = jnp.zeros_like(seen)
    for group in range(4):
        seen[2 + group * 4 : 6 + group * 4] = masks[group, 0:4]
    stats[...] = jnp.zeros_like(stats)
    for part in range(2):
        stats[0:1, part * 128 : part * 128 + 128] = 1.0 - masks[f, pl.ds(quarter, 1), :]
    stats[1:2, 0:128] = total
    stats[2:3, 0:128] = 0.5 * masks[f, pl.ds(4 + quarter, 1), :]
    mine = spectrum[2 + block]
    lines[0:128] = mine[:, 0:128]
    lines[128:256] = mine[:, 128:256]
    sampled = seen[0:20]
    reach = [sampled[2:18]]
    reach.append(sampled[1:17] + sampled[2:18] + sampled[3:19])
    reach.append(reach[1] + sampled[0:16] + sampled[4:20])
    scales = [1.0 / jnp.maximum(count, 1.0) for count in reach]
    scales = [jnp.concatenate([scale, scale], axis=1) for scale in scales]

    loads[0].wait()
    channel = lax.rem(lax.broadcasted_iota(jnp.int32, (128, 256), 0), 8)
    table = rows_table[...].astype(F32)
    tables = [
        jnp.where(channel < 4, table, 0.0),
        jnp.where((channel == 4) | (channel == 5), table, 0.0),
        jnp.where(channel > 5, table, 0.0),
    ]
    for frame in range(16):
        near = [spectrum[frame + step].astype(F32) for step in range(5)]
        sums = [near[2]]
        sums.append(near[1] + near[2] + near[3])
        sums.append(sums[1] + near[0] + near[4])
        left = [(tables[radius] * scales[radius][frame : frame + 1]).astype(BF) for radius in range(3)]
        right = []
        for radius in range(3):
            value = sums[radius].astype(BF)
            right += [value[:, 0:128], value[:, 128:256]]
        image = dot(jnp.concatenate(left, axis=1), jnp.concatenate(right, axis=0))
        natural[frame] = image.astype(BF)

        def store(slabs, values, frame=frame):
            feature[frame + 1, slabs] = values

        put_slabs(store, jnp.transpose(image.astype(BF)).astype(F32))
    move(natural, natural_hbm, done, 0)
    loads.append(move(fwd_mid_hbm, fwd_mid, came, 2))
    loads[1].wait()
    half_lane = lax.broadcasted_iota(jnp.int32, (1, 128), 1) // 64

    def finish_first(hidden, frame, pair, at):
        chunk = hidden[at : at + 128, pair * 128 : pair * 128 + 128]
        value, slope = gelu_and_slope(chunk + bias[0:1, pair * 128 : pair * 128 + 128])
        if pair in (0, 5):
            row = block * 8 - 2 + 2 * pair + half_lane
            value = jnp.where((row >= 0) & (row < 128), value, 0.0)
        else:
            at = (pair - 1) * 128
            slope_in[pl.ds(frame * 128, 128), at : at + 128] = slope.astype(BF)
            turned[frame + 1, :, at : at + 128] = jnp.transpose(value.astype(BF))

        def store(slabs, values):
            active[frame + 1, pair, slabs] = values

        put_slabs(store, value)

    def first_product(group):
        pieces = []
        for time_off in range(3):
            for col_off in range(3):
                piece = feature[group * 2 + time_off : group * 2 + time_off + 2, col_off : col_off + 8]
                pieces.append(piece.reshape(256, 128))
        return dot(jnp.concatenate(pieces, axis=1), fwd_in[...])

    def finish_frames(hidden, group):
        for step in range(2):
            for pair in range(6):
                finish_first(hidden, group * 2 + step, pair, step * 128)

    firsts = (hidden, hidden_other)
    hidden[...] = first_product(0)
    for group in range(1, 8):
        firsts[group % 2][...] = first_product(group)
        finish_frames(firsts[(group - 1) % 2], group - 1)
    finish_frames(firsts[1], 7)
    move(slope_in, slope_in_hbm, done, 2)
    move(turned, turned_hbm, done, 1)
    loads[2].wait()

    def finish_second(second, pair_of, pair, at):
        for side in range(2):
            chunk = second[at : at + 128, side * 128 : side * 128 + 128]
            value, slope = gelu_and_slope(chunk + bias[1:2, 0:128])
            if pair in (0, 4):
                row = block * 8 - 1 + 2 * pair + half_lane
                inside = (row >= 0) & (row < 128)
                value = jnp.where(inside, value, 0.0)
                slope = jnp.where(inside, slope, 0.0)
            row = (pair_of * 2 + side) * 128
            active_out[pl.ds(row, 128), pair * 128 : pair * 128 + 128] = value.astype(BF)
            slope_out[pl.ds(row, 128), pair * 128 : pair * 128 + 128] = slope.astype(BF)

    def finish_group(second, group):
        for pair in range(5):
            finish_second(second, group, pair, pair * 128)
        rows = pl.ds(group * 256, 256)
        made = dot(active_out[rows], fwd_out[...])
        for frame in range(2):
            taps[group * 2 + frame + 1] = jnp.transpose(made[frame * 128 : frame * 128 + 128])[0:144]
        move(active_out.at[rows], active_hbm.at[rows], done, 3)
        move(slope_out.at[rows], slope_out_hbm.at[rows], done, 4)

    def second_product(pair_of):
        pieces = []
        for step in range(4):
            for col_off in range(3):
                pieces.append(two_rows(active, pair_of * 2 + step, 0, 5, col_off))
        return dot(jnp.concatenate(pieces, axis=1), fwd_mid[...])

    seconds = (second, second_other)
    second[...] = second_product(0)
    for group in range(1, 8):
        seconds[group % 2][...] = second_product(group)
        finish_group(seconds[(group - 1) % 2], group - 1)
    finish_group(seconds[1], 7)
    for frame in range(16):
        columns = []
        for col_off in range(3):
            value = None
            for time_off in range(3):
                at = (time_off * 3 + col_off) * 16
                piece = taps[frame + time_off, at : at + 16]
                value = piece if value is None else value + piece
            columns.append(value)
        result = previous_column(columns[0]) + columns[1] + next_column(columns[2])
        branch[frame * 16 : frame * 16 + 16] = result.astype(BF)
    stored = (natural, turned, slope_in, active_out, slope_out)
    homes = (natural_hbm, turned_hbm, slope_in_hbm, active_hbm, slope_out_hbm)
    for at, (source, to) in enumerate(zip(stored, homes)):
        pltpu.make_async_copy(source, to, done.at[at]).wait()


def consistency_kernel(
    gathered, lines, stats, own, others, to_lines, to_rows, lines_again, spread, out, loss, target
):
    f, half, chip, core = place()
    for side, source in enumerate((own, others[256:320])):
        for slot in range(4):
            row = jnp.bitwise_xor(half * 4 + chip * 2 + core, slot * 2 + side) * 16
            row = pl.multiple_of(row, 16)
            for part in range(2):
                target[pl.ds(part * 128 + row, 16), :] = source[slot * 16 : slot * 16 + 16, part * 128 : part * 128 + 128]
    weight = stats[2:3, 0:128]
    free = jnp.transpose(jnp.zeros((128, 128), F32) + stats[0:1, 0:128])
    free = jnp.concatenate([free, free], axis=0)
    wanted = target[...]
    made = dot(to_lines[...], gathered[...])
    wanted_spectrum = dot(lines_again[...], wanted)
    held = lines[...].astype(F32)
    kept = free * (made + held) + held
    grad = (free * (kept - wanted_spectrum) * (2.0 * weight)).astype(BF)
    out[...] = dot(spread[...], grad).astype(BF)
    residual = dot(to_rows[...], kept.astype(BF)) - wanted.astype(F32)
    loss[...] = jnp.zeros((8, 128), F32) + jnp.sum(residual * residual * weight)


def backward_kernel(
    grads, bwd_out_hbm, slope_out_hbm, active_hbm, turned_hbm, bwd_mid_hbm, slope_in_hbm, natural_hbm,
    out,
    bwd_out, slope_out, active, turned, bwd_mid, slope_in, natural, came,
    stack, product, product_other, grad_mid, grad_in, result, result_other, sum_mid, sum_out, sum_in, patches, tall, tiles, line,
):
    sources = (bwd_out_hbm, slope_out_hbm, active_hbm, turned_hbm, bwd_mid_hbm, slope_in_hbm, natural_hbm)
    targets = (bwd_out, slope_out, active, turned, bwd_mid, slope_in, natural)
    loads = [move(source, to, came, at) for at, (source, to) in enumerate(zip(sources[0:4], targets[0:4]))]
    zero32 = jnp.zeros((96, 128), BF)
    stack[0:96, 1920:2048] = zero32
    stack[192:288, 0:128] = zero32
    for frame in range(16):
        value = grads[frame * 32 : frame * 32 + 32].astype(F32)
        shifted = [next_column(value).astype(BF), value.astype(BF), previous_column(value).astype(BF)]
        for time_off in range(3):
            to = frame + time_off - 1
            if 0 <= to < 16:
                for col_off in range(3):
                    at = (time_off * 3 + col_off) * 32
                    stack[at : at + 32, to * 128 : to * 128 + 128] = shifted[col_off]
    grad_mid[0] = jnp.zeros((5, 10, 16, 128), BF)
    grad_mid[17] = jnp.zeros((5, 10, 16, 128), BF)
    tall[...] = jnp.zeros_like(tall)

    lane = lax.broadcasted_iota(jnp.int32, (1, 128), 1)
    bias_mid = jnp.zeros((1, 128), F32)
    buffers = (product, product_other)

    def finish_mid(buffer, group):
        own = jnp.zeros((1, 128), F32)
        for step in range(4):
            frame = group * 4 + step
            for pair in range(5):
                chunk = buffer[step * 128 : step * 128 + 128, pair * 128 : pair * 128 + 128]
                slope = slope_out[frame * 128 : frame * 128 + 128, pair * 128 : pair * 128 + 128]
                value = (chunk * slope.astype(F32)).astype(BF).astype(F32)
                added = jnp.sum(value, axis=0, keepdims=True)
                if pair == 0:
                    added = jnp.where(lane >= 64, added, 0.0)
                if pair == 4:
                    added = jnp.where(lane < 64, added, 0.0)
                own = own + added

                def store(slabs, values, frame=frame, pair=pair):
                    grad_mid[frame + 1, pair, slabs] = values

                put_slabs(store, value)
        return own

    loads[0].wait()
    groups = 16 // 4
    for group in range(groups + 1):
        if group < groups:
            at = group * 4 * 128
            buffers[group % 2][...] = dot_first(stack[:, at : at + 4 * 128], bwd_out[...])
        if group == 1:
            loads[1].wait()
            loads += [move(sources[at], targets[at], came, at) for at in (4, 5, 6)]
        if group > 0:
            bias_mid = bias_mid + finish_mid(buffers[(group - 1) % 2], group - 1)

    loads[2].wait()
    made = dot(stack[...], active[...])
    for pair in range(5):
        sum_out[pair] = made[:, pair * 128 : pair * 128 + 128]
    loads[3].wait()
    for group in range(16 // 4):
        frames = [group * 4 + step for step in range(4)]
        left = jnp.concatenate([turned[frame : frame + 3].reshape(384, 512) for frame in frames], axis=1)
        right = []
        for col_off in range(3):
            right.append(jnp.concatenate([two_rows(grad_mid, frame + 1, 0, 4, 2 - col_off) for frame in frames], axis=0))
        made = dot(left, jnp.concatenate(right, axis=1))
        sum_mid[...] = made if group == 0 else sum_mid[...] + made

    def lay_out_mid(time_off, row_off):
        for col_off in range(3):
            tap = (time_off * 3 + row_off) * 3 + col_off
            at, lane = time_off * 128, col_off * 256
            upper = sum_mid[at : at + 64, lane + (2 - row_off) * 64 : lane + (2 - row_off) * 64 + 64]
            lower = sum_mid[at + 64 : at + 128, lane + (3 - row_off) * 64 : lane + (3 - row_off) * 64 + 64]
            tall[tap * 64 : tap * 64 + 64, 0:64] = upper + lower

    def lay_out_last():
        for row_off in range(3):
            value = None
            for row in range(2, 10):
                lane = (row - 2 + row_off) * 64
                piece = sum_out[lane // 128, pl.ds(row, 18, stride=16), :][:, lane % 128 : lane % 128 + 64]
                value = piece if value is None else value + piece
            for time_off in range(3):
                for col_off in range(3):
                    tap = (time_off * 3 + row_off) * 3 + col_off
                    for part in range(2):
                        row = (time_off * 3 + col_off) * 2 + part
                        line[part : part + 1, tap * 64 : tap * 64 + 64] = value[row : row + 1]

    def lay_out_pieces():
        for owner in range(8):
            for part in range(2):
                for piece in range(4):
                    at = owner * 216 + piece * 54
                    row = owner * 8 + part * 4 + piece
                    tiles[13, row : row + 1, 64:118] = line[part : part + 1, at : at + 54]

    def lay_out_patches(first, last):
        for frame in range(first, last):
            value = natural[frame].astype(F32)
            shifted = (previous_column(value).astype(BF), natural[frame], next_column(value).astype(BF))
            for col_off in range(3):
                for pair in range(4):
                    piece = shifted[col_off][pair * 16 + 16 : pair * 16 + 48]
                    for time_off in range(3):
                        to = frame - time_off + 1
                        if 0 <= to < 16:
                            at = (time_off * 3 + col_off) * 32
                            lane = (to * 4 + pair) * 128
                            patches[at : at + 32, lane : lane + 128] = piece

    def input_product(group):
        rows = []
        for half_of in range(2):
            pieces = []
            for step in range(4):
                for col_off in range(3):
                    pieces.append(two_rows(grad_mid, group * 4 + half_of * 2 + step, 0, 4, col_off))
            rows.append(jnp.concatenate(pieces, axis=1))
        return dot(jnp.concatenate(rows, axis=0), bwd_mid[...])

    def finish_input(buffer, group):
        own = jnp.zeros((1, 128), F32)
        for half_of in range(2):
            for pair in range(4):
                for side in range(2):
                    frame = group * 4 + half_of * 2 + side
                    at = half_of * 512 + pair * 128
                    chunk = buffer[at : at + 128, side * 128 : side * 128 + 128]
                    slope = slope_in[frame * 128 : frame * 128 + 128, pair * 128 : pair * 128 + 128]
                    value = (chunk * slope.astype(F32)).astype(BF)
                    grad_in[frame * 512 + pair * 128 : frame * 512 + pair * 128 + 128, :] = value
                    own = own + jnp.sum(value.astype(F32), axis=0, keepdims=True)
        return own

    loads[4].wait()
    loads[5].wait()
    loads[6].wait()
    patches[0:96, 0:512] = jnp.zeros((96, 512), BF)
    patches[192:288, 7680:8192] = jnp.zeros((96, 512), BF)
    results = (result, result_other)
    bias_in = jnp.zeros((1, 128), F32)
    for group in range(5):
        if group < 4:
            results[group % 2][...] = input_product(group)
        if group == 0:
            for time_off in range(3):
                lay_out_mid(time_off, 0)
            lay_out_last()
            lay_out_patches(0, 4)
        else:
            bias_in = bias_in + finish_input(results[(group - 1) % 2], group - 1)
        if group == 1:
            for time_off in range(3):
                lay_out_mid(time_off, 1)
            lay_out_patches(4, 10)
        if group == 2:
            for time_off in range(3):
                lay_out_mid(time_off, 2)
            lay_out_patches(10, 16)
        if group == 3:
            for tile in range(14):
                tiles[tile] = jnp.transpose(tall[tile * 128 : tile * 128 + 128])[0:64]
            lay_out_pieces()

    sum_in[...] = dot(patches[...], grad_in[...])
    for time_off in range(3):
        for row_off in range(3):
            for col_off in range(3):
                tap = (time_off * 3 + row_off) * 3 + col_off
                at = (time_off * 3 + col_off) * 32 + row_off * 8
                upper = sum_in[at : at + 8, 0:64]
                lower = sum_in[at + 8 : at + 16, 64:128]
                tall[1792 + tap * 8 : 1792 + tap * 8 + 8, 0:64] = upper + lower
    tall[2008:2009, 0:64] = bias_in[:, 0:64] + bias_in[:, 64:128]
    tall[2009:2010, 0:64] = bias_mid[:, 0:64] + bias_mid[:, 64:128]
    for tile in range(14, 16):
        tiles[tile] = jnp.transpose(tall[tile * 128 : tile * 128 + 128])[0:64]
    for quarter in range(4):
        for owner in range(8):
            value = tiles[quarter * 4 : quarter * 4 + 4, owner * 8 : owner * 8 + 8]
            out[quarter * 8 + owner] = value.reshape(32, 128).astype(BF)


def sum_kernel(parts, stats, loss, shard, shared):
    total = parts[0].astype(F32)
    for source in range(1, 32):
        total = total + parts[source].astype(F32)
    divisor = jnp.maximum(stats[1:2, 0:1] * (2.0 * 128 * 128), 1.0)
    total = total / divisor
    shard[...] = total
    lane = lax.broadcasted_iota(jnp.int32, (32, 128), 1)
    shared[...] = jnp.where(lane == 0, jnp.sum(total * total), loss[0:1] + jnp.zeros((32, 128), F32))


def update_kernel(
    own, near, mid, far, messages, stats,
    w_in, w_mid, w_out, w_bias, f_in, f_mid, f_out, f_bias, s_in, s_mid, s_out, s_bias,
    loss_sum, valid_count, grad_norm, mf_in, mf_mid, mf_out, mf_bias, ms_in, ms_mid, ms_out, ms_bias,
    mw_in, mw_mid, mw_out, mw_bias, mc_in, mc_mid, mc_out, mc_bias,
    shards, g_mid, g_in, g_out, g_bias,
):
    f, half, chip, core = place()
    for slot, source in enumerate((own, near, mid, far)):
        shards[jnp.bitwise_xor(f, slot)] = source[...]
    message = jnp.sum(messages[...], axis=0, keepdims=True)
    norm = jnp.sqrt(message[:, 0:1])
    loss_sum[0, 0] = jnp.sum(message[:, 1:2])
    valid_count[0, 0] = jnp.sum(stats[1:2, 0:1]) * (2.0 * 128 * 128)
    grad_norm[0, 0] = jnp.sum(norm)
    factor = jnp.minimum(1.0, CLIP / (norm + 1e-06))

    def tile_of(tile):
        at = (tile % 4) * 8
        return shards[tile // 4, at : at + 8]

    for tile in range(13):
        g_mid[:, tile * 128 : tile * 128 + 128] = tile_of(tile)
    mixed = tile_of(13)
    g_mid[:, 1664:1728] = mixed[:, 0:64]
    for part in range(2):
        for piece in range(4):
            row = part * 4 + piece
            g_out[part : part + 1, piece * 54 : piece * 54 + 54] = mixed[row : row + 1, 64:118]
    g_in[:, 0:128] = tile_of(14)
    mixed = tile_of(15)
    g_in[:, 128:216] = mixed[:, 0:88]
    square = jnp.concatenate([mixed, jnp.zeros((120, 128), F32)], axis=0)
    g_bias[...] = jnp.transpose(square)[88:90, 0:8]
    for grad, weight, one, two, new_one, new_two, new_weight, new_copy in (
        (g_in, w_in, f_in, s_in, mf_in, ms_in, mw_in, mc_in),
        (g_mid, w_mid, f_mid, s_mid, mf_mid, ms_mid, mw_mid, mc_mid),
        (g_out, w_out, f_out, s_out, mf_out, ms_out, mw_out, mc_out),
        (g_bias, w_bias, f_bias, s_bias, mf_bias, ms_bias, mw_bias, mc_bias),
    ):
        results = adamw(weight[...], grad[...] * factor, one[...], two[...])
        for ref, value in zip((new_one, new_two, new_weight, new_copy), results):
            ref[...] = value


VECTOR = pl.BlockSpec(memory_space=pltpu.VMEM)
SCALAR = pl.BlockSpec(memory_space=pltpu.SMEM)
LEFT = pl.BlockSpec(memory_space=pl.ANY)


def shape(*dims, dtype=BF):
    return jax.ShapeDtypeStruct(dims, dtype)


def kernel_call(kernel, name, micros, operands, results, scratch, in_specs=None, out_specs=None):
    return pl.pallas_call(
        kernel,
        name=name,
        out_shape=results,
        in_specs=in_specs or [VECTOR] * len(operands),
        out_specs=out_specs or [VECTOR] * len(results),
        scratch_shapes=scratch,
        cost_estimate=pl.CostEstimate(flops=int(micros * 1e9), bytes_accessed=0, transcendentals=0),
        compiler_params=pltpu.CompilerParams(vmem_limit_bytes=VMEM),
    )(*operands)


def swap(value, axis, bit):
    return lax.ppermute(value, axis, [(i, i ^ bit) for i in range(lax.axis_size(axis))])


def by_rows(
    kspace, line_mask, valid_flags, target, conv_in, conv_mid, conv_out, conv_bias,
    first_in, first_mid, first_out, first_bias, second_in, second_mid, second_out, second_bias,
):
    tables = make_tables()

    mine, theirs, far, mine_target = kernel_call(
        lines_kernel,
        "prepare_lines",
        2,
        [
            valid_flags, kspace.reshape(2, 4, 32, 128), line_mask.reshape(8, 16), target.reshape(2, 4, 32, 128),
            tables["columns"], tables["permute"], conv_mid[0, 0].T, conv_in[0].T, conv_out[0], conv_bias[0],
        ],
        [shape(176, 256), shape(176, 256), shape(176, 256), shape(32, 256)],
        [pltpu.VMEM((2, 80, 256), BF), pltpu.VMEM((2, 4, 16, 256), BF), pltpu.VMEM((16, 8, 128), F32)],
        in_specs=[SCALAR] + [VECTOR] * 9,
    )

    sent = ((mine, 1), (theirs, 2), (far, 3))
    beside, other, far = (swap(value, ("half", "chip"), step) for value, step in sent)

    def two(one, another):
        return jnp.concatenate([one[0:64], another[0:64], one[64:80] + another[64:80]], axis=0)

    half_a, half_b = two(mine, beside), two(other, far)
    column = jnp.concatenate([half_a, half_b], axis=0)
    gathered = [column] + [swap(column, "frames", step) for step in (1, 2, 3)]
    sources = (mine, beside, other, far)
    images = [mine_target, beside[144:176], other[144:176], far[144:176]]
    chips = jnp.concatenate([source[80:144] for source in sources] + [image[16:32] for image in images], axis=0)
    others = swap(chips, "core", 1)
    scratch = [pltpu.VMEM((16, 64, 128), F32), pltpu.VMEM((2, 1792), F32), pltpu.VMEM((64, 128), F32)]
    fwd_in, fwd_mid, fwd_out, bias = kernel_call(
        forward_weight_kernel,
        "lay_out_forward_weights",
        4,
        [chips, others, tables["pick_out"]],
        [shape(1152, 768), shape(3072, 256), shape(640, 256), shape(8, 768, dtype=F32)],
        scratch,
    )
    *gathered, bias = lax.optimization_barrier((*gathered, bias))
    gathered += [swap(piece, "core", 1) for piece in gathered]
    kept = [(16, 128, 128), (18, 128, 512), (2048, 640), (2048, 512), (2048, 640)]
    moved = [(128, 256), (1152, 768), (3072, 256)]
    branch, stats, lines, natural, turned, active, slope_in, slope_out = kernel_call(
        forward_kernel,
        "features_and_branch",
        27,
        [*gathered, tables["feature"], fwd_in, fwd_mid, fwd_out, bias],
        [shape(256, 128), shape(8, 256, dtype=F32), shape(256, 128)] + [shape(*dims) for dims in kept],
        [pltpu.VMEM(dims, BF) for dims in moved]
        + [pltpu.SemaphoreType.DMA((3,))]
        + [
            pltpu.VMEM((20, 128, 256), BF),
            pltpu.VMEM((4, 8, 128), F32),
            pltpu.VMEM((24, 128), F32),
            pltpu.VMEM((18, 10, 16, 128), BF),
            pltpu.VMEM((18, 6, 10, 16, 128), BF),
            pltpu.VMEM((256, 768), F32),
            pltpu.VMEM((256, 768), F32),
            pltpu.VMEM((640, 256), F32),
            pltpu.VMEM((640, 256), F32),
            pltpu.VMEM((18, 144, 128), F32),
        ]
        + [pltpu.VMEM(dims, BF) for dims in kept]
        + [pltpu.SemaphoreType.DMA((5,))],
        in_specs=[VECTOR] * 8 + [LEFT] * 3 + [VECTOR] * 2,
        out_specs=[VECTOR] * 3 + [LEFT] * 5,
    )
    branch, *images = lax.optimization_barrier((branch, *images))
    wanted = jnp.concatenate([image[0:16] for image in images], axis=0)
    branch, chips, others = lax.optimization_barrier((branch, chips, others))
    bwd_mid, bwd_out = kernel_call(
        backward_weight_kernel,
        "lay_out_backward_weights",
        3,
        [chips, others, tables["pick_back"]],
        [shape(3072, 256), shape(288, 640)],
        scratch,
    )
    lines, bwd_out = lax.optimization_barrier((lines, bwd_out))
    by_frame = lax.all_to_all(branch.reshape(16, 16, 128), ("frames", "chip", "core"), 0, 0, tiled=True)
    grads, loss = kernel_call(
        consistency_kernel,
        "data_consistency",
        2.5,
        [
            by_frame.reshape(256, 128), lines, stats, wanted, others,
            tables["to_lines"], tables["to_rows"], tables["lines_again"], tables["spread"],
        ],
        [shape(512, 128), shape(8, 128, dtype=F32)],
        [pltpu.VMEM((256, 128), BF)],
    )
    by_block = lax.all_to_all(grads.reshape(16, 32, 128), ("frames", "chip", "core"), 0, 0, tiled=True)
    moved = [(288, 640), (2048, 640), (2048, 640), (18, 128, 512), (3072, 256), (2048, 512), (16, 128, 128)]
    (parts,) = kernel_call(
        backward_kernel,
        "weight_gradients",
        27,
        [by_block.reshape(512, 128), bwd_out, slope_out, active, turned, bwd_mid, slope_in, natural],
        [shape(32, 32, 128)],
        [pltpu.VMEM(dims, BF) for dims in moved]
        + [pltpu.SemaphoreType.DMA((7,))]
        + [
            pltpu.VMEM((288, 2048), BF),
            pltpu.VMEM((512, 640), F32),
            pltpu.VMEM((512, 640), F32),
            pltpu.VMEM((18, 5, 10, 16, 128), BF),
            pltpu.VMEM((8192, 128), BF),
            pltpu.VMEM((1024, 256), F32),
            pltpu.VMEM((1024, 256), F32),
            pltpu.VMEM((384, 768), F32),
            pltpu.VMEM((5, 288, 128), F32),
            pltpu.VMEM((288, 128), F32),
            pltpu.VMEM((288, 8192), BF),
            pltpu.VMEM((2048, 128), F32),
            pltpu.VMEM((16, 64, 128), F32),
            pltpu.VMEM((2, 1792), F32),
        ],
        in_specs=[VECTOR] + [LEFT] * 7,
    )
    parts = lax.all_to_all(parts, ("frames", "half", "chip", "core"), 0, 0, tiled=True)
    shard, messages = kernel_call(
        sum_kernel,
        "sum_gradients",
        2,
        [parts, stats, loss],
        [shape(32, 128, dtype=F32), shape(32, 128, dtype=F32)],
        [],
    )
    shards = [shard] + [swap(shard, "frames", step) for step in (1, 2, 3)]
    messages = lax.all_to_all(messages, ("frames", "half", "chip", "core"), 0, 0, tiled=True)
    groups = (
        (conv_in, conv_mid, conv_out, conv_bias),
        (first_in, first_mid, first_out, first_bias),
        (second_in, second_mid, second_out, second_bias),
    )
    state = []
    for of_in, of_mid, of_out, of_bias in groups:
        state += [of_in[0].T, of_mid[0, 0].T, of_out[0], of_bias[0]]
    shapes = [(8, 216), (8, 1728), (2, 216), (2, 8)]
    results = kernel_call(
        update_kernel,
        "adamw",
        2,
        [*shards, messages, stats, *state],
        [shape(1, 1, dtype=F32)] * 3
        + [shape(*dims, dtype=F32) for dims in shapes * 3]
        + [shape(*dims, dtype=BF) for dims in shapes],
        [pltpu.VMEM((4, 32, 128), F32)] + [pltpu.VMEM(shapes[at], F32) for at in (1, 0, 2, 3)],
        out_specs=[SCALAR] * 3 + [VECTOR] * 16,
    )
    outputs = [result[0, 0] for result in results[0:3]]
    for at in range(3, 19, 4):
        of_in, of_mid, of_out, of_bias = results[at : at + 4]
        outputs += [of_in.T[None], of_mid.T[None, None], of_out[None], of_bias[None]]
    return tuple(outputs)


def specs_for(rows):
    lines = P(None, "frames", rows)
    images = P(None, "frames", rows, None, None)
    weights = [P(None, None, rows), P(None, None, None, rows), P(None, None, rows), P(None, None, rows)]
    in_specs = (images, lines, P(None, "frames"), images, *(weights * 3))
    out_specs = (P(), P(), P(), *(weights * 4))
    return in_specs, out_specs


def solution(mesh):
    frames, rows = (mesh.shape[axis] for axis in ("frames", "rows"))
    if (frames, rows) != (4, 8):
        in_specs, out_specs = specs_for("rows")
        return jax.shard_map(local, mesh=mesh, in_specs=in_specs, out_specs=out_specs, check_vma=False)
    chips = Mesh(mesh.devices.reshape(frames, 2, rows // 4, 2), ("frames", "half", "chip", "core"))
    in_specs, out_specs = specs_for(("half", "chip", "core"))
    return jax.shard_map(by_rows, mesh=chips, in_specs=in_specs, out_specs=out_specs, check_vma=False)
```

```python
import jax
import jax.numpy as jnp
import ml_dtypes
import numpy as np
from jax import lax
from jax.experimental import pallas as pl
from jax.experimental.pallas import tpu as pltpu
from jax.sharding import Mesh
from jax.sharding import PartitionSpec as P

NX = 128
CAS = 1
MIDS = 1
STEP = 10


CLIP = 0.05
RATE = 0.03
BETA_ONE = 0.9
BETA_TWO = 0.999
EPSILON = 1e-08
DECAY = 0.01
HIGHEST = lax.Precision.HIGHEST


def with_halo(shard, sides, width):
    for axis, dim in sides:
        size, length = (lax.axis_size(axis), shard.shape[dim])
        up = [(i, (i + 1) % size) for i in range(size - 1)]
        down = [(j, i) for i, j in up]
        last = lax.slice_in_dim(shard, length - width, length, axis=dim)
        first = lax.slice_in_dim(shard, 0, width, axis=dim)
        before = lax.ppermute(last, axis, up)
        after = lax.ppermute(first, axis, down)
        shard = jnp.concatenate([before, shard, after], axis=dim)
    return shard


def from_behind(block, axis, distance):
    devices = range(lax.axis_size(axis))
    route = [(i - distance, i) for i in devices if i - distance in devices]
    return lax.ppermute(block, axis, route)


def dft_blocks(length, sign):
    counter = jnp.arange(length, dtype=jnp.int32)
    turns = counter[:, None] * counter[None, :] % length
    angle = turns.astype(jnp.float32) * (2.0 * jnp.pi / length)
    norm_factor = 1.0 / jnp.sqrt(jnp.float32(length))
    cosine = jnp.cos(angle) * norm_factor
    sine = sign * jnp.sin(angle) * norm_factor
    return jnp.stack([jnp.stack([cosine, -sine]), jnp.stack([sine, cosine])])


def transform(image, sign):
    rows_here = image.shape[1]
    rows_all = rows_here * lax.axis_size("rows")
    first_row = lax.axis_index("rows") * rows_here
    across = jnp.einsum(
        "byix,oikx->byok", image, dft_blocks(image.shape[3], sign), precision=HIGHEST
    )
    table = dft_blocks(rows_all, sign)
    window = lax.dynamic_slice(
        table, (0, 0, 0, first_row), (2, 2, lax.axis_size("rows") * rows_here, rows_here)
    )
    return lax.psum_scatter(
        jnp.einsum("byix,oiky->kbox", across, window, precision=HIGHEST),
        "rows",
        scatter_dimension=0,
        tiled=True,
    ).transpose(1, 0, 2, 3)


def taps(widened, offset, frames, rows_here, columns):
    time_off = offset // 3
    row_off = offset % 3
    return jnp.concatenate(
        [
            widened[
                time_off : time_off + frames,
                row_off : row_off + rows_here,
                :,
                col_off : col_off + columns,
            ]
            for col_off in range(3)
        ],
        axis=2,
    )


def convolve(padded, kernel):
    frames = padded.shape[0] - 2
    rows_here = padded.shape[1] - 2
    width_in = padded.shape[2]
    columns = padded.shape[3]
    widened = jnp.pad(padded, ((0, 0), (0, 0), (0, 0), (1, 1)))
    blocks = kernel.reshape(9, 3 * width_in, kernel.shape[1])
    summed = jnp.zeros((frames, rows_here, kernel.shape[1], columns), jnp.float32)
    for offset in range(9):
        gathered = taps(widened, offset, frames, rows_here, columns)
        summed = summed + jnp.einsum(
            "tykx,kj->tyjx", gathered, blocks[offset], preferred_element_type=jnp.float32
        )
    return summed


def kernel_grad(padded, grad_out):
    frames, rows_here, columns = (grad_out.shape[0], grad_out.shape[1], grad_out.shape[3])
    widened = jnp.pad(padded, ((0, 0), (0, 0), (0, 0), (1, 1)))
    pieces = [
        jnp.einsum(
            "tykx,tyjx->kj",
            taps(widened, offset, frames, rows_here, columns),
            grad_out,
            preferred_element_type=jnp.float32,
        )
        for offset in range(9)
    ]
    return jnp.concatenate(pieces, axis=0)


def flipped(kernel):
    width_in = kernel.shape[0] // 27
    shaped = kernel.reshape(3, 3, 3, width_in, kernel.shape[1])[::-1, ::-1, ::-1]
    return shaped.transpose(0, 1, 2, 4, 3).reshape(27 * kernel.shape[1], width_in)


def activation_rim(values):
    return with_halo(values, (("frames", 0), ("rows", 1)), 1)


def gradient_rim(values):
    return with_halo(values, (("frames", 0), ("rows", 1)), 1)


def layer_forward(inputs, kernel, bias_row):
    padded = activation_rim(inputs)
    return (padded, convolve(padded, kernel) + bias_row.astype(jnp.float32)[None, None, :, None])


def layer_backward(padded, kernel, grad_hidden, needs_input):
    kernel_delta = kernel_grad(padded, grad_hidden)
    bias_delta = jnp.sum(grad_hidden, axis=(0, 1, 3), dtype=jnp.float32)
    input_delta = None
    if needs_input:
        input_delta = convolve(gradient_rim(grad_hidden), flipped(kernel))
    return (kernel_delta, bias_delta, input_delta)


def share(measured, sampled):
    frames = measured.shape[0]
    reach = (frames + 1) // frames
    before = []
    after = []
    for distance in range(1, reach + 1):
        for direction in (1, -1):
            moved = from_behind((measured, sampled), "frames", direction * distance)
            if direction == 1:
                before.insert(0, moved)
            else:
                after.append(moved)
    data_line = jnp.concatenate(
        [moved_pair[0] for moved_pair in before]
        + [measured]
        + [moved_pair[0] for moved_pair in after],
        axis=0,
    )
    mask_line = jnp.concatenate(
        [moved_pair[1] for moved_pair in before]
        + [sampled]
        + [moved_pair[1] for moved_pair in after],
        axis=0,
    )
    centre = reach * frames
    windows = []
    for radius in range(3):
        data_sum = data_line[centre - radius : centre - radius + frames]
        mask_sum = mask_line[centre - radius : centre - radius + frames]
        for offset in range(1 - radius, radius + 1):
            data_sum = data_sum + data_line[centre + offset : centre + offset + frames]
            mask_sum = mask_sum + mask_line[centre + offset : centre + offset + frames]
        windows.append(data_sum / jnp.maximum(mask_sum, 1.0)[:, :, None, None])
    return jnp.stack(windows, 1)


def adamw(weight, grad_piece, moment_one, moment_two):
    first_new = BETA_ONE * moment_one + (1.0 - BETA_ONE) * grad_piece
    second_new = BETA_TWO * moment_two + (1.0 - BETA_TWO) * grad_piece * grad_piece
    ascent = (
        first_new
        / (1.0 - BETA_ONE**STEP)
        / (jnp.sqrt(second_new / (1.0 - BETA_TWO**STEP)) + EPSILON)
    )
    weight_new = weight - RATE * (ascent + DECAY * weight)
    return (first_new, second_new, weight_new, weight_new.astype(jnp.bfloat16))


def local(
    kspace,
    line_mask,
    valid_flags,
    target,
    conv_in,
    conv_mid,
    conv_out,
    conv_bias,
    first_in,
    first_mid,
    first_out,
    first_bias,
    second_in,
    second_mid,
    second_out,
    second_bias,
):
    masters = (conv_in, conv_mid, conv_out, conv_bias)

    def reduce_grads(grads):
        shards = (
            lax.psum_scatter(
                grads[0].astype(jnp.bfloat16), "rows", scatter_dimension=2, tiled=True
            ).astype(jnp.float32),
            lax.psum_scatter(
                grads[1].astype(jnp.bfloat16), "rows", scatter_dimension=3, tiled=True
            ).astype(jnp.float32),
            lax.psum_scatter(
                grads[2].astype(jnp.bfloat16), "rows", scatter_dimension=2, tiled=True
            ).astype(jnp.float32),
            lax.psum_scatter(
                grads[3].astype(jnp.bfloat16), "rows", scatter_dimension=2, tiled=True
            ).astype(jnp.float32),
        )
        return lax.psum((shards[0], shards[1], shards[2], shards[3]), "frames")

    def micro_batch(carry, batch_data):
        grad_carry, loss_carry, count_carry = carry
        measured_full, mask_rows, frame_flags, wanted = batch_data
        full_in, full_mid, full_out, full_bias = (
            lax.all_gather(conv_in.astype(jnp.bfloat16), "rows", axis=2, tiled=True),
            lax.all_gather(conv_mid.astype(jnp.bfloat16), "rows", axis=3, tiled=True),
            lax.all_gather(conv_out.astype(jnp.bfloat16), "rows", axis=2, tiled=True),
            lax.all_gather(conv_bias.astype(jnp.bfloat16), "rows", axis=2, tiled=True),
        )
        sampled = mask_rows.astype(jnp.float32)
        measured = measured_full * sampled[:, :, None, None]
        shared = share(measured, sampled)
        frames, rows_here = (measured.shape[0], measured.shape[1])
        images = transform(shared.reshape(frames * 3, rows_here, 2, NX), 1.0).reshape(
            frames, 3, rows_here, 2, NX
        )
        shared_images = images.transpose(0, 2, 1, 3, 4).reshape(frames, rows_here, 6, NX)
        current = images[:, 0]
        unsampled = (1.0 - sampled)[:, :, None, None]
        no_bias = jnp.zeros((2,), jnp.bfloat16)

        def kernels_of(cascade):
            return [full_in[cascade]] + [full_mid[cascade, 0]] + [full_out[cascade].T]

        cascade = 0
        kernels = kernels_of(cascade)
        biases = [full_bias[cascade, layer_at] for layer_at in range(MIDS + 1)] + [no_bias]
        inputs = jnp.concatenate([current, shared_images], axis=2).astype(jnp.bfloat16)
        saved = []
        for layer_at in range(MIDS + 2):
            padded, hidden = layer_forward(inputs, kernels[layer_at], biases[layer_at])
            saved.append((padded, hidden))
            if layer_at < MIDS + 1:
                inputs = jax.nn.gelu(hidden).astype(jnp.bfloat16)
        current = transform(unsampled * transform(current + hidden, -1.0) + measured, 1.0)
        kept = [saved]
        frame_weight = frame_flags.astype(jnp.float32)[:, None, None, None]
        residual_error = current - wanted
        loss_part = jnp.sum(frame_weight * residual_error * residual_error)
        count_part = 2.0 * rows_here * NX * jnp.sum(frame_flags.astype(jnp.float32))
        grad_current = 2.0 * frame_weight * residual_error
        delta_in = [None] * CAS
        delta_mid = [None] * CAS
        delta_out = [None] * CAS
        delta_bias = [None] * CAS
        for cascade in reversed(range(CAS)):
            kernels = kernels_of(cascade)
            grad_sum = transform(unsampled * transform(grad_current, -1.0), 1.0)
            grad_hidden = grad_sum.astype(jnp.bfloat16)
            kernel_deltas = [None] * (MIDS + 2)
            bias_deltas = [None] * (MIDS + 2)
            grad_input = None
            for layer_at in reversed(range(MIDS + 2)):
                padded, hidden = kept[cascade][layer_at]
                if layer_at < MIDS + 1:
                    pullback = jax.vjp(jax.nn.gelu, hidden)[1]
                    grad_hidden = pullback(grad_input)[0].astype(jnp.bfloat16)
                needs_input = cascade > 0 or layer_at > 0
                kernel_deltas[layer_at], bias_deltas[layer_at], grad_input = layer_backward(
                    padded, kernels[layer_at], grad_hidden, needs_input
                )
            delta_in[cascade] = kernel_deltas[0]
            delta_mid[cascade] = jnp.stack(kernel_deltas[1 : MIDS + 1])
            delta_out[cascade] = kernel_deltas[MIDS + 1].T
            delta_bias[cascade] = jnp.stack(bias_deltas[0 : MIDS + 1])
        grads = (
            jnp.stack(delta_in),
            jnp.stack(delta_mid),
            jnp.stack(delta_out),
            jnp.stack(delta_bias),
        )
        grads = reduce_grads(grads)
        grad_carry = jax.tree.map(jnp.add, grad_carry, grads)
        return ((grad_carry, loss_carry + loss_part, count_carry + count_part), None)

    start_grads = jax.tree.map(jnp.zeros_like, masters)
    start = (start_grads, jnp.zeros((), jnp.float32), jnp.zeros((), jnp.float32))
    (summed, loss_local, count_local), unused = lax.scan(
        micro_batch, start, (kspace, line_mask, valid_flags, target)
    )
    summed = tuple(summed)
    loss_sum, valid_count = lax.psum((loss_local, count_local), ("frames", "rows"))
    divisor = jnp.maximum(valid_count, 1.0)
    grads = [grad_piece / divisor for grad_piece in summed]
    squares = sum((jnp.sum(grad_piece * grad_piece) for grad_piece in grads))
    grad_norm = jnp.sqrt(lax.psum(squares, "rows"))
    factor = jnp.minimum(1.0, CLIP / (grad_norm + 1e-06))
    firsts = (first_in, first_mid, first_out, first_bias)
    seconds = (second_in, second_mid, second_out, second_bias)
    results = [
        adamw(masters[which], grads[which] * factor, firsts[which], seconds[which])
        for which in range(4)
    ]
    return (
        loss_sum,
        valid_count,
        grad_norm,
        results[0][0],
        results[1][0],
        results[2][0],
        results[3][0],
        results[0][1],
        results[1][1],
        results[2][1],
        results[3][1],
        results[0][2],
        results[1][2],
        results[2][2],
        results[3][2],
        results[0][3],
        results[1][3],
        results[2][3],
        results[3][3],
    )


BF = jnp.bfloat16
F32 = jnp.float32
SQRT_TWO_OVER_PI = 0.7978845608028654
CUBIC = 0.044715 * SQRT_TWO_OVER_PI
UNITS = 16


def column_order():
    lanes = np.arange(128)
    return (lanes % 16) * 8 + lanes // 16


def dft_tables(sign):
    counter = np.arange(128)
    angle = (counter[:, None] * counter[None, :] % 128) * (2.0 * np.pi / 128)
    cosine, sine = np.cos(angle) / np.sqrt(128.0), sign * np.sin(angle) / np.sqrt(128.0)
    return np.stack([np.stack([cosine, -sine]), np.stack([sine, cosine])])


def make_tables():
    inverse, forward = dft_tables(1.0), dft_tables(-1.0)
    order = column_order()
    columns = inverse[:, :, :, order].transpose(1, 2, 0, 3).reshape(256, 256)
    blocks = np.arange(UNITS)[:, None] * 8

    def rows_of(first, kept):
        rows = blocks + first + np.arange(16)[None, :]
        inside = (rows >= 0) & (rows < 128) & (np.arange(16)[None, :] < kept)
        return np.clip(rows, 0, 127), inside

    rows, inside = rows_of(-3, 14)
    feature = inverse[:, :, rows, :] * inside[None, None, :, :, None]
    feature = feature.transpose(2, 3, 0, 1, 4).reshape(UNITS, 16, 2, 256)
    feature = np.tile(feature, (1, 1, 4, 1)).reshape(UNITS, 128, 256)
    to_lines = forward.reshape(2, 2, 128, UNITS, 8).transpose(0, 2, 3, 1, 4).reshape(256, 256)
    to_rows = inverse.transpose(0, 2, 1, 3).reshape(256, 256)
    lines_again = forward.transpose(0, 2, 1, 3).reshape(256, 256)
    rows, inside = rows_of(-2, 12)
    spread = inverse[:, :, rows, :] * inside[None, None, :, :, None]
    spread = spread.transpose(2, 0, 3, 1, 4).reshape(UNITS * 32, 256)
    permute = np.zeros((128, 128))
    permute[order, np.arange(128)] = 1.0
    pick_out = np.zeros((64, 10, 256))
    pick_back = np.zeros((10, 288, 64))
    for time_off in range(3):
        for row_off in range(3):
            for col_off in range(3):
                tap = (time_off * 3 + row_off) * 3 + col_off
                for part in range(2):
                    for row in range(8):
                        lane = (time_off * 3 + col_off) * 16 + part * 8 + row
                        pick_out[tap * 2 + part, row + row_off, lane] = 1.0
                    for row in range(12):
                        into = row + row_off - 2
                        if 0 <= into < 10:
                            at = (time_off * 3 + col_off) * 32 + part * 16 + row
                            pick_back[into, at, tap * 2 + part] = 1.0
    made = dict(
        columns=columns,
        feature=feature,
        to_lines=to_lines,
        lines_again=lines_again,
        to_rows=to_rows,
        spread=spread,
        permute=permute,
        pick_out=pick_out.reshape(64, 2560),
        pick_back=pick_back.reshape(2880, 64),
    )
    return {name: jnp.asarray(table.astype(ml_dtypes.bfloat16)) for name, table in made.items()}


def dot(left, right):
    return jnp.dot(left, right, preferred_element_type=F32)


def dot_first(left, right):
    return lax.dot_general(left, right, (((0,), (0,)), ((), ())), preferred_element_type=F32)


def next_column(values):
    lane = lax.broadcasted_iota(jnp.int32, values.shape, 1)
    inner = pltpu.roll(values, 112, 1)
    wrapped = jnp.where(lane == 127, 0.0, pltpu.roll(values, 111, 1))
    return jnp.where(lane < 112, inner, wrapped)


def previous_column(values):
    lane = lax.broadcasted_iota(jnp.int32, values.shape, 1)
    inner = pltpu.roll(values, 16, 1)
    wrapped = jnp.where(lane == 0, 0.0, pltpu.roll(values, 17, 1))
    return jnp.where(lane >= 16, inner, wrapped)


def put_slabs(store, values):
    store(slice(1, 9), values.astype(BF).reshape(8, 16, 128))
    first, last = values[0:16], values[112:128]
    at = lax.broadcasted_iota(jnp.int32, (16, 128), 0)
    before = jnp.where(at == 0, 0.0, pltpu.roll(last, 1, 0))
    after = jnp.where(at == 15, 0.0, pltpu.roll(first, 15, 0))
    store(slice(0, 1), before.astype(BF).reshape(1, 16, 128))
    store(slice(9, 10), after.astype(BF).reshape(1, 16, 128))


def two_rows(ref, frame, pair, count, first_slab):
    upper = ref[frame, pair : pair + count, first_slab : first_slab + 8]
    lower = ref[frame, pair + 1 : pair + 1 + count, first_slab : first_slab + 8]
    rows = count * 128
    return jnp.concatenate([upper.reshape(rows, 128), lower.reshape(rows, 128)], axis=1)


def gelu_and_slope(hidden):
    square = hidden * hidden
    half = 0.5 * jnp.tanh(hidden * (CUBIC * square + SQRT_TWO_OVER_PI)) + 0.5
    active = hidden * half
    slope = half + active * (1.0 - half) * (6.0 * CUBIC * square + 2.0 * SQRT_TWO_OVER_PI)
    return active, slope


def place():
    return tuple(lax.axis_index(name) for name in ("frames", "half", "chip", "core"))


def lines_kernel(
    valid, kspace, line_mask, target, columns_table, permute, conv_mid, conv_in, conv_out, conv_bias,
    beside, other, far, mine_target, both, images, tiles,
):
    f, half, chip, core = place()
    quarter = chip * 2 + core
    sampled = line_mask[...].astype(F32)
    wide = jnp.concatenate([sampled, jnp.zeros((8, 112), F32)], axis=1)
    column = jnp.transpose(jnp.concatenate([wide, jnp.zeros((120, 128), F32)], axis=0))
    placed = pltpu.roll(wide, (half * 4 + quarter) * 16, 1)
    total = jnp.zeros((1, 128), F32)
    flags = []
    for batch in range(2):
        for frame in range(4):
            flag = jnp.zeros((1, 128), F32) + valid[batch, frame].astype(F32)
            flags.append(flag)
            total = total + flag
    for batch in range(2):
        shown = [[], []]
        sampled_lines = []
        for frame in range(4):
            at = batch * 4 + frame
            own = column[0:16, at : at + 1]
            lines = [kspace[batch, frame, pl.ds(part, 16, stride=2), :] * own for part in range(2)]
            sampled_lines.append(jnp.concatenate(lines, axis=1).astype(BF))
            for part in range(2):
                shown[part].append(target[batch, frame, pl.ds(part, 16, stride=2), :])
        both[batch, 0:64] = dot(jnp.concatenate(sampled_lines, axis=0), columns_table[...]).astype(BF)
        rows = [placed[batch * 4 : batch * 4 + 4]] + flags[batch * 4 : batch * 4 + 4] + [total, jnp.zeros((7, 128), F32)]
        both[batch, 64:80, 0:128] = jnp.concatenate(rows, axis=0).astype(BF)
        both[batch, 64:80, 128:256] = jnp.zeros((16, 128), BF)
        for part in range(2):
            image = jnp.concatenate(shown[part], axis=0).astype(BF)
            image = dot(image, permute[...]).astype(BF)
            for frame in range(4):
                images[batch, frame, :, part * 128 : part * 128 + 128] = image[frame * 16 : frame * 16 + 16]
    for step, to in ((1, beside), (2, other), (3, far)):
        batch = half if step == 1 else 1 - half
        to[0:80] = both[batch]
        for sibling in range(2):
            frame = jnp.bitwise_xor(quarter, (step % 2) * 2 + sibling)
            to[144 + sibling * 16 : 160 + sibling * 16] = images[batch, frame]
    for sibling in range(2):
        mine_target[sibling * 16 : sibling * 16 + 16] = images[half, jnp.bitwise_xor(quarter, sibling)]
    tiles[...] = jnp.zeros_like(tiles)
    for tile in range(13):
        tiles[tile] = conv_mid[:, tile * 128 : tile * 128 + 128]
    tiles[13, :, 0:64] = conv_mid[:, 1664:1728]
    for part in range(2):
        for piece in range(4):
            row = part * 4 + piece
            tiles[13, row : row + 1, 64:118] = conv_out[part : part + 1, piece * 54 : piece * 54 + 54]
    tiles[14] = conv_in[:, 0:128]
    tiles[15, :, 0:88] = conv_in[:, 128:216]
    wide = jnp.concatenate([conv_bias[...], jnp.zeros((2, 120), F32)], axis=1)
    wide = jnp.transpose(jnp.concatenate([wide, jnp.zeros((126, 128), F32)], axis=0))
    tiles[15, :, 88:90] = wide[0:8, 0:2]
    packed = tiles[...].reshape(128, 128).astype(BF)
    packed = jnp.concatenate([packed[0:64], packed[64:128]], axis=1)
    for to in (beside, other, far):
        to[80:144] = packed


def unpack_weights(own, other, whole):
    f, half, chip, core = place()
    for side, source in enumerate((own, other)):
        for slot in range(4):
            row = jnp.bitwise_xor(half * 4 + chip * 2 + core, slot * 2 + side)
            row = pl.multiple_of(row * 8, 8)
            values = source[slot * 64 : slot * 64 + 64].astype(F32)
            for part in range(2):
                half_of = values[:, part * 128 : part * 128 + 128].reshape(8, 8, 128)
                whole[part * 8 : part * 8 + 8, pl.ds(row, 8), :] = half_of


def unpack_last(whole, line, taps):
    for owner in range(8):
        for part in range(2):
            for piece in range(4):
                at = owner * 216 + piece * 54
                row = owner * 8 + part * 4 + piece
                line[part : part + 1, at : at + 54] = whole[13, row : row + 1, 64:118]
    taps[...] = jnp.zeros_like(taps)
    for tap in range(27):
        for part in range(2):
            row = tap * 2 + part
            taps[row : row + 1, 0:64] = line[part : part + 1, tap * 64 : tap * 64 + 64]
    return taps[...].astype(BF)[:, 0:64]


def forward_weight_kernel(own, other, pick_out, fwd_in, fwd_mid, fwd_out, bias, whole, line, taps):
    unpack_weights(own, other, whole)
    zero = jnp.zeros((64, 64), F32)
    turned = [jnp.transpose(whole[tile]) for tile in range(16)]

    def of_tap(time_off, row_off, col_off):
        tap = (time_off * 3 + row_off) * 3 + col_off
        return turned[tap // 2][(tap % 2) * 64 : (tap % 2) * 64 + 64]

    for time_off in range(4):
        for col_off in range(3):
            at = (time_off * 3 + col_off) * 256
            if time_off == 0:
                fwd_mid[at : at + 256, 128:256] = jnp.zeros((256, 128), BF)
            if time_off == 3:
                fwd_mid[at : at + 256, 0:128] = jnp.zeros((256, 128), BF)
    for time_off in range(3):
        for col_off in range(3):
            for level in range(4):
                left = of_tap(time_off, level, col_off) if level < 3 else zero
                right = of_tap(time_off, level - 1, col_off) if level > 0 else zero
                strip = jnp.concatenate([left, right], axis=1).astype(BF)
                for pair in range(2):
                    at = ((time_off + pair) * 3 + col_off) * 256 + level * 64
                    fwd_mid[at : at + 64, pair * 128 : pair * 128 + 128] = strip
    first = jnp.concatenate([turned[14], turned[15]], axis=0)
    fwd_in[...] = jnp.zeros_like(fwd_in)
    pad = jnp.zeros((8, 64), F32)
    for time_off in range(3):
        for col_off in range(3):
            three = []
            for row_off in range(3):
                tap = (time_off * 3 + row_off) * 3 + col_off
                three.append(first[tap * 8 : tap * 8 + 8, 0:64])
            left = jnp.concatenate(three + [pad], axis=0)
            right = jnp.concatenate([pad] + three, axis=0)
            strip = jnp.concatenate([left, right], axis=1).astype(BF)
            at = (time_off * 3 + col_off) * 128
            for pair in range(6):
                fwd_in[at + pair * 16 : at + pair * 16 + 32, pair * 128 : pair * 128 + 128] = strip
    bias[...] = jnp.zeros_like(bias)
    for layer in range(2):
        row = turned[15][88 + layer : 89 + layer, 0:64]
        row = jnp.concatenate([row, row], axis=1)
        for pair in range(6):
            bias[layer : layer + 1, pair * 128 : pair * 128 + 128] = row
    spread = dot_first(unpack_last(whole, line, taps), pick_out[...]).astype(BF)
    for row in range(10):
        fwd_out[row * 64 : row * 64 + 64, :] = spread[:, row * 256 : row * 256 + 256]


def backward_weight_kernel(own, other, pick_back, bwd_mid, bwd_out, whole, line, taps):
    unpack_weights(own, other, whole)
    zero = jnp.zeros((64, 64), F32)
    plain = [whole[tile] for tile in range(14)]

    def of_tap(time_off, row_off, col_off):
        tap = (time_off * 3 + row_off) * 3 + col_off
        return plain[tap // 2][:, (tap % 2) * 64 : (tap % 2) * 64 + 64]

    for time_off in range(4):
        for col_off in range(3):
            at = (time_off * 3 + col_off) * 256
            if time_off == 0:
                bwd_mid[at : at + 256, 128:256] = jnp.zeros((256, 128), BF)
            if time_off == 3:
                bwd_mid[at : at + 256, 0:128] = jnp.zeros((256, 128), BF)
    for time_off in range(3):
        for col_off in range(3):
            for level in range(4):
                left = of_tap(time_off, 2 - level, col_off) if level < 3 else zero
                right = of_tap(time_off, 3 - level, col_off) if level > 0 else zero
                strip = jnp.concatenate([left, right], axis=1).astype(BF)
                for pair in range(2):
                    at = ((2 + pair - time_off) * 3 + 2 - col_off) * 256 + level * 64
                    bwd_mid[at : at + 64, pair * 128 : pair * 128 + 128] = strip
    back = dot(pick_back[...], unpack_last(whole, line, taps)).astype(BF)
    for pair in range(5):
        at = pair * 2 * 288
        bwd_out[:, pair * 128 : pair * 128 + 128] = jnp.concatenate(
            [back[at : at + 288], back[at + 288 : at + 576]], axis=1
        )


def move(source, target, semaphores, at):
    copy = pltpu.make_async_copy(source, target, semaphores.at[at])
    copy.start()
    return copy


def forward_kernel(*refs):
    gathered, refs = refs[0:8], refs[8:]
    row_tables, fwd_in_hbm, fwd_mid_hbm, fwd_out, bias = refs[0:5]
    branch, stats, lines, natural, turned, active_out, slope_in, slope_out = refs[5:13]
    rows_table, fwd_in, fwd_mid, came = refs[13:17]
    spectrum, masks, seen, feature, active, hidden, hidden_other, second, second_other, taps = refs[17:]
    f, half, chip, core = place()
    quarter = chip * 2 + core
    block = f * 4 + quarter
    loads = [move(row_tables.at[block], rows_table, came, 0), move(fwd_in_hbm, fwd_in, came, 1)]
    spectrum[0:2] = jnp.zeros((2, 128, 256), BF)
    spectrum[18:20] = jnp.zeros((2, 128, 256), BF)
    feature[0] = jnp.zeros((10, 16, 128), BF)
    feature[17] = jnp.zeros((10, 16, 128), BF)
    active[0] = jnp.zeros((6, 10, 16, 128), BF)
    active[17] = jnp.zeros((6, 10, 16, 128), BF)
    turned[0] = jnp.zeros((128, 512), BF)
    turned[17] = jnp.zeros((128, 512), BF)
    taps[0] = jnp.zeros((144, 128), F32)
    taps[17] = jnp.zeros((144, 128), F32)
    total = jnp.zeros((1, 128), F32)
    masks[...] = jnp.zeros_like(masks)
    for at in range(8):
        side, which = at // 4, at % 4
        group = jnp.bitwise_xor(f, which)
        for chips_away in range(4):
            row = jnp.bitwise_xor(half * 4 + quarter, chips_away * 2 + side) * 16
            row = pl.multiple_of(row, 16)
            for frame in range(4):
                at_row = chips_away * 64 + frame * 16
                spectrum[2 + group * 4 + frame, pl.ds(row, 16), :] = gathered[at][at_row : at_row + 16]
        flags = gathered[at][256:272, 0:128].astype(F32)
        if side == 0:
            total = total + 0.25 * flags[8:9]
            masks[group] = masks[group] + flags[0:8]
        else:
            masks[group, 0:4] = masks[group, 0:4] + flags[0:4]
    seen[...] = jnp.zeros_like(seen)
    for group in range(4):
        seen[2 + group * 4 : 6 + group * 4] = masks[group, 0:4]
    stats[...] = jnp.zeros_like(stats)
    for part in range(2):
        stats[0:1, part * 128 : part * 128 + 128] = 1.0 - masks[f, pl.ds(quarter, 1), :]
    stats[1:2, 0:128] = total
    stats[2:3, 0:128] = 0.25 * masks[f, pl.ds(4 + quarter, 1), :]
    mine = spectrum[2 + block]
    lines[0:128] = mine[:, 0:128]
    lines[128:256] = mine[:, 128:256]
    sampled = seen[0:20]
    reach = [sampled[2:18]]
    reach.append(sampled[1:17] + sampled[2:18] + sampled[3:19])
    reach.append(reach[1] + sampled[0:16] + sampled[4:20])
    scales = [1.0 / jnp.maximum(count, 1.0) for count in reach]
    scales = [jnp.concatenate([scale, scale], axis=1) for scale in scales]

    loads[0].wait()
    channel = lax.rem(lax.broadcasted_iota(jnp.int32, (128, 256), 0), 8)
    table = rows_table[...].astype(F32)
    tables = [
        jnp.where(channel < 4, table, 0.0),
        jnp.where((channel == 4) | (channel == 5), table, 0.0),
        jnp.where(channel > 5, table, 0.0),
    ]
    for frame in range(16):
        near = [spectrum[frame + step].astype(F32) for step in range(5)]
        sums = [near[2]]
        sums.append(near[1] + near[2] + near[3])
        sums.append(sums[1] + near[0] + near[4])
        left = [(tables[radius] * scales[radius][frame : frame + 1]).astype(BF) for radius in range(3)]
        right = []
        for radius in range(3):
            value = sums[radius].astype(BF)
            right += [value[:, 0:128], value[:, 128:256]]
        image = dot(jnp.concatenate(left, axis=1), jnp.concatenate(right, axis=0))
        natural[frame] = image.astype(BF)

        def store(slabs, values, frame=frame):
            feature[frame + 1, slabs] = values

        put_slabs(store, jnp.transpose(image.astype(BF)).astype(F32))
    loads.append(move(fwd_mid_hbm, fwd_mid, came, 2))
    loads[1].wait()
    half_lane = lax.broadcasted_iota(jnp.int32, (1, 128), 1) // 64

    def finish_first(hidden, frame, pair, at):
        chunk = hidden[at : at + 128, pair * 128 : pair * 128 + 128]
        value, slope = gelu_and_slope(chunk + bias[0:1, pair * 128 : pair * 128 + 128])
        if pair in (0, 5):
            row = block * 8 - 2 + 2 * pair + half_lane
            value = jnp.where((row >= 0) & (row < 128), value, 0.0)
        else:
            at = (pair - 1) * 128
            slope_in[pl.ds(frame * 128, 128), at : at + 128] = slope.astype(BF)
            turned[frame + 1, :, at : at + 128] = jnp.transpose(value.astype(BF))

        def store(slabs, values):
            active[frame + 1, pair, slabs] = values

        put_slabs(store, value)

    def first_product(group):
        pieces = []
        for time_off in range(3):
            for col_off in range(3):
                piece = feature[group * 2 + time_off : group * 2 + time_off + 2, col_off : col_off + 8]
                pieces.append(piece.reshape(256, 128))
        return dot(jnp.concatenate(pieces, axis=1), fwd_in[...])

    def finish_frames(hidden, group):
        for step in range(2):
            for pair in range(6):
                finish_first(hidden, group * 2 + step, pair, step * 128)

    firsts = (hidden, hidden_other)
    hidden[...] = first_product(0)
    for group in range(1, 8):
        firsts[group % 2][...] = first_product(group)
        finish_frames(firsts[(group - 1) % 2], group - 1)
    finish_frames(firsts[1], 7)
    loads[2].wait()

    def finish_second(second, pair_of, pair, at):
        for side in range(2):
            chunk = second[at : at + 128, side * 128 : side * 128 + 128]
            value, slope = gelu_and_slope(chunk + bias[1:2, 0:128])
            if pair in (0, 4):
                row = block * 8 - 1 + 2 * pair + half_lane
                inside = (row >= 0) & (row < 128)
                value = jnp.where(inside, value, 0.0)
                slope = jnp.where(inside, slope, 0.0)
            row = (pair_of * 2 + side) * 128
            active_out[pl.ds(row, 128), pair * 128 : pair * 128 + 128] = value.astype(BF)
            slope_out[pl.ds(row, 128), pair * 128 : pair * 128 + 128] = slope.astype(BF)

    def finish_group(second, group):
        for pair in range(5):
            finish_second(second, group, pair, pair * 128)
        rows = pl.ds(group * 256, 256)
        made = dot(active_out[rows], fwd_out[...])
        for frame in range(2):
            taps[group * 2 + frame + 1] = jnp.transpose(made[frame * 128 : frame * 128 + 128])[0:144]

    def second_product(pair_of):
        pieces = []
        for step in range(4):
            for col_off in range(3):
                pieces.append(two_rows(active, pair_of * 2 + step, 0, 5, col_off))
        return dot(jnp.concatenate(pieces, axis=1), fwd_mid[...])

    seconds = (second, second_other)
    second[...] = second_product(0)
    for group in range(1, 8):
        seconds[group % 2][...] = second_product(group)
        finish_group(seconds[(group - 1) % 2], group - 1)
    finish_group(seconds[1], 7)
    for frame in range(16):
        columns = []
        for col_off in range(3):
            value = None
            for time_off in range(3):
                at = (time_off * 3 + col_off) * 16
                piece = taps[frame + time_off, at : at + 16]
                value = piece if value is None else value + piece
            columns.append(value)
        result = previous_column(columns[0]) + columns[1] + next_column(columns[2])
        branch[frame * 16 : frame * 16 + 16] = result.astype(BF)


def consistency_kernel(
    gathered, lines, stats, mine_target, beside, other, far, others, to_lines, to_rows, lines_again, spread, out, loss, target
):
    f, half, chip, core = place()
    for slot, source in enumerate((mine_target, beside, other, far)):
        at = 144 if slot else 0
        for side, image in enumerate((source[at : at + 16], others[256 + slot * 16 : 272 + slot * 16])):
            row = jnp.bitwise_xor(half * 4 + chip * 2 + core, slot * 2 + side) * 16
            row = pl.multiple_of(row, 16)
            for part in range(2):
                target[pl.ds(part * 128 + row, 16), :] = image[:, part * 128 : part * 128 + 128]
    weight = stats[2:3, 0:128]
    free = jnp.transpose(jnp.zeros((128, 128), F32) + stats[0:1, 0:128])
    free = jnp.concatenate([free, free], axis=0)
    wanted = target[...]
    made = dot(to_lines[...], gathered[...])
    wanted_spectrum = dot(lines_again[...], wanted)
    held = lines[...].astype(F32)
    kept = free * (made + held) + held
    grad = (free * (kept - wanted_spectrum) * (2.0 * weight)).astype(BF)
    out[...] = dot(spread[...], grad).astype(BF)
    residual = dot(to_rows[...], kept.astype(BF)) - wanted.astype(F32)
    loss[...] = jnp.zeros((8, 128), F32) + jnp.sum(residual * residual * weight)


def backward_kernel(
    grads, bwd_out_hbm, slope_out, active, turned, bwd_mid_hbm, slope_in, natural,
    out,
    bwd_out, bwd_mid, came,
    stack, product, product_other, grad_mid, grad_in, result, result_other, sum_mid, sum_out, sum_in, patches, tall, tiles, line,
):
    loads = [move(bwd_out_hbm, bwd_out, came, 0), move(bwd_mid_hbm, bwd_mid, came, 1)]
    zero32 = jnp.zeros((96, 128), BF)
    stack[0:96, 1920:2048] = zero32
    stack[192:288, 0:128] = zero32
    for frame in range(16):
        value = grads[frame * 32 : frame * 32 + 32].astype(F32)
        shifted = [next_column(value).astype(BF), value.astype(BF), previous_column(value).astype(BF)]
        for time_off in range(3):
            to = frame + time_off - 1
            if 0 <= to < 16:
                for col_off in range(3):
                    at = (time_off * 3 + col_off) * 32
                    stack[at : at + 32, to * 128 : to * 128 + 128] = shifted[col_off]
    grad_mid[0] = jnp.zeros((5, 10, 16, 128), BF)
    grad_mid[17] = jnp.zeros((5, 10, 16, 128), BF)
    tall[...] = jnp.zeros_like(tall)

    lane = lax.broadcasted_iota(jnp.int32, (1, 128), 1)
    bias_mid = jnp.zeros((1, 128), F32)
    buffers = (product, product_other)

    def finish_mid(buffer, group):
        own = jnp.zeros((1, 128), F32)
        for step in range(4):
            frame = group * 4 + step
            for pair in range(5):
                chunk = buffer[step * 128 : step * 128 + 128, pair * 128 : pair * 128 + 128]
                slope = slope_out[frame * 128 : frame * 128 + 128, pair * 128 : pair * 128 + 128]
                value = (chunk * slope.astype(F32)).astype(BF).astype(F32)
                added = jnp.sum(value, axis=0, keepdims=True)
                if pair == 0:
                    added = jnp.where(lane >= 64, added, 0.0)
                if pair == 4:
                    added = jnp.where(lane < 64, added, 0.0)
                own = own + added

                def store(slabs, values, frame=frame, pair=pair):
                    grad_mid[frame + 1, pair, slabs] = values

                put_slabs(store, value)
        return own

    loads[0].wait()
    groups = 16 // 4
    for group in range(groups + 1):
        if group < groups:
            at = group * 4 * 128
            buffers[group % 2][...] = dot_first(stack[:, at : at + 4 * 128], bwd_out[...])
        if group > 0:
            bias_mid = bias_mid + finish_mid(buffers[(group - 1) % 2], group - 1)

    made = dot(stack[...], active[...])
    for pair in range(5):
        sum_out[pair] = made[:, pair * 128 : pair * 128 + 128]
    for group in range(16 // 4):
        frames = [group * 4 + step for step in range(4)]
        left = jnp.concatenate([turned[frame : frame + 3].reshape(384, 512) for frame in frames], axis=1)
        right = []
        for col_off in range(3):
            right.append(jnp.concatenate([two_rows(grad_mid, frame + 1, 0, 4, 2 - col_off) for frame in frames], axis=0))
        made = dot(left, jnp.concatenate(right, axis=1))
        sum_mid[...] = made if group == 0 else sum_mid[...] + made

    def lay_out_mid(time_off, row_off):
        for col_off in range(3):
            tap = (time_off * 3 + row_off) * 3 + col_off
            at, lane = time_off * 128, col_off * 256
            upper = sum_mid[at : at + 64, lane + (2 - row_off) * 64 : lane + (2 - row_off) * 64 + 64]
            lower = sum_mid[at + 64 : at + 128, lane + (3 - row_off) * 64 : lane + (3 - row_off) * 64 + 64]
            tall[tap * 64 : tap * 64 + 64, 0:64] = upper + lower

    def lay_out_last():
        for row_off in range(3):
            value = None
            for row in range(2, 10):
                lane = (row - 2 + row_off) * 64
                piece = sum_out[lane // 128, pl.ds(row, 18, stride=16), :][:, lane % 128 : lane % 128 + 64]
                value = piece if value is None else value + piece
            for time_off in range(3):
                for col_off in range(3):
                    tap = (time_off * 3 + row_off) * 3 + col_off
                    for part in range(2):
                        row = (time_off * 3 + col_off) * 2 + part
                        line[part : part + 1, tap * 64 : tap * 64 + 64] = value[row : row + 1]

    def lay_out_pieces():
        for owner in range(8):
            for part in range(2):
                for piece in range(4):
                    at = owner * 216 + piece * 54
                    row = owner * 8 + part * 4 + piece
                    tiles[13, row : row + 1, 64:118] = line[part : part + 1, at : at + 54]

    def lay_out_patches(first, last):
        for frame in range(first, last):
            value = natural[frame].astype(F32)
            shifted = (previous_column(value).astype(BF), natural[frame], next_column(value).astype(BF))
            for col_off in range(3):
                for pair in range(4):
                    piece = shifted[col_off][pair * 16 + 16 : pair * 16 + 48]
                    for time_off in range(3):
                        to = frame - time_off + 1
                        if 0 <= to < 16:
                            at = (time_off * 3 + col_off) * 32
                            lane = (to * 4 + pair) * 128
                            patches[at : at + 32, lane : lane + 128] = piece

    def input_product(group):
        rows = []
        for half_of in range(2):
            pieces = []
            for step in range(4):
                for col_off in range(3):
                    pieces.append(two_rows(grad_mid, group * 4 + half_of * 2 + step, 0, 4, col_off))
            rows.append(jnp.concatenate(pieces, axis=1))
        return dot(jnp.concatenate(rows, axis=0), bwd_mid[...])

    def finish_input(buffer, group):
        own = jnp.zeros((1, 128), F32)
        for half_of in range(2):
            for pair in range(4):
                for side in range(2):
                    frame = group * 4 + half_of * 2 + side
                    at = half_of * 512 + pair * 128
                    chunk = buffer[at : at + 128, side * 128 : side * 128 + 128]
                    slope = slope_in[frame * 128 : frame * 128 + 128, pair * 128 : pair * 128 + 128]
                    value = (chunk * slope.astype(F32)).astype(BF)
                    grad_in[frame * 512 + pair * 128 : frame * 512 + pair * 128 + 128, :] = value
                    own = own + jnp.sum(value.astype(F32), axis=0, keepdims=True)
        return own

    loads[1].wait()
    patches[0:96, 0:512] = jnp.zeros((96, 512), BF)
    patches[192:288, 7680:8192] = jnp.zeros((96, 512), BF)
    results = (result, result_other)
    bias_in = jnp.zeros((1, 128), F32)
    for group in range(5):
        if group < 4:
            results[group % 2][...] = input_product(group)
        if group == 0:
            for time_off in range(3):
                lay_out_mid(time_off, 0)
            lay_out_last()
            lay_out_patches(0, 4)
        else:
            bias_in = bias_in + finish_input(results[(group - 1) % 2], group - 1)
        if group == 1:
            for time_off in range(3):
                lay_out_mid(time_off, 1)
            lay_out_patches(4, 10)
        if group == 2:
            for time_off in range(3):
                lay_out_mid(time_off, 2)
            lay_out_patches(10, 16)
        if group == 3:
            for tile in range(14):
                tiles[tile] = jnp.transpose(tall[tile * 128 : tile * 128 + 128])[0:64]
            lay_out_pieces()

    sum_in[...] = dot(patches[...], grad_in[...])
    for time_off in range(3):
        for row_off in range(3):
            for col_off in range(3):
                tap = (time_off * 3 + row_off) * 3 + col_off
                at = (time_off * 3 + col_off) * 32 + row_off * 8
                upper = sum_in[at : at + 8, 0:64]
                lower = sum_in[at + 8 : at + 16, 64:128]
                tall[1792 + tap * 8 : 1792 + tap * 8 + 8, 0:64] = upper + lower
    tall[2008:2009, 0:64] = bias_in[:, 0:64] + bias_in[:, 64:128]
    tall[2009:2010, 0:64] = bias_mid[:, 0:64] + bias_mid[:, 64:128]
    for tile in range(14, 16):
        tiles[tile] = jnp.transpose(tall[tile * 128 : tile * 128 + 128])[0:64]
    for quarter in range(4):
        for owner in range(8):
            value = tiles[quarter * 4 : quarter * 4 + 4, owner * 8 : owner * 8 + 8]
            out[quarter * 8 + owner] = value.reshape(32, 128).astype(BF)


def sum_kernel(parts, stats, loss, shard, shared):
    total = parts[0].astype(F32)
    for source in range(1, 32):
        total = total + parts[source].astype(F32)
    divisor = jnp.maximum(stats[1:2, 0:1] * (2.0 * 128 * 128), 1.0)
    total = total / divisor
    shard[...] = total
    lane = lax.broadcasted_iota(jnp.int32, (32, 128), 1)
    shared[...] = jnp.where(lane == 0, jnp.sum(total * total), loss[0:1] + jnp.zeros((32, 128), F32))


def update_kernel(
    own, near, mid, far, messages, stats,
    w_in, w_mid, w_out, w_bias, f_in, f_mid, f_out, f_bias, s_in, s_mid, s_out, s_bias,
    loss_sum, valid_count, grad_norm, mf_in, mf_mid, mf_out, mf_bias, ms_in, ms_mid, ms_out, ms_bias,
    mw_in, mw_mid, mw_out, mw_bias, mc_in, mc_mid, mc_out, mc_bias,
    shards, g_mid, g_in, g_out, g_bias,
):
    f, half, chip, core = place()
    for slot, source in enumerate((own, near, mid, far)):
        shards[jnp.bitwise_xor(f, slot)] = source[...]
    message = jnp.sum(messages[...], axis=0, keepdims=True)
    norm = jnp.sqrt(message[:, 0:1])
    loss_sum[0, 0] = jnp.sum(message[:, 1:2])
    valid_count[0, 0] = jnp.sum(stats[1:2, 0:1]) * (2.0 * 128 * 128)
    grad_norm[0, 0] = jnp.sum(norm)
    factor = jnp.minimum(1.0, CLIP / (norm + 1e-06))

    def tile_of(tile):
        at = (tile % 4) * 8
        return shards[tile // 4, at : at + 8]

    for tile in range(13):
        g_mid[:, tile * 128 : tile * 128 + 128] = tile_of(tile)
    mixed = tile_of(13)
    g_mid[:, 1664:1728] = mixed[:, 0:64]
    for part in range(2):
        for piece in range(4):
            row = part * 4 + piece
            g_out[part : part + 1, piece * 54 : piece * 54 + 54] = mixed[row : row + 1, 64:118]
    g_in[:, 0:128] = tile_of(14)
    mixed = tile_of(15)
    g_in[:, 128:216] = mixed[:, 0:88]
    square = jnp.concatenate([mixed, jnp.zeros((120, 128), F32)], axis=0)
    g_bias[...] = jnp.transpose(square)[88:90, 0:8]
    for grad, weight, one, two, new_one, new_two, new_weight, new_copy in (
        (g_in, w_in, f_in, s_in, mf_in, ms_in, mw_in, mc_in),
        (g_mid, w_mid, f_mid, s_mid, mf_mid, ms_mid, mw_mid, mc_mid),
        (g_out, w_out, f_out, s_out, mf_out, ms_out, mw_out, mc_out),
        (g_bias, w_bias, f_bias, s_bias, mf_bias, ms_bias, mw_bias, mc_bias),
    ):
        results = adamw(weight[...], grad[...] * factor, one[...], two[...])
        for ref, value in zip((new_one, new_two, new_weight, new_copy), results):
            ref[...] = value


VECTOR = pl.BlockSpec(memory_space=pltpu.VMEM)
SCALAR = pl.BlockSpec(memory_space=pltpu.SMEM)
LEFT = pl.BlockSpec(memory_space=pl.ANY)


def near(value):
    return pltpu.with_memory_space_constraint(value, pltpu.VMEM)


def shape(*dims, dtype=BF):
    return jax.ShapeDtypeStruct(dims, dtype)


def kernel_call(kernel, name, micros, megabytes, operands, results, scratch, in_specs=None, out_specs=None):
    return pl.pallas_call(
        kernel,
        name=name,
        out_shape=results,
        in_specs=in_specs or [VECTOR] * len(operands),
        out_specs=out_specs or [VECTOR] * len(results),
        scratch_shapes=scratch,
        cost_estimate=pl.CostEstimate(flops=int(micros * 1e9), bytes_accessed=0, transcendentals=0),
        compiler_params=pltpu.CompilerParams(vmem_limit_bytes=megabytes * 2**20),
    )(*operands)


def swap(value, axis, bit):
    return lax.ppermute(value, axis, [(i, i ^ bit) for i in range(lax.axis_size(axis))])


def by_rows(
    kspace, line_mask, valid_flags, target, conv_in, conv_mid, conv_out, conv_bias,
    first_in, first_mid, first_out, first_bias, second_in, second_mid, second_out, second_bias,
):
    tables = make_tables()

    mine, theirs, far, mine_target = kernel_call(
        lines_kernel,
        "prepare_lines",
        2,
        56,
        [
            valid_flags, kspace.reshape(2, 4, 32, 128), line_mask.reshape(8, 16), target.reshape(2, 4, 32, 128),
            tables["columns"], tables["permute"], conv_mid[0, 0].T, conv_in[0].T, conv_out[0], conv_bias[0],
        ],
        [shape(176, 256), shape(176, 256), shape(176, 256), shape(32, 256)],
        [pltpu.VMEM((2, 80, 256), BF), pltpu.VMEM((2, 4, 16, 256), BF), pltpu.VMEM((16, 8, 128), F32)],
        in_specs=[SCALAR] + [VECTOR] * 9,
    )

    sent = ((mine, 1), (theirs, 2), (far, 3))
    beside, other, far = (swap(value, ("half", "chip"), step) for value, step in sent)

    sources = (mine, beside, other, far)
    flags = mine[64:80] + beside[64:80] + other[64:80] + far[64:80]
    column = jnp.concatenate([source[0:64] for source in sources] + [flags], axis=0)
    gathered = [column] + [swap(column, "frames", step) for step in (1, 2, 3)]
    images = [mine_target, beside[144:176], other[144:176], far[144:176]]
    chips = jnp.concatenate([source[80:144] for source in sources] + [image[16:32] for image in images], axis=0)
    others = swap(chips, "core", 1)
    scratch = [pltpu.VMEM((16, 64, 128), F32), pltpu.VMEM((2, 1792), F32), pltpu.VMEM((64, 128), F32)]
    fwd_in, fwd_mid, fwd_out, bias = kernel_call(
        forward_weight_kernel,
        "lay_out_forward_weights",
        4,
        20,
        [near(chips), near(others), tables["pick_out"]],
        [shape(1152, 768), shape(3072, 256), shape(640, 256), shape(8, 768, dtype=F32)],
        scratch,
    )
    bwd_mid, bwd_out = kernel_call(
        backward_weight_kernel,
        "lay_out_backward_weights",
        3,
        16,
        [near(chips), near(others), tables["pick_back"]],
        [shape(3072, 256), shape(288, 640)],
        scratch,
    )
    *gathered, bias, bwd_out = lax.optimization_barrier((*gathered, bias, bwd_out))
    gathered += [swap(piece, "core", 1) for piece in gathered]
    kept = [(16, 128, 128), (18, 128, 512), (2048, 640), (2048, 512), (2048, 640)]
    moved = [(128, 256), (1152, 768), (3072, 256)]
    branch, stats, lines, natural, turned, active, slope_in, slope_out = kernel_call(
        forward_kernel,
        "features_and_branch",
        27,
        26,
        [*map(near, gathered), tables["feature"], fwd_in, fwd_mid, fwd_out, bias],
        [shape(256, 128), shape(8, 256, dtype=F32), shape(256, 128)] + [shape(*dims) for dims in kept],
        [pltpu.VMEM(dims, BF) for dims in moved]
        + [pltpu.SemaphoreType.DMA((3,))]
        + [
            pltpu.VMEM((20, 128, 256), BF),
            pltpu.VMEM((4, 8, 128), F32),
            pltpu.VMEM((24, 128), F32),
            pltpu.VMEM((18, 10, 16, 128), BF),
            pltpu.VMEM((18, 6, 10, 16, 128), BF),
            pltpu.VMEM((256, 768), F32),
            pltpu.VMEM((256, 768), F32),
            pltpu.VMEM((640, 256), F32),
            pltpu.VMEM((640, 256), F32),
            pltpu.VMEM((18, 144, 128), F32),
        ],
        in_specs=[VECTOR] * 8 + [LEFT] * 3 + [VECTOR] * 2,
    )
    by_frame = lax.all_to_all(branch.reshape(16, 16, 128), ("frames", "chip", "core"), 0, 0, tiled=True)
    grads, loss = kernel_call(
        consistency_kernel,
        "data_consistency",
        2.5,
        12,
        [
            near(by_frame.reshape(256, 128)), lines, stats, mine_target, beside, other, far, others,
            tables["to_lines"], tables["to_rows"], tables["lines_again"], tables["spread"],
        ],
        [shape(512, 128), shape(8, 128, dtype=F32)],
        [pltpu.VMEM((256, 128), BF)],
    )
    by_block = lax.all_to_all(grads.reshape(16, 32, 128), ("frames", "chip", "core"), 0, 0, tiled=True)
    moved = [(288, 640), (3072, 256)]
    (parts,) = kernel_call(
        backward_kernel,
        "weight_gradients",
        27,
        30,
        [near(by_block.reshape(512, 128)), bwd_out, slope_out, active, turned, bwd_mid, slope_in, natural],
        [shape(32, 32, 128)],
        [pltpu.VMEM(dims, BF) for dims in moved]
        + [pltpu.SemaphoreType.DMA((2,))]
        + [
            pltpu.VMEM((288, 2048), BF),
            pltpu.VMEM((512, 640), F32),
            pltpu.VMEM((512, 640), F32),
            pltpu.VMEM((18, 5, 10, 16, 128), BF),
            pltpu.VMEM((8192, 128), BF),
            pltpu.VMEM((1024, 256), F32),
            pltpu.VMEM((1024, 256), F32),
            pltpu.VMEM((384, 768), F32),
            pltpu.VMEM((5, 288, 128), F32),
            pltpu.VMEM((288, 128), F32),
            pltpu.VMEM((288, 8192), BF),
            pltpu.VMEM((2048, 128), F32),
            pltpu.VMEM((16, 64, 128), F32),
            pltpu.VMEM((2, 1792), F32),
        ],
        in_specs=[VECTOR, LEFT] + [VECTOR] * 3 + [LEFT] + [VECTOR] * 2,
    )
    parts = lax.all_to_all(parts, ("frames", "half", "chip", "core"), 0, 0, tiled=True)
    shard, messages = kernel_call(
        sum_kernel,
        "sum_gradients",
        2,
        8,
        [near(parts), stats, loss],
        [shape(32, 128, dtype=F32), shape(32, 128, dtype=F32)],
        [],
    )
    shards = [shard] + [swap(shard, "frames", step) for step in (1, 2, 3)]
    messages = lax.all_to_all(messages, ("frames", "half", "chip", "core"), 0, 0, tiled=True)
    groups = (
        (conv_in, conv_mid, conv_out, conv_bias),
        (first_in, first_mid, first_out, first_bias),
        (second_in, second_mid, second_out, second_bias),
    )
    state = []
    for of_in, of_mid, of_out, of_bias in groups:
        state += [of_in[0].T, of_mid[0, 0].T, of_out[0], of_bias[0]]
    shapes = [(8, 216), (8, 1728), (2, 216), (2, 8)]
    results = kernel_call(
        update_kernel,
        "adamw",
        2,
        8,
        [*map(near, shards), near(messages), stats, *state],
        [shape(1, 1, dtype=F32)] * 3
        + [shape(*dims, dtype=F32) for dims in shapes * 3]
        + [shape(*dims, dtype=BF) for dims in shapes],
        [pltpu.VMEM((4, 32, 128), F32)] + [pltpu.VMEM(shapes[at], F32) for at in (1, 0, 2, 3)],
        out_specs=[SCALAR] * 3 + [VECTOR] * 16,
    )
    outputs = [result[0, 0] for result in results[0:3]]
    for at in range(3, 19, 4):
        of_in, of_mid, of_out, of_bias = results[at : at + 4]
        outputs += [of_in.T[None], of_mid.T[None, None], of_out[None], of_bias[None]]
    return tuple(outputs)


def specs_for(rows):
    lines = P(None, "frames", rows)
    images = P(None, "frames", rows, None, None)
    weights = [P(None, None, rows), P(None, None, None, rows), P(None, None, rows), P(None, None, rows)]
    in_specs = (images, lines, P(None, "frames"), images, *(weights * 3))
    out_specs = (P(), P(), P(), *(weights * 4))
    return in_specs, out_specs


def solution(mesh):
    frames, rows = (mesh.shape[axis] for axis in ("frames", "rows"))
    if (frames, rows) != (4, 8):
        in_specs, out_specs = specs_for("rows")
        return jax.shard_map(local, mesh=mesh, in_specs=in_specs, out_specs=out_specs, check_vma=False)
    chips = Mesh(mesh.devices.reshape(frames, 2, rows // 4, 2), ("frames", "half", "chip", "core"))
    in_specs, out_specs = specs_for(("half", "chip", "core"))
    return jax.shard_map(by_rows, mesh=chips, in_specs=in_specs, out_specs=out_specs, check_vma=False)
```

```python
import jax
import jax.numpy as jnp
import ml_dtypes
import numpy as np
from jax import lax
from jax.experimental import pallas as pl
from jax.experimental.pallas import tpu as pltpu
from jax.sharding import Mesh
from jax.sharding import PartitionSpec as P

NX = 128
CAS = 1
MIDS = 1
STEP = 10


CLIP = 0.05
RATE = 0.03
BETA_ONE = 0.9
BETA_TWO = 0.999
EPSILON = 1e-08
DECAY = 0.01
HIGHEST = lax.Precision.HIGHEST


def with_halo(shard, sides, width):
    for axis, dim in sides:
        size, length = (lax.axis_size(axis), shard.shape[dim])
        up = [(i, (i + 1) % size) for i in range(size - 1)]
        down = [(j, i) for i, j in up]
        last = lax.slice_in_dim(shard, length - width, length, axis=dim)
        first = lax.slice_in_dim(shard, 0, width, axis=dim)
        before = lax.ppermute(last, axis, up)
        after = lax.ppermute(first, axis, down)
        shard = jnp.concatenate([before, shard, after], axis=dim)
    return shard


def from_behind(block, axis, distance):
    devices = range(lax.axis_size(axis))
    route = [(i - distance, i) for i in devices if i - distance in devices]
    return lax.ppermute(block, axis, route)


def dft_blocks(length, sign):
    counter = jnp.arange(length, dtype=jnp.int32)
    turns = counter[:, None] * counter[None, :] % length
    angle = turns.astype(jnp.float32) * (2.0 * jnp.pi / length)
    norm_factor = 1.0 / jnp.sqrt(jnp.float32(length))
    cosine = jnp.cos(angle) * norm_factor
    sine = sign * jnp.sin(angle) * norm_factor
    return jnp.stack([jnp.stack([cosine, -sine]), jnp.stack([sine, cosine])])


def transform(image, sign):
    rows_here = image.shape[1]
    rows_all = rows_here * lax.axis_size("rows")
    first_row = lax.axis_index("rows") * rows_here
    across = jnp.einsum(
        "byix,oikx->byok", image, dft_blocks(image.shape[3], sign), precision=HIGHEST
    )
    table = dft_blocks(rows_all, sign)
    window = lax.dynamic_slice(
        table, (0, 0, 0, first_row), (2, 2, lax.axis_size("rows") * rows_here, rows_here)
    )
    return lax.psum_scatter(
        jnp.einsum("byix,oiky->kbox", across, window, precision=HIGHEST),
        "rows",
        scatter_dimension=0,
        tiled=True,
    ).transpose(1, 0, 2, 3)


def taps(widened, offset, frames, rows_here, columns):
    time_off = offset // 3
    row_off = offset % 3
    return jnp.concatenate(
        [
            widened[
                time_off : time_off + frames,
                row_off : row_off + rows_here,
                :,
                col_off : col_off + columns,
            ]
            for col_off in range(3)
        ],
        axis=2,
    )


def convolve(padded, kernel):
    frames = padded.shape[0] - 2
    rows_here = padded.shape[1] - 2
    width_in = padded.shape[2]
    columns = padded.shape[3]
    widened = jnp.pad(padded, ((0, 0), (0, 0), (0, 0), (1, 1)))
    blocks = kernel.reshape(9, 3 * width_in, kernel.shape[1])
    summed = jnp.zeros((frames, rows_here, kernel.shape[1], columns), jnp.float32)
    for offset in range(9):
        gathered = taps(widened, offset, frames, rows_here, columns)
        summed = summed + jnp.einsum(
            "tykx,kj->tyjx", gathered, blocks[offset], preferred_element_type=jnp.float32
        )
    return summed


def kernel_grad(padded, grad_out):
    frames, rows_here, columns = (grad_out.shape[0], grad_out.shape[1], grad_out.shape[3])
    widened = jnp.pad(padded, ((0, 0), (0, 0), (0, 0), (1, 1)))
    pieces = [
        jnp.einsum(
            "tykx,tyjx->kj",
            taps(widened, offset, frames, rows_here, columns),
            grad_out,
            preferred_element_type=jnp.float32,
        )
        for offset in range(9)
    ]
    return jnp.concatenate(pieces, axis=0)


def flipped(kernel):
    width_in = kernel.shape[0] // 27
    shaped = kernel.reshape(3, 3, 3, width_in, kernel.shape[1])[::-1, ::-1, ::-1]
    return shaped.transpose(0, 1, 2, 4, 3).reshape(27 * kernel.shape[1], width_in)


def activation_rim(values):
    return with_halo(values, (("frames", 0), ("rows", 1)), 1)


def gradient_rim(values):
    return with_halo(values, (("frames", 0), ("rows", 1)), 1)


def layer_forward(inputs, kernel, bias_row):
    padded = activation_rim(inputs)
    return (padded, convolve(padded, kernel) + bias_row.astype(jnp.float32)[None, None, :, None])


def layer_backward(padded, kernel, grad_hidden, needs_input):
    kernel_delta = kernel_grad(padded, grad_hidden)
    bias_delta = jnp.sum(grad_hidden, axis=(0, 1, 3), dtype=jnp.float32)
    input_delta = None
    if needs_input:
        input_delta = convolve(gradient_rim(grad_hidden), flipped(kernel))
    return (kernel_delta, bias_delta, input_delta)


def share(measured, sampled):
    frames = measured.shape[0]
    reach = (frames + 1) // frames
    before = []
    after = []
    for distance in range(1, reach + 1):
        for direction in (1, -1):
            moved = from_behind((measured, sampled), "frames", direction * distance)
            if direction == 1:
                before.insert(0, moved)
            else:
                after.append(moved)
    data_line = jnp.concatenate(
        [moved_pair[0] for moved_pair in before]
        + [measured]
        + [moved_pair[0] for moved_pair in after],
        axis=0,
    )
    mask_line = jnp.concatenate(
        [moved_pair[1] for moved_pair in before]
        + [sampled]
        + [moved_pair[1] for moved_pair in after],
        axis=0,
    )
    centre = reach * frames
    windows = []
    for radius in range(3):
        data_sum = data_line[centre - radius : centre - radius + frames]
        mask_sum = mask_line[centre - radius : centre - radius + frames]
        for offset in range(1 - radius, radius + 1):
            data_sum = data_sum + data_line[centre + offset : centre + offset + frames]
            mask_sum = mask_sum + mask_line[centre + offset : centre + offset + frames]
        windows.append(data_sum / jnp.maximum(mask_sum, 1.0)[:, :, None, None])
    return jnp.stack(windows, 1)


def adamw(weight, grad_piece, moment_one, moment_two):
    first_new = BETA_ONE * moment_one + (1.0 - BETA_ONE) * grad_piece
    second_new = BETA_TWO * moment_two + (1.0 - BETA_TWO) * grad_piece * grad_piece
    ascent = (
        first_new
        / (1.0 - BETA_ONE**STEP)
        / (jnp.sqrt(second_new / (1.0 - BETA_TWO**STEP)) + EPSILON)
    )
    weight_new = weight - RATE * (ascent + DECAY * weight)
    return (first_new, second_new, weight_new, weight_new.astype(jnp.bfloat16))


def local(
    kspace,
    line_mask,
    valid_flags,
    target,
    conv_in,
    conv_mid,
    conv_out,
    conv_bias,
    first_in,
    first_mid,
    first_out,
    first_bias,
    second_in,
    second_mid,
    second_out,
    second_bias,
):
    masters = (conv_in, conv_mid, conv_out, conv_bias)

    def reduce_grads(grads):
        shards = (
            lax.psum_scatter(
                grads[0].astype(jnp.bfloat16), "rows", scatter_dimension=2, tiled=True
            ).astype(jnp.float32),
            lax.psum_scatter(
                grads[1].astype(jnp.bfloat16), "rows", scatter_dimension=3, tiled=True
            ).astype(jnp.float32),
            lax.psum_scatter(
                grads[2].astype(jnp.bfloat16), "rows", scatter_dimension=2, tiled=True
            ).astype(jnp.float32),
            lax.psum_scatter(
                grads[3].astype(jnp.bfloat16), "rows", scatter_dimension=2, tiled=True
            ).astype(jnp.float32),
        )
        return lax.psum((shards[0], shards[1], shards[2], shards[3]), "frames")

    def micro_batch(carry, batch_data):
        grad_carry, loss_carry, count_carry = carry
        measured_full, mask_rows, frame_flags, wanted = batch_data
        full_in, full_mid, full_out, full_bias = (
            lax.all_gather(conv_in.astype(jnp.bfloat16), "rows", axis=2, tiled=True),
            lax.all_gather(conv_mid.astype(jnp.bfloat16), "rows", axis=3, tiled=True),
            lax.all_gather(conv_out.astype(jnp.bfloat16), "rows", axis=2, tiled=True),
            lax.all_gather(conv_bias.astype(jnp.bfloat16), "rows", axis=2, tiled=True),
        )
        sampled = mask_rows.astype(jnp.float32)
        measured = measured_full * sampled[:, :, None, None]
        shared = share(measured, sampled)
        frames, rows_here = (measured.shape[0], measured.shape[1])
        images = transform(shared.reshape(frames * 3, rows_here, 2, NX), 1.0).reshape(
            frames, 3, rows_here, 2, NX
        )
        shared_images = images.transpose(0, 2, 1, 3, 4).reshape(frames, rows_here, 6, NX)
        current = images[:, 0]
        unsampled = (1.0 - sampled)[:, :, None, None]
        no_bias = jnp.zeros((2,), jnp.bfloat16)

        def kernels_of(cascade):
            return [full_in[cascade]] + [full_mid[cascade, 0]] + [full_out[cascade].T]

        cascade = 0
        kernels = kernels_of(cascade)
        biases = [full_bias[cascade, layer_at] for layer_at in range(MIDS + 1)] + [no_bias]
        inputs = jnp.concatenate([current, shared_images], axis=2).astype(jnp.bfloat16)
        saved = []
        for layer_at in range(MIDS + 2):
            padded, hidden = layer_forward(inputs, kernels[layer_at], biases[layer_at])
            saved.append((padded, hidden))
            if layer_at < MIDS + 1:
                inputs = jax.nn.gelu(hidden).astype(jnp.bfloat16)
        current = transform(unsampled * transform(current + hidden, -1.0) + measured, 1.0)
        kept = [saved]
        frame_weight = frame_flags.astype(jnp.float32)[:, None, None, None]
        residual_error = current - wanted
        loss_part = jnp.sum(frame_weight * residual_error * residual_error)
        count_part = 2.0 * rows_here * NX * jnp.sum(frame_flags.astype(jnp.float32))
        grad_current = 2.0 * frame_weight * residual_error
        delta_in = [None] * CAS
        delta_mid = [None] * CAS
        delta_out = [None] * CAS
        delta_bias = [None] * CAS
        for cascade in reversed(range(CAS)):
            kernels = kernels_of(cascade)
            grad_sum = transform(unsampled * transform(grad_current, -1.0), 1.0)
            grad_hidden = grad_sum.astype(jnp.bfloat16)
            kernel_deltas = [None] * (MIDS + 2)
            bias_deltas = [None] * (MIDS + 2)
            grad_input = None
            for layer_at in reversed(range(MIDS + 2)):
                padded, hidden = kept[cascade][layer_at]
                if layer_at < MIDS + 1:
                    pullback = jax.vjp(jax.nn.gelu, hidden)[1]
                    grad_hidden = pullback(grad_input)[0].astype(jnp.bfloat16)
                needs_input = cascade > 0 or layer_at > 0
                kernel_deltas[layer_at], bias_deltas[layer_at], grad_input = layer_backward(
                    padded, kernels[layer_at], grad_hidden, needs_input
                )
            delta_in[cascade] = kernel_deltas[0]
            delta_mid[cascade] = jnp.stack(kernel_deltas[1 : MIDS + 1])
            delta_out[cascade] = kernel_deltas[MIDS + 1].T
            delta_bias[cascade] = jnp.stack(bias_deltas[0 : MIDS + 1])
        grads = (
            jnp.stack(delta_in),
            jnp.stack(delta_mid),
            jnp.stack(delta_out),
            jnp.stack(delta_bias),
        )
        grads = reduce_grads(grads)
        grad_carry = jax.tree.map(jnp.add, grad_carry, grads)
        return ((grad_carry, loss_carry + loss_part, count_carry + count_part), None)

    start_grads = jax.tree.map(jnp.zeros_like, masters)
    start = (start_grads, jnp.zeros((), jnp.float32), jnp.zeros((), jnp.float32))
    (summed, loss_local, count_local), unused = lax.scan(
        micro_batch, start, (kspace, line_mask, valid_flags, target)
    )
    summed = tuple(summed)
    loss_sum, valid_count = lax.psum((loss_local, count_local), ("frames", "rows"))
    divisor = jnp.maximum(valid_count, 1.0)
    grads = [grad_piece / divisor for grad_piece in summed]
    squares = sum((jnp.sum(grad_piece * grad_piece) for grad_piece in grads))
    grad_norm = jnp.sqrt(lax.psum(squares, "rows"))
    factor = jnp.minimum(1.0, CLIP / (grad_norm + 1e-06))
    firsts = (first_in, first_mid, first_out, first_bias)
    seconds = (second_in, second_mid, second_out, second_bias)
    results = [
        adamw(masters[which], grads[which] * factor, firsts[which], seconds[which])
        for which in range(4)
    ]
    return (
        loss_sum,
        valid_count,
        grad_norm,
        results[0][0],
        results[1][0],
        results[2][0],
        results[3][0],
        results[0][1],
        results[1][1],
        results[2][1],
        results[3][1],
        results[0][2],
        results[1][2],
        results[2][2],
        results[3][2],
        results[0][3],
        results[1][3],
        results[2][3],
        results[3][3],
    )


BF = jnp.bfloat16
F32 = jnp.float32
SQRT_TWO_OVER_PI = 0.7978845608028654
CUBIC = 0.044715 * SQRT_TWO_OVER_PI
UNITS = 16


def column_order():
    lanes = np.arange(128)
    return (lanes % 16) * 8 + lanes // 16


def dft_tables(sign):
    counter = np.arange(128)
    angle = (counter[:, None] * counter[None, :] % 128) * (2.0 * np.pi / 128)
    cosine, sine = np.cos(angle) / np.sqrt(128.0), sign * np.sin(angle) / np.sqrt(128.0)
    return np.stack([np.stack([cosine, -sine]), np.stack([sine, cosine])])


def make_tables():
    inverse, forward = dft_tables(1.0), dft_tables(-1.0)
    order = column_order()
    columns = inverse[:, :, :, order].transpose(1, 2, 0, 3).reshape(256, 256)
    blocks = np.arange(UNITS)[:, None] * 8

    def rows_of(first, kept):
        rows = blocks + first + np.arange(16)[None, :]
        inside = (rows >= 0) & (rows < 128) & (np.arange(16)[None, :] < kept)
        return np.clip(rows, 0, 127), inside

    rows, inside = rows_of(-3, 14)
    feature = inverse[:, :, rows, :] * inside[None, None, :, :, None]
    feature = feature.transpose(2, 3, 0, 1, 4).reshape(UNITS, 16, 2, 256)
    feature = np.tile(feature, (1, 1, 4, 1)).reshape(UNITS, 128, 256)
    to_lines = forward.reshape(2, 2, 128, UNITS, 8).transpose(0, 2, 3, 1, 4).reshape(256, 256)
    to_rows = inverse.transpose(0, 2, 1, 3).reshape(256, 256)
    lines_again = forward.transpose(0, 2, 1, 3).reshape(256, 256)
    rows, inside = rows_of(-2, 12)
    spread = inverse[:, :, rows, :] * inside[None, None, :, :, None]
    spread = spread.transpose(2, 0, 3, 1, 4).reshape(UNITS * 32, 256)
    permute = np.zeros((128, 128))
    permute[order, np.arange(128)] = 1.0
    pick_out = np.zeros((64, 10, 256))
    pick_back = np.zeros((10, 288, 64))
    for time_off in range(3):
        for row_off in range(3):
            for col_off in range(3):
                tap = (time_off * 3 + row_off) * 3 + col_off
                for part in range(2):
                    for row in range(8):
                        lane = (time_off * 3 + col_off) * 16 + part * 8 + row
                        pick_out[tap * 2 + part, row + row_off, lane] = 1.0
                    for row in range(12):
                        into = row + row_off - 2
                        if 0 <= into < 10:
                            at = (time_off * 3 + col_off) * 32 + part * 16 + row
                            pick_back[into, at, tap * 2 + part] = 1.0
    made = dict(
        columns=columns,
        feature=feature,
        to_lines=to_lines,
        lines_again=lines_again,
        to_rows=to_rows,
        spread=spread,
        permute=permute,
        pick_out=pick_out.reshape(64, 2560),
        pick_back=pick_back.reshape(2880, 64),
    )
    return {name: jnp.asarray(table.astype(ml_dtypes.bfloat16)) for name, table in made.items()}


def dot(left, right):
    return jnp.dot(left, right, preferred_element_type=F32)


def dot_first(left, right):
    return lax.dot_general(left, right, (((0,), (0,)), ((), ())), preferred_element_type=F32)


def next_column(values):
    lane = lax.broadcasted_iota(jnp.int32, values.shape, 1)
    inner = pltpu.roll(values, 112, 1)
    wrapped = jnp.where(lane == 127, 0.0, pltpu.roll(values, 111, 1))
    return jnp.where(lane < 112, inner, wrapped)


def previous_column(values):
    lane = lax.broadcasted_iota(jnp.int32, values.shape, 1)
    inner = pltpu.roll(values, 16, 1)
    wrapped = jnp.where(lane == 0, 0.0, pltpu.roll(values, 17, 1))
    return jnp.where(lane >= 16, inner, wrapped)


def put_slabs(store, values):
    store(slice(1, 9), values.astype(BF).reshape(8, 16, 128))
    first, last = values[0:16], values[112:128]
    at = lax.broadcasted_iota(jnp.int32, (16, 128), 0)
    before = jnp.where(at == 0, 0.0, pltpu.roll(last, 1, 0))
    after = jnp.where(at == 15, 0.0, pltpu.roll(first, 15, 0))
    store(slice(0, 1), before.astype(BF).reshape(1, 16, 128))
    store(slice(9, 10), after.astype(BF).reshape(1, 16, 128))


def two_rows(ref, frame, pair, count, first_slab):
    upper = ref[frame, pair : pair + count, first_slab : first_slab + 8]
    lower = ref[frame, pair + 1 : pair + 1 + count, first_slab : first_slab + 8]
    rows = count * 128
    return jnp.concatenate([upper.reshape(rows, 128), lower.reshape(rows, 128)], axis=1)


def gelu_and_slope(hidden):
    square = hidden * hidden
    half = 0.5 * jnp.tanh(hidden * (CUBIC * square + SQRT_TWO_OVER_PI)) + 0.5
    active = hidden * half
    slope = half + active * (1.0 - half) * (6.0 * CUBIC * square + 2.0 * SQRT_TWO_OVER_PI)
    return active, slope


def place():
    return tuple(lax.axis_index(name) for name in ("frames", "half", "chip", "core"))


def lines_kernel(
    valid, kspace, line_mask, target, columns_table, permute, conv_mid, conv_in, conv_out, conv_bias,
    beside, other, far, mine_target, both, images, tiles,
):
    f, half, chip, core = place()
    quarter = chip * 2 + core
    sampled = line_mask[...].astype(F32)
    wide = jnp.concatenate([sampled, jnp.zeros((8, 112), F32)], axis=1)
    column = jnp.transpose(jnp.concatenate([wide, jnp.zeros((120, 128), F32)], axis=0))
    placed = pltpu.roll(wide, (half * 4 + quarter) * 16, 1)
    total = jnp.zeros((1, 128), F32)
    flags = []
    for batch in range(2):
        for frame in range(4):
            flag = jnp.zeros((1, 128), F32) + valid[batch, frame].astype(F32)
            flags.append(flag)
            total = total + flag
    for batch in range(2):
        shown = [[], []]
        sampled_lines = []
        for frame in range(4):
            at = batch * 4 + frame
            own = column[0:16, at : at + 1]
            lines = [kspace[batch, frame, pl.ds(part, 16, stride=2), :] * own for part in range(2)]
            sampled_lines.append(jnp.concatenate(lines, axis=1).astype(BF))
            for part in range(2):
                shown[part].append(target[batch, frame, pl.ds(part, 16, stride=2), :])
        both[batch, 0:64] = dot(jnp.concatenate(sampled_lines, axis=0), columns_table[...]).astype(BF)
        rows = [placed[batch * 4 : batch * 4 + 4]] + flags[batch * 4 : batch * 4 + 4] + [total, jnp.zeros((7, 128), F32)]
        both[batch, 64:80, 0:128] = jnp.concatenate(rows, axis=0).astype(BF)
        both[batch, 64:80, 128:256] = jnp.zeros((16, 128), BF)
        for part in range(2):
            image = jnp.concatenate(shown[part], axis=0).astype(BF)
            image = dot(image, permute[...]).astype(BF)
            for frame in range(4):
                images[batch, frame, :, part * 128 : part * 128 + 128] = image[frame * 16 : frame * 16 + 16]
    for step, to in ((1, beside), (2, other), (3, far)):
        batch = half if step == 1 else 1 - half
        to[0:80] = both[batch]
        for sibling in range(2):
            frame = jnp.bitwise_xor(quarter, (step % 2) * 2 + sibling)
            to[144 + sibling * 16 : 160 + sibling * 16] = images[batch, frame]
    for sibling in range(2):
        mine_target[sibling * 16 : sibling * 16 + 16] = images[half, jnp.bitwise_xor(quarter, sibling)]
    tiles[...] = jnp.zeros_like(tiles)
    for tile in range(13):
        tiles[tile] = conv_mid[:, tile * 128 : tile * 128 + 128]
    tiles[13, :, 0:64] = conv_mid[:, 1664:1728]
    for part in range(2):
        for piece in range(4):
            row = part * 4 + piece
            tiles[13, row : row + 1, 64:118] = conv_out[part : part + 1, piece * 54 : piece * 54 + 54]
    tiles[14] = conv_in[:, 0:128]
    tiles[15, :, 0:88] = conv_in[:, 128:216]
    wide = jnp.concatenate([conv_bias[...], jnp.zeros((2, 120), F32)], axis=1)
    wide = jnp.transpose(jnp.concatenate([wide, jnp.zeros((126, 128), F32)], axis=0))
    tiles[15, :, 88:90] = wide[0:8, 0:2]
    packed = tiles[...].reshape(128, 128).astype(BF)
    packed = jnp.concatenate([packed[0:64], packed[64:128]], axis=1)
    for to in (beside, other, far):
        to[80:144] = packed


def merge_kernel(mine, beside, other, far, mine_target, column, chips):
    flags = jnp.zeros((16, 256), F32)
    for slot, source in enumerate((mine, beside, other, far)):
        column[slot * 64 : slot * 64 + 64] = source[0:64]
        flags = flags + source[64:80].astype(F32)
        chips[slot * 64 : slot * 64 + 64] = source[80:144]
        image = source[160:176] if slot else mine_target[16:32]
        chips[256 + slot * 16 : 272 + slot * 16] = image
    column[256:272] = flags.astype(BF)


def unpack_weights(own, other, whole):
    f, half, chip, core = place()
    for side, source in enumerate((own, other)):
        for slot in range(4):
            row = jnp.bitwise_xor(half * 4 + chip * 2 + core, slot * 2 + side)
            row = pl.multiple_of(row * 8, 8)
            values = source[slot * 64 : slot * 64 + 64].astype(F32)
            for part in range(2):
                half_of = values[:, part * 128 : part * 128 + 128].reshape(8, 8, 128)
                whole[part * 8 : part * 8 + 8, pl.ds(row, 8), :] = half_of


def unpack_last(whole, line, taps):
    for owner in range(8):
        for part in range(2):
            for piece in range(4):
                at = owner * 216 + piece * 54
                row = owner * 8 + part * 4 + piece
                line[part : part + 1, at : at + 54] = whole[13, row : row + 1, 64:118]
    taps[...] = jnp.zeros_like(taps)
    for tap in range(27):
        for part in range(2):
            row = tap * 2 + part
            taps[row : row + 1, 0:64] = line[part : part + 1, tap * 64 : tap * 64 + 64]
    return taps[...].astype(BF)[:, 0:64]


def forward_weight_kernel(own, other, pick_out, fwd_in, fwd_mid, fwd_out, bias, whole, line, taps):
    unpack_weights(own, other, whole)
    zero = jnp.zeros((64, 64), F32)
    turned = [jnp.transpose(whole[tile]) for tile in range(16)]

    def of_tap(time_off, row_off, col_off):
        tap = (time_off * 3 + row_off) * 3 + col_off
        return turned[tap // 2][(tap % 2) * 64 : (tap % 2) * 64 + 64]

    for time_off in range(4):
        for col_off in range(3):
            at = (time_off * 3 + col_off) * 256
            if time_off == 0:
                fwd_mid[at : at + 256, 128:256] = jnp.zeros((256, 128), BF)
            if time_off == 3:
                fwd_mid[at : at + 256, 0:128] = jnp.zeros((256, 128), BF)
    for time_off in range(3):
        for col_off in range(3):
            for level in range(4):
                left = of_tap(time_off, level, col_off) if level < 3 else zero
                right = of_tap(time_off, level - 1, col_off) if level > 0 else zero
                strip = jnp.concatenate([left, right], axis=1).astype(BF)
                for pair in range(2):
                    at = ((time_off + pair) * 3 + col_off) * 256 + level * 64
                    fwd_mid[at : at + 64, pair * 128 : pair * 128 + 128] = strip
    first = jnp.concatenate([turned[14], turned[15]], axis=0)
    fwd_in[...] = jnp.zeros_like(fwd_in)
    pad = jnp.zeros((8, 64), F32)
    for time_off in range(3):
        for col_off in range(3):
            three = []
            for row_off in range(3):
                tap = (time_off * 3 + row_off) * 3 + col_off
                three.append(first[tap * 8 : tap * 8 + 8, 0:64])
            left = jnp.concatenate(three + [pad], axis=0)
            right = jnp.concatenate([pad] + three, axis=0)
            strip = jnp.concatenate([left, right], axis=1).astype(BF)
            at = (time_off * 3 + col_off) * 128
            for pair in range(6):
                fwd_in[at + pair * 16 : at + pair * 16 + 32, pair * 128 : pair * 128 + 128] = strip
    bias[...] = jnp.zeros_like(bias)
    for layer in range(2):
        row = turned[15][88 + layer : 89 + layer, 0:64]
        row = jnp.concatenate([row, row], axis=1)
        for pair in range(6):
            bias[layer : layer + 1, pair * 128 : pair * 128 + 128] = row
    spread = dot_first(unpack_last(whole, line, taps), pick_out[...]).astype(BF)
    for row in range(10):
        fwd_out[row * 64 : row * 64 + 64, :] = spread[:, row * 256 : row * 256 + 256]


def backward_weight_kernel(own, other, pick_back, bwd_mid, bwd_out, whole, line, taps):
    unpack_weights(own, other, whole)
    zero = jnp.zeros((64, 64), F32)
    plain = [whole[tile] for tile in range(14)]

    def of_tap(time_off, row_off, col_off):
        tap = (time_off * 3 + row_off) * 3 + col_off
        return plain[tap // 2][:, (tap % 2) * 64 : (tap % 2) * 64 + 64]

    for time_off in range(4):
        for col_off in range(3):
            at = (time_off * 3 + col_off) * 256
            if time_off == 0:
                bwd_mid[at : at + 256, 128:256] = jnp.zeros((256, 128), BF)
            if time_off == 3:
                bwd_mid[at : at + 256, 0:128] = jnp.zeros((256, 128), BF)
    for time_off in range(3):
        for col_off in range(3):
            for level in range(4):
                left = of_tap(time_off, 2 - level, col_off) if level < 3 else zero
                right = of_tap(time_off, 3 - level, col_off) if level > 0 else zero
                strip = jnp.concatenate([left, right], axis=1).astype(BF)
                for pair in range(2):
                    at = ((2 + pair - time_off) * 3 + 2 - col_off) * 256 + level * 64
                    bwd_mid[at : at + 64, pair * 128 : pair * 128 + 128] = strip
    back = dot(pick_back[...], unpack_last(whole, line, taps)).astype(BF)
    for pair in range(5):
        at = pair * 2 * 288
        bwd_out[:, pair * 128 : pair * 128 + 128] = jnp.concatenate(
            [back[at : at + 288], back[at + 288 : at + 576]], axis=1
        )


def move(source, target, semaphores, at):
    copy = pltpu.make_async_copy(source, target, semaphores.at[at])
    copy.start()
    return copy


def forward_kernel(*refs):
    gathered, refs = refs[0:8], refs[8:]
    row_tables, fwd_in_hbm, fwd_mid_hbm, fwd_out, bias = refs[0:5]
    branch, stats, lines, natural, turned, active_out, slope_in, slope_out = refs[5:13]
    rows_table, fwd_in, fwd_mid, came = refs[13:17]
    spectrum, masks, seen, feature, active, hidden, hidden_other, second, second_other, taps = refs[17:]
    f, half, chip, core = place()
    quarter = chip * 2 + core
    block = f * 4 + quarter
    loads = [move(row_tables.at[block], rows_table, came, 0), move(fwd_in_hbm, fwd_in, came, 1)]
    spectrum[0:2] = jnp.zeros((2, 128, 256), BF)
    spectrum[18:20] = jnp.zeros((2, 128, 256), BF)
    feature[0] = jnp.zeros((10, 16, 128), BF)
    feature[17] = jnp.zeros((10, 16, 128), BF)
    active[0] = jnp.zeros((6, 10, 16, 128), BF)
    active[17] = jnp.zeros((6, 10, 16, 128), BF)
    turned[0] = jnp.zeros((128, 512), BF)
    turned[17] = jnp.zeros((128, 512), BF)
    taps[0] = jnp.zeros((144, 128), F32)
    taps[17] = jnp.zeros((144, 128), F32)
    total = jnp.zeros((1, 128), F32)
    masks[...] = jnp.zeros_like(masks)
    for at in range(8):
        side, which = at // 4, at % 4
        group = jnp.bitwise_xor(f, which)
        for chips_away in range(4):
            row = jnp.bitwise_xor(half * 4 + quarter, chips_away * 2 + side) * 16
            row = pl.multiple_of(row, 16)
            for frame in range(4):
                at_row = chips_away * 64 + frame * 16
                spectrum[2 + group * 4 + frame, pl.ds(row, 16), :] = gathered[at][at_row : at_row + 16]
        flags = gathered[at][256:272, 0:128].astype(F32)
        if side == 0:
            total = total + 0.25 * flags[8:9]
            masks[group] = masks[group] + flags[0:8]
        else:
            masks[group, 0:4] = masks[group, 0:4] + flags[0:4]
    seen[...] = jnp.zeros_like(seen)
    for group in range(4):
        seen[2 + group * 4 : 6 + group * 4] = masks[group, 0:4]
    stats[...] = jnp.zeros_like(stats)
    for part in range(2):
        stats[0:1, part * 128 : part * 128 + 128] = 1.0 - masks[f, pl.ds(quarter, 1), :]
    stats[1:2, 0:128] = total
    stats[2:3, 0:128] = 0.25 * masks[f, pl.ds(4 + quarter, 1), :]
    mine = spectrum[2 + block]
    lines[0:128] = mine[:, 0:128]
    lines[128:256] = mine[:, 128:256]
    sampled = seen[0:20]
    reach = [sampled[2:18]]
    reach.append(sampled[1:17] + sampled[2:18] + sampled[3:19])
    reach.append(reach[1] + sampled[0:16] + sampled[4:20])
    scales = [1.0 / jnp.maximum(count, 1.0) for count in reach]
    scales = [jnp.concatenate([scale, scale], axis=1) for scale in scales]

    loads[0].wait()
    channel = lax.rem(lax.broadcasted_iota(jnp.int32, (128, 256), 0), 8)
    table = rows_table[...].astype(F32)
    tables = [
        jnp.where(channel < 4, table, 0.0),
        jnp.where((channel == 4) | (channel == 5), table, 0.0),
        jnp.where(channel > 5, table, 0.0),
    ]
    for frame in range(16):
        near = [spectrum[frame + step].astype(F32) for step in range(5)]
        sums = [near[2]]
        sums.append(near[1] + near[2] + near[3])
        sums.append(sums[1] + near[0] + near[4])
        left = [(tables[radius] * scales[radius][frame : frame + 1]).astype(BF) for radius in range(3)]
        right = []
        for radius in range(3):
            value = sums[radius].astype(BF)
            right += [value[:, 0:128], value[:, 128:256]]
        image = dot(jnp.concatenate(left, axis=1), jnp.concatenate(right, axis=0))
        natural[frame] = image.astype(BF)

        def store(slabs, values, frame=frame):
            feature[frame + 1, slabs] = values

        put_slabs(store, jnp.transpose(image.astype(BF)).astype(F32))
    loads.append(move(fwd_mid_hbm, fwd_mid, came, 2))
    loads[1].wait()
    half_lane = lax.broadcasted_iota(jnp.int32, (1, 128), 1) // 64

    def finish_first(hidden, frame, pair, at):
        chunk = hidden[at : at + 128, pair * 128 : pair * 128 + 128]
        value, slope = gelu_and_slope(chunk + bias[0:1, pair * 128 : pair * 128 + 128])
        if pair in (0, 5):
            row = block * 8 - 2 + 2 * pair + half_lane
            value = jnp.where((row >= 0) & (row < 128), value, 0.0)
        else:
            at = (pair - 1) * 128
            slope_in[pl.ds(frame * 128, 128), at : at + 128] = slope.astype(BF)
            turned[frame + 1, :, at : at + 128] = jnp.transpose(value.astype(BF))

        def store(slabs, values):
            active[frame + 1, pair, slabs] = values

        put_slabs(store, value)

    def first_product(group):
        pieces = []
        for time_off in range(3):
            for col_off in range(3):
                piece = feature[group * 2 + time_off : group * 2 + time_off + 2, col_off : col_off + 8]
                pieces.append(piece.reshape(256, 128))
        return dot(jnp.concatenate(pieces, axis=1), fwd_in[...])

    def finish_frames(hidden, group):
        for step in range(2):
            for pair in range(6):
                finish_first(hidden, group * 2 + step, pair, step * 128)

    firsts = (hidden, hidden_other)
    hidden[...] = first_product(0)
    for group in range(1, 8):
        firsts[group % 2][...] = first_product(group)
        finish_frames(firsts[(group - 1) % 2], group - 1)
    finish_frames(firsts[1], 7)
    loads[2].wait()

    def finish_second(second, pair_of, pair, at):
        for side in range(2):
            chunk = second[at : at + 128, side * 128 : side * 128 + 128]
            value, slope = gelu_and_slope(chunk + bias[1:2, 0:128])
            if pair in (0, 4):
                row = block * 8 - 1 + 2 * pair + half_lane
                inside = (row >= 0) & (row < 128)
                value = jnp.where(inside, value, 0.0)
                slope = jnp.where(inside, slope, 0.0)
            row = (pair_of * 2 + side) * 128
            active_out[pl.ds(row, 128), pair * 128 : pair * 128 + 128] = value.astype(BF)
            slope_out[pl.ds(row, 128), pair * 128 : pair * 128 + 128] = slope.astype(BF)

    def finish_group(second, group):
        for pair in range(5):
            finish_second(second, group, pair, pair * 128)
        rows = pl.ds(group * 256, 256)
        made = dot(active_out[rows], fwd_out[...])
        for frame in range(2):
            taps[group * 2 + frame + 1] = jnp.transpose(made[frame * 128 : frame * 128 + 128])[0:144]

    def second_product(pair_of):
        pieces = []
        for step in range(4):
            for col_off in range(3):
                pieces.append(two_rows(active, pair_of * 2 + step, 0, 5, col_off))
        return dot(jnp.concatenate(pieces, axis=1), fwd_mid[...])

    seconds = (second, second_other)
    second[...] = second_product(0)
    for group in range(1, 8):
        seconds[group % 2][...] = second_product(group)
        finish_group(seconds[(group - 1) % 2], group - 1)
    finish_group(seconds[1], 7)
    for frame in range(16):
        columns = []
        for col_off in range(3):
            value = None
            for time_off in range(3):
                at = (time_off * 3 + col_off) * 16
                piece = taps[frame + time_off, at : at + 16]
                value = piece if value is None else value + piece
            columns.append(value)
        result = previous_column(columns[0]) + columns[1] + next_column(columns[2])
        branch[frame * 16 : frame * 16 + 16] = result.astype(BF)


def consistency_kernel(
    gathered, lines, stats, mine_target, beside, other, far, others, to_lines, to_rows, lines_again, spread, out, loss, target
):
    f, half, chip, core = place()
    for slot, source in enumerate((mine_target, beside, other, far)):
        at = 144 if slot else 0
        for side, image in enumerate((source[at : at + 16], others[256 + slot * 16 : 272 + slot * 16])):
            row = jnp.bitwise_xor(half * 4 + chip * 2 + core, slot * 2 + side) * 16
            row = pl.multiple_of(row, 16)
            for part in range(2):
                target[pl.ds(part * 128 + row, 16), :] = image[:, part * 128 : part * 128 + 128]
    weight = stats[2:3, 0:128]
    free = jnp.transpose(jnp.zeros((128, 128), F32) + stats[0:1, 0:128])
    free = jnp.concatenate([free, free], axis=0)
    wanted = target[...]
    made = dot(to_lines[...], gathered[...])
    wanted_spectrum = dot(lines_again[...], wanted)
    held = lines[...].astype(F32)
    kept = free * (made + held) + held
    grad = (free * (kept - wanted_spectrum) * (2.0 * weight)).astype(BF)
    out[...] = dot(spread[...], grad).astype(BF)
    residual = dot(to_rows[...], kept.astype(BF)) - wanted.astype(F32)
    loss[...] = jnp.zeros((8, 128), F32) + jnp.sum(residual * residual * weight)


def backward_kernel(
    grads, bwd_out_hbm, slope_out, active, turned, bwd_mid_hbm, slope_in, natural,
    out,
    bwd_out, bwd_mid, came,
    stack, product, product_other, grad_mid, grad_in, result, result_other, sum_mid, sum_out, sum_in, patches, tall, tiles, line,
):
    loads = [move(bwd_out_hbm, bwd_out, came, 0), move(bwd_mid_hbm, bwd_mid, came, 1)]
    zero32 = jnp.zeros((96, 128), BF)
    stack[0:96, 1920:2048] = zero32
    stack[192:288, 0:128] = zero32
    for frame in range(16):
        value = grads[frame * 32 : frame * 32 + 32].astype(F32)
        shifted = [next_column(value).astype(BF), value.astype(BF), previous_column(value).astype(BF)]
        for time_off in range(3):
            to = frame + time_off - 1
            if 0 <= to < 16:
                for col_off in range(3):
                    at = (time_off * 3 + col_off) * 32
                    stack[at : at + 32, to * 128 : to * 128 + 128] = shifted[col_off]
    grad_mid[0] = jnp.zeros((5, 10, 16, 128), BF)
    grad_mid[17] = jnp.zeros((5, 10, 16, 128), BF)
    tall[...] = jnp.zeros_like(tall)

    lane = lax.broadcasted_iota(jnp.int32, (1, 128), 1)
    bias_mid = jnp.zeros((1, 128), F32)
    buffers = (product, product_other)

    def finish_mid(buffer, group):
        own = jnp.zeros((1, 128), F32)
        for step in range(4):
            frame = group * 4 + step
            for pair in range(5):
                chunk = buffer[step * 128 : step * 128 + 128, pair * 128 : pair * 128 + 128]
                slope = slope_out[frame * 128 : frame * 128 + 128, pair * 128 : pair * 128 + 128]
                value = (chunk * slope.astype(F32)).astype(BF).astype(F32)
                added = jnp.sum(value, axis=0, keepdims=True)
                if pair == 0:
                    added = jnp.where(lane >= 64, added, 0.0)
                if pair == 4:
                    added = jnp.where(lane < 64, added, 0.0)
                own = own + added

                def store(slabs, values, frame=frame, pair=pair):
                    grad_mid[frame + 1, pair, slabs] = values

                put_slabs(store, value)
        return own

    loads[0].wait()
    groups = 16 // 4
    for group in range(groups + 1):
        if group < groups:
            at = group * 4 * 128
            buffers[group % 2][...] = dot_first(stack[:, at : at + 4 * 128], bwd_out[...])
        if group > 0:
            bias_mid = bias_mid + finish_mid(buffers[(group - 1) % 2], group - 1)

    made = dot(stack[...], active[...])
    for pair in range(5):
        sum_out[pair] = made[:, pair * 128 : pair * 128 + 128]
    for group in range(16 // 4):
        frames = [group * 4 + step for step in range(4)]
        left = jnp.concatenate([turned[frame : frame + 3].reshape(384, 512) for frame in frames], axis=1)
        right = []
        for col_off in range(3):
            right.append(jnp.concatenate([two_rows(grad_mid, frame + 1, 0, 4, 2 - col_off) for frame in frames], axis=0))
        made = dot(left, jnp.concatenate(right, axis=1))
        sum_mid[...] = made if group == 0 else sum_mid[...] + made

    def lay_out_mid(time_off, row_off):
        for col_off in range(3):
            tap = (time_off * 3 + row_off) * 3 + col_off
            at, lane = time_off * 128, col_off * 256
            upper = sum_mid[at : at + 64, lane + (2 - row_off) * 64 : lane + (2 - row_off) * 64 + 64]
            lower = sum_mid[at + 64 : at + 128, lane + (3 - row_off) * 64 : lane + (3 - row_off) * 64 + 64]
            tall[tap * 64 : tap * 64 + 64, 0:64] = upper + lower

    def lay_out_last():
        for row_off in range(3):
            value = None
            for row in range(2, 10):
                lane = (row - 2 + row_off) * 64
                piece = sum_out[lane // 128, pl.ds(row, 18, stride=16), :][:, lane % 128 : lane % 128 + 64]
                value = piece if value is None else value + piece
            for time_off in range(3):
                for col_off in range(3):
                    tap = (time_off * 3 + row_off) * 3 + col_off
                    for part in range(2):
                        row = (time_off * 3 + col_off) * 2 + part
                        line[part : part + 1, tap * 64 : tap * 64 + 64] = value[row : row + 1]

    def lay_out_pieces():
        for owner in range(8):
            for part in range(2):
                for piece in range(4):
                    at = owner * 216 + piece * 54
                    row = owner * 8 + part * 4 + piece
                    tiles[13, row : row + 1, 64:118] = line[part : part + 1, at : at + 54]

    def lay_out_patches(first, last):
        for frame in range(first, last):
            value = natural[frame].astype(F32)
            shifted = (previous_column(value).astype(BF), natural[frame], next_column(value).astype(BF))
            for col_off in range(3):
                for pair in range(4):
                    piece = shifted[col_off][pair * 16 + 16 : pair * 16 + 48]
                    for time_off in range(3):
                        to = frame - time_off + 1
                        if 0 <= to < 16:
                            at = (time_off * 3 + col_off) * 32
                            lane = (to * 4 + pair) * 128
                            patches[at : at + 32, lane : lane + 128] = piece

    def input_product(group):
        rows = []
        for half_of in range(2):
            pieces = []
            for step in range(4):
                for col_off in range(3):
                    pieces.append(two_rows(grad_mid, group * 4 + half_of * 2 + step, 0, 4, col_off))
            rows.append(jnp.concatenate(pieces, axis=1))
        return dot(jnp.concatenate(rows, axis=0), bwd_mid[...])

    def finish_input(buffer, group):
        own = jnp.zeros((1, 128), F32)
        for half_of in range(2):
            for pair in range(4):
                for side in range(2):
                    frame = group * 4 + half_of * 2 + side
                    at = half_of * 512 + pair * 128
                    chunk = buffer[at : at + 128, side * 128 : side * 128 + 128]
                    slope = slope_in[frame * 128 : frame * 128 + 128, pair * 128 : pair * 128 + 128]
                    value = (chunk * slope.astype(F32)).astype(BF)
                    grad_in[frame * 512 + pair * 128 : frame * 512 + pair * 128 + 128, :] = value
                    own = own + jnp.sum(value.astype(F32), axis=0, keepdims=True)
        return own

    loads[1].wait()
    patches[0:96, 0:512] = jnp.zeros((96, 512), BF)
    patches[192:288, 7680:8192] = jnp.zeros((96, 512), BF)
    results = (result, result_other)
    bias_in = jnp.zeros((1, 128), F32)
    for group in range(5):
        if group < 4:
            results[group % 2][...] = input_product(group)
        if group == 0:
            for time_off in range(3):
                lay_out_mid(time_off, 0)
            lay_out_last()
            lay_out_patches(0, 4)
        else:
            bias_in = bias_in + finish_input(results[(group - 1) % 2], group - 1)
        if group == 1:
            for time_off in range(3):
                lay_out_mid(time_off, 1)
            lay_out_patches(4, 10)
        if group == 2:
            for time_off in range(3):
                lay_out_mid(time_off, 2)
            lay_out_patches(10, 16)
        if group == 3:
            for tile in range(14):
                tiles[tile] = jnp.transpose(tall[tile * 128 : tile * 128 + 128])[0:64]
            lay_out_pieces()

    sum_in[...] = dot(patches[...], grad_in[...])
    for time_off in range(3):
        for row_off in range(3):
            for col_off in range(3):
                tap = (time_off * 3 + row_off) * 3 + col_off
                at = (time_off * 3 + col_off) * 32 + row_off * 8
                upper = sum_in[at : at + 8, 0:64]
                lower = sum_in[at + 8 : at + 16, 64:128]
                tall[1792 + tap * 8 : 1792 + tap * 8 + 8, 0:64] = upper + lower
    tall[2008:2009, 0:64] = bias_in[:, 0:64] + bias_in[:, 64:128]
    tall[2009:2010, 0:64] = bias_mid[:, 0:64] + bias_mid[:, 64:128]
    for tile in range(14, 16):
        tiles[tile] = jnp.transpose(tall[tile * 128 : tile * 128 + 128])[0:64]
    for quarter in range(4):
        for owner in range(8):
            value = tiles[quarter * 4 : quarter * 4 + 4, owner * 8 : owner * 8 + 8]
            out[quarter * 8 + owner] = value.reshape(32, 128).astype(BF)


def sum_kernel(parts, stats, loss, shard, shared):
    total = parts[0].astype(F32)
    for source in range(1, 32):
        total = total + parts[source].astype(F32)
    divisor = jnp.maximum(stats[1:2, 0:1] * (2.0 * 128 * 128), 1.0)
    total = total / divisor
    shard[...] = total
    lane = lax.broadcasted_iota(jnp.int32, (32, 128), 1)
    shared[...] = jnp.where(lane == 0, jnp.sum(total * total), loss[0:1] + jnp.zeros((32, 128), F32))


def update_kernel(
    own, near, mid, far, messages, stats,
    w_in, w_mid, w_out, w_bias, f_in, f_mid, f_out, f_bias, s_in, s_mid, s_out, s_bias,
    loss_sum, valid_count, grad_norm, mf_in, mf_mid, mf_out, mf_bias, ms_in, ms_mid, ms_out, ms_bias,
    mw_in, mw_mid, mw_out, mw_bias, mc_in, mc_mid, mc_out, mc_bias,
    shards, g_mid, g_in, g_out, g_bias,
):
    f, half, chip, core = place()
    for slot, source in enumerate((own, near, mid, far)):
        shards[jnp.bitwise_xor(f, slot)] = source[...]
    message = jnp.sum(messages[...], axis=0, keepdims=True)
    norm = jnp.sqrt(message[:, 0:1])
    loss_sum[0, 0] = jnp.sum(message[:, 1:2])
    valid_count[0, 0] = jnp.sum(stats[1:2, 0:1]) * (2.0 * 128 * 128)
    grad_norm[0, 0] = jnp.sum(norm)
    factor = jnp.minimum(1.0, CLIP / (norm + 1e-06))

    def tile_of(tile):
        at = (tile % 4) * 8
        return shards[tile // 4, at : at + 8]

    for tile in range(13):
        g_mid[:, tile * 128 : tile * 128 + 128] = tile_of(tile)
    mixed = tile_of(13)
    g_mid[:, 1664:1728] = mixed[:, 0:64]
    for part in range(2):
        for piece in range(4):
            row = part * 4 + piece
            g_out[part : part + 1, piece * 54 : piece * 54 + 54] = mixed[row : row + 1, 64:118]
    g_in[:, 0:128] = tile_of(14)
    mixed = tile_of(15)
    g_in[:, 128:216] = mixed[:, 0:88]
    square = jnp.concatenate([mixed, jnp.zeros((120, 128), F32)], axis=0)
    g_bias[...] = jnp.transpose(square)[88:90, 0:8]
    for grad, weight, one, two, new_one, new_two, new_weight, new_copy in (
        (g_in, w_in, f_in, s_in, mf_in, ms_in, mw_in, mc_in),
        (g_mid, w_mid, f_mid, s_mid, mf_mid, ms_mid, mw_mid, mc_mid),
        (g_out, w_out, f_out, s_out, mf_out, ms_out, mw_out, mc_out),
        (g_bias, w_bias, f_bias, s_bias, mf_bias, ms_bias, mw_bias, mc_bias),
    ):
        results = adamw(weight[...], grad[...] * factor, one[...], two[...])
        for ref, value in zip((new_one, new_two, new_weight, new_copy), results):
            ref[...] = value


VECTOR = pl.BlockSpec(memory_space=pltpu.VMEM)
SCALAR = pl.BlockSpec(memory_space=pltpu.SMEM)
LEFT = pl.BlockSpec(memory_space=pl.ANY)


def near(value):
    return pltpu.with_memory_space_constraint(value, pltpu.VMEM)


def shape(*dims, dtype=BF):
    return jax.ShapeDtypeStruct(dims, dtype)


def kernel_call(kernel, name, micros, megabytes, operands, results, scratch, in_specs=None, out_specs=None):
    return pl.pallas_call(
        kernel,
        name=name,
        out_shape=results,
        in_specs=in_specs or [VECTOR] * len(operands),
        out_specs=out_specs or [VECTOR] * len(results),
        scratch_shapes=scratch,
        cost_estimate=pl.CostEstimate(flops=int(micros * 1e9), bytes_accessed=0, transcendentals=0),
        compiler_params=pltpu.CompilerParams(vmem_limit_bytes=megabytes * 2**20),
    )(*operands)


def swap(value, axis, bit):
    return lax.ppermute(value, axis, [(i, i ^ bit) for i in range(lax.axis_size(axis))])


def by_rows(
    kspace, line_mask, valid_flags, target, conv_in, conv_mid, conv_out, conv_bias,
    first_in, first_mid, first_out, first_bias, second_in, second_mid, second_out, second_bias,
):
    tables = make_tables()

    mine, theirs, far, mine_target = kernel_call(
        lines_kernel,
        "prepare_lines",
        2,
        56,
        [
            valid_flags, kspace.reshape(2, 4, 32, 128), line_mask.reshape(8, 16), target.reshape(2, 4, 32, 128),
            tables["columns"], tables["permute"], conv_mid[0, 0].T, conv_in[0].T, conv_out[0], conv_bias[0],
        ],
        [pltpu.VMEM((176, 256), BF)] * 3 + [pltpu.VMEM((32, 256), BF)],
        [pltpu.VMEM((2, 80, 256), BF), pltpu.VMEM((2, 4, 16, 256), BF), pltpu.VMEM((16, 8, 128), F32)],
        in_specs=[SCALAR] + [VECTOR] * 9,
    )

    sent = ((mine, 1), (theirs, 2), (far, 3))
    beside, other, far = (swap(value, ("half", "chip"), step) for value, step in sent)

    column, chips = kernel_call(
        merge_kernel,
        "merge_lines",
        0.5,
        8,
        [mine, near(beside), near(other), near(far), mine_target],
        [shape(272, 256), shape(320, 256)],
        [],
    )
    gathered = [column] + [swap(column, "frames", step) for step in (1, 2, 3)]
    others = swap(chips, "core", 1)
    scratch = [pltpu.VMEM((16, 64, 128), F32), pltpu.VMEM((2, 1792), F32), pltpu.VMEM((64, 128), F32)]
    fwd_in, fwd_mid, fwd_out, bias = kernel_call(
        forward_weight_kernel,
        "lay_out_forward_weights",
        4,
        20,
        [near(chips), near(others), tables["pick_out"]],
        [shape(1152, 768), shape(3072, 256), shape(640, 256), shape(8, 768, dtype=F32)],
        scratch,
    )
    bwd_mid, bwd_out = kernel_call(
        backward_weight_kernel,
        "lay_out_backward_weights",
        3,
        16,
        [near(chips), near(others), tables["pick_back"]],
        [shape(3072, 256), shape(288, 640)],
        scratch,
    )
    *gathered, bias, bwd_out = lax.optimization_barrier((*gathered, bias, bwd_out))
    gathered += [swap(piece, "core", 1) for piece in gathered]
    kept = [(16, 128, 128), (18, 128, 512), (2048, 640), (2048, 512), (2048, 640)]
    moved = [(128, 256), (1152, 768), (3072, 256)]
    branch, stats, lines, natural, turned, active, slope_in, slope_out = kernel_call(
        forward_kernel,
        "features_and_branch",
        27,
        26,
        [*map(near, gathered), tables["feature"], fwd_in, fwd_mid, fwd_out, bias],
        [shape(256, 128), shape(8, 256, dtype=F32), shape(256, 128)] + [shape(*dims) for dims in kept],
        [pltpu.VMEM(dims, BF) for dims in moved]
        + [pltpu.SemaphoreType.DMA((3,))]
        + [
            pltpu.VMEM((20, 128, 256), BF),
            pltpu.VMEM((4, 8, 128), F32),
            pltpu.VMEM((24, 128), F32),
            pltpu.VMEM((18, 10, 16, 128), BF),
            pltpu.VMEM((18, 6, 10, 16, 128), BF),
            pltpu.VMEM((256, 768), F32),
            pltpu.VMEM((256, 768), F32),
            pltpu.VMEM((640, 256), F32),
            pltpu.VMEM((640, 256), F32),
            pltpu.VMEM((18, 144, 128), F32),
        ],
        in_specs=[VECTOR] * 8 + [LEFT] * 3 + [VECTOR] * 2,
    )
    by_frame = lax.all_to_all(branch.reshape(16, 16, 128), ("frames", "chip", "core"), 0, 0, tiled=True)
    grads, loss = kernel_call(
        consistency_kernel,
        "data_consistency",
        2.5,
        12,
        [
            near(by_frame.reshape(256, 128)), lines, stats, mine_target, beside, other, far, others,
            tables["to_lines"], tables["to_rows"], tables["lines_again"], tables["spread"],
        ],
        [shape(512, 128), shape(8, 128, dtype=F32)],
        [pltpu.VMEM((256, 128), BF)],
    )
    by_block = lax.all_to_all(grads.reshape(16, 32, 128), ("frames", "chip", "core"), 0, 0, tiled=True)
    moved = [(288, 640), (3072, 256)]
    (parts,) = kernel_call(
        backward_kernel,
        "weight_gradients",
        27,
        30,
        [near(by_block.reshape(512, 128)), bwd_out, slope_out, active, turned, bwd_mid, slope_in, natural],
        [shape(32, 32, 128)],
        [pltpu.VMEM(dims, BF) for dims in moved]
        + [pltpu.SemaphoreType.DMA((2,))]
        + [
            pltpu.VMEM((288, 2048), BF),
            pltpu.VMEM((512, 640), F32),
            pltpu.VMEM((512, 640), F32),
            pltpu.VMEM((18, 5, 10, 16, 128), BF),
            pltpu.VMEM((8192, 128), BF),
            pltpu.VMEM((1024, 256), F32),
            pltpu.VMEM((1024, 256), F32),
            pltpu.VMEM((384, 768), F32),
            pltpu.VMEM((5, 288, 128), F32),
            pltpu.VMEM((288, 128), F32),
            pltpu.VMEM((288, 8192), BF),
            pltpu.VMEM((2048, 128), F32),
            pltpu.VMEM((16, 64, 128), F32),
            pltpu.VMEM((2, 1792), F32),
        ],
        in_specs=[VECTOR, LEFT] + [VECTOR] * 3 + [LEFT] + [VECTOR] * 2,
    )
    parts = lax.all_to_all(parts, ("frames", "half", "chip", "core"), 0, 0, tiled=True)
    shard, messages = kernel_call(
        sum_kernel,
        "sum_gradients",
        2,
        8,
        [near(parts), stats, loss],
        [shape(32, 128, dtype=F32), shape(32, 128, dtype=F32)],
        [],
    )
    shards = [shard] + [swap(shard, "frames", step) for step in (1, 2, 3)]
    messages = lax.all_to_all(messages, ("frames", "half", "chip", "core"), 0, 0, tiled=True)
    groups = (
        (conv_in, conv_mid, conv_out, conv_bias),
        (first_in, first_mid, first_out, first_bias),
        (second_in, second_mid, second_out, second_bias),
    )
    state = []
    for of_in, of_mid, of_out, of_bias in groups:
        state += [of_in[0].T, of_mid[0, 0].T, of_out[0], of_bias[0]]
    shapes = [(8, 216), (8, 1728), (2, 216), (2, 8)]
    results = kernel_call(
        update_kernel,
        "adamw",
        2,
        8,
        [*map(near, shards), near(messages), stats, *state],
        [shape(1, 1, dtype=F32)] * 3
        + [shape(*dims, dtype=F32) for dims in shapes * 3]
        + [shape(*dims, dtype=BF) for dims in shapes],
        [pltpu.VMEM((4, 32, 128), F32)] + [pltpu.VMEM(shapes[at], F32) for at in (1, 0, 2, 3)],
        out_specs=[SCALAR] * 3 + [VECTOR] * 16,
    )
    outputs = [result[0, 0] for result in results[0:3]]
    for at in range(3, 19, 4):
        of_in, of_mid, of_out, of_bias = results[at : at + 4]
        outputs += [of_in.T[None], of_mid.T[None, None], of_out[None], of_bias[None]]
    return tuple(outputs)


def specs_for(rows):
    lines = P(None, "frames", rows)
    images = P(None, "frames", rows, None, None)
    weights = [P(None, None, rows), P(None, None, None, rows), P(None, None, rows), P(None, None, rows)]
    in_specs = (images, lines, P(None, "frames"), images, *(weights * 3))
    out_specs = (P(), P(), P(), *(weights * 4))
    return in_specs, out_specs


def solution(mesh):
    frames, rows = (mesh.shape[axis] for axis in ("frames", "rows"))
    if (frames, rows) != (4, 8):
        in_specs, out_specs = specs_for("rows")
        return jax.shard_map(local, mesh=mesh, in_specs=in_specs, out_specs=out_specs, check_vma=False)
    chips = Mesh(mesh.devices.reshape(frames, 2, rows // 4, 2), ("frames", "half", "chip", "core"))
    in_specs, out_specs = specs_for(("half", "chip", "core"))
    return jax.shard_map(by_rows, mesh=chips, in_specs=in_specs, out_specs=out_specs, check_vma=False)
```
